256 devices in a mesh: shot: 8 (over z_lo, core), rcv: 32 (over y, z_hi, x).
Axes of the slice: x: 4, y: 4, z: 8 (z_hi: 2, z_lo: 4; z = z_hi * 4 + z_lo), core: 2. Of those that a mesh axis runs over, the one named last changes fastest.
Arguments:
- reflection: bfloat16 [512, 512, 256], P('shot', 'rcv'), may hold values from -6 to 6
- focus_index: int32 [2], replicated, may hold values from 0 to 511
- shot_window: int32 [2, 512, 2], P(None, 'shot'), may hold values from 0 to 256, as said below
- rcv_window: int32 [2, 512, 2], P(None, 'rcv'), may hold values from 0 to 256, as said below
Outputs:
- focus_down: float32 [512, 2, 256], P('rcv', None, 'shot')
- focus_up: float32 [512, 2, 256], P(('shot', 'rcv'))
The draws below stay inside these ranges and needn't reach their ends.
Inputs may be any that keep to these rules, and one draw needn't show every extreme that they name: `shot_window`: onset (index 0) is below end (index 1) for every shot and focal point. `rcv_window`: onset (index 0) is below end (index 1) for every receiver and focal point.
All inputs are finite; a program needn't handle non-finite values.
Results may differ from the reference program's by a relative error of at most 0.0022.
Values may be sent and summed in bfloat16 or wider, within the bound.
No kernel may reach another device: no remote copies, remote signals or barrier semaphores. Data moves between devices by JAX's collectives and lax.ppermute only.
A program may use at most 192 MiB of HBM per device.

```python
import math
import jax
import jax.numpy as jnp
from jax import lax

LAGS = 256
FOCI = 2
ITERS = 2
SHOTS = 512
RECEIVERS = 512


def window_pairs(key, count):
    first_key, second_key = jax.random.split(key)
    onset = jnp.maximum(jax.random.randint(first_key, (count, FOCI), -(LAGS // 8), LAGS // 2), 0)
    length = jax.random.randint(second_key, (count, FOCI), LAGS // 4, LAGS)
    ending = jnp.minimum(onset + length, LAGS)
    return jnp.stack([onset, ending]).astype(jnp.int32)


def draw_shot_window(key, part):
    key = jax.random.fold_in(key, 11)
    return window_pairs(key, SHOTS)


def draw_rcv_window(key, part):
    key = jax.random.fold_in(key, 23)
    return window_pairs(key, RECEIVERS)


def levels(own_key, extent, pieces, least, largest):
    def one(position, shards_of):
        heights = jax.random.uniform(jax.random.fold_in(jax.random.fold_in(own_key, 6), position), (shards_of,), jnp.float32, least / len(pieces), largest / len(pieces))
        return jnp.repeat(jnp.exp(heights), extent[position] // shards_of).reshape((-1,) + (1,) * (len(extent) - position - 1))

    loudness = one(*pieces[0])
    for cut in pieces[1:]:
        loudness = loudness * one(*cut)
    return loudness


def noise(own_key, extent, scale, reach, shards=(), kind=jnp.bfloat16):
    drawn = scale * jax.random.normal(own_key, extent, jnp.float32)
    if shards:
        drawn = drawn * levels(own_key, extent, shards, -0.22, 0.18)
    return jnp.clip(drawn, -reach, reach).astype(kind)


def setup_inputs(seed: int = 0) -> dict:
    streams_of = jax.random.split(jax.random.key(seed), 5)
    return {
        "reflection": noise(streams_of[0], (SHOTS, RECEIVERS, LAGS), 1.0, 6.0, ((0, 8), (1, 32))),
        "focus_index": jax.random.randint(streams_of[1], (FOCI,), 0, SHOTS).astype(jnp.int32),
        "shot_window": draw_shot_window(jax.random.fold_in(streams_of[4], 71), 0),
        "rcv_window": draw_rcv_window(jax.random.fold_in(streams_of[4], 71), 0),
    }


def window_mask(window, lag_total):
    lag_axis = jnp.arange(lag_total, dtype=jnp.int32)
    onset = window[0].astype(jnp.int32)[:, :, None]
    ending = window[1].astype(jnp.int32)[:, :, None]
    return (lag_axis >= onset) & (lag_axis < ending)

def lower_toeplitz(field):
    width, foci, lag_total = field.shape
    padded = jnp.concatenate([field, jnp.zeros_like(field)], axis=2)
    tiled = jnp.tile(padded, (1, 1, lag_total))[:, :, :lag_total * (2 * lag_total - 1)]
    skewed = tiled.reshape(width, foci, lag_total, 2 * lag_total - 1)[:, :, :, :lag_total]
    return jnp.transpose(skewed, (0, 2, 1, 3)).reshape(width * lag_total, foci * lag_total)

def upper_toeplitz(upgoing):
    count, foci, lag_total = upgoing.shape
    padded = jnp.concatenate([upgoing, jnp.zeros_like(upgoing)], axis=2)
    tiled = jnp.tile(padded, (1, 1, lag_total + 1))[:, :, :lag_total * (2 * lag_total + 1)]
    skewed = tiled.reshape(count, foci, lag_total, 2 * lag_total + 1)[:, :, :, :lag_total]
    return jnp.transpose(skewed, (0, 2, 1, 3)).reshape(count * lag_total, foci * lag_total)

def convolve(kernel, field):
    count, width, lag_total = kernel.shape
    foci = field.shape[1]
    block = math.gcd(width, 32)

    def add_block(block_id, total):
        start = (block_id * block).astype(jnp.int32)
        piece = lax.dynamic_slice_in_dim(field, start, block, 0)
        slab = lax.dynamic_slice_in_dim(kernel, start, block, 1).reshape(count, block * lag_total)
        product = jnp.dot(slab, lower_toeplitz(piece), preferred_element_type=jnp.float32)
        return total + product.reshape(count, foci, lag_total)
    return lax.fori_loop(0, width // block, add_block, jnp.zeros((count, foci, lag_total), jnp.float32))

def correlate(kernel, upgoing):
    count, width, lag_total = kernel.shape
    foci = upgoing.shape[1]
    block = math.gcd(count, 32)

    def add_block(block_id, total):
        start = (block_id * block).astype(jnp.int32)
        piece = lax.dynamic_slice_in_dim(upgoing, start, block, 0)
        slab = lax.dynamic_slice_in_dim(kernel, start, block, 0)
        slab = jnp.transpose(slab, (1, 0, 2)).reshape(width, block * lag_total)
        product = jnp.dot(slab, upper_toeplitz(piece), preferred_element_type=jnp.float32)
        return total + product.reshape(width, foci, lag_total)
    return lax.fori_loop(0, count // block, add_block, jnp.zeros((width, foci, lag_total), jnp.float32))

def reference(reflection, focus_index, shot_window, rcv_window):
    lag_total = reflection.shape[2]
    start_field = jnp.flip(jnp.transpose(reflection[focus_index.astype(jnp.int32)], (1, 0, 2)), axis=2)
    conv_scale = 1.0 / math.sqrt(RECEIVERS * LAGS)
    corr_scale = 1.0 / math.sqrt(SHOTS * LAGS)
    shot_mask = window_mask(shot_window, lag_total)
    rcv_mask = window_mask(rcv_window, lag_total)
    field = start_field
    up_exact = None
    down_exact = None
    for iteration in range(ITERS):
        convolved = convolve(reflection, field) * conv_scale
        up_exact = jnp.where(shot_mask, convolved, 0.0)
        upgoing = up_exact.astype(jnp.bfloat16)
        correlated = correlate(reflection, upgoing) * corr_scale
        down_exact = start_field.astype(jnp.float32) + jnp.where(rcv_mask, correlated, 0.0)
        field = down_exact.astype(jnp.bfloat16)
    return (down_exact, up_exact)
```

```python
import functools
import math

import jax
import jax.numpy as jnp
import ml_dtypes
import numpy as np
from jax import lax
from jax.experimental import pallas as pl
from jax.experimental.pallas import tpu as pltpu
from jax.sharding import PartitionSpec as P


ITERS = 2
LAGS = 256
LANES = 128
FOCI = 2
SHOTS_HERE = 64
RCV_HERE = 16
RCV_AXIS = 32
SHOT_AXIS = 8
SHARE = SHOTS_HERE * FOCI * 2 // 16
HALVES = LAGS // LANES
F32 = jnp.float32
BF16 = jnp.bfloat16


def split_bf16(matrix):
    high = matrix.astype(ml_dtypes.bfloat16)
    low = (matrix - high.astype(np.float64)).astype(ml_dtypes.bfloat16)
    return high, low


def tables():
    times = np.arange(LAGS)[:, None]
    angles = (np.arange(LAGS)[None, :] + 0.5) * (np.pi / LAGS) * times
    forward = np.concatenate([np.cos(angles), -np.sin(angles)], axis=1)
    fwd_high, fwd_low = split_bf16(forward)
    inv_high, inv_low = split_bf16(np.ascontiguousarray(forward.T))
    flip = np.ascontiguousarray(np.eye(LAGS)[::-1]).astype(ml_dtypes.bfloat16)
    return fwd_high, fwd_low, inv_high, inv_low, flip


def dot(left, right):
    return jnp.dot(left, right, preferred_element_type=F32)


def to_spectrum(traces, high, low):
    return dot(traces, high[...]) + dot(traces, low[...])


def to_traces(spectrum, high, low, scale):
    top = spectrum.astype(BF16)
    rest = (spectrum - top.astype(F32)).astype(BF16)
    return (dot(top, high[...]) + (dot(top, low[...]) + dot(rest, high[...]))) * scale


def pick_kernel(focus, reflection, flip, out):
    first = lax.axis_index("shot") * SHOTS_HERE
    picked = []
    for which in range(FOCI):
        row = focus[which] - first
        inside = jnp.logical_and(row >= 0, row < SHOTS_HERE)
        trace = reflection[jnp.clip(row, 0, SHOTS_HERE - 1)].astype(F32)
        picked.append(jnp.where(inside, trace, 0.0).astype(BF16))
    flipped = dot(jnp.concatenate(picked, axis=0), flip[...]).astype(BF16)
    for place in range(SHOT_AXIS):
        out[place] = flipped


def shot_slot(shot):
    y, z, x, j = shot // 16, (shot // 8) % 2, (shot // 2) % 4, shot % 2
    return y * 16 + x * 4 + z * 2 + j


def reflection_kernel(reflection, high, low, out):
    step = 16
    for begin in range(0, SHOTS_HERE, step):
        rows = reflection[begin : begin + step].reshape(step * RCV_HERE, LAGS)
        spectrum = to_spectrum(rows, high, low)
        for local in range(step):
            piece = spectrum[local * RCV_HERE : (local + 1) * RCV_HERE]
            slot = shot_slot(begin + local)
            for chunk in range(4):
                out[chunk, pl.ds(slot, RCV_HERE, SHOTS_HERE), :] = piece[
                    :, chunk * LANES : (chunk + 1) * LANES
                ]


def convolve_in(field, refl, fwd_high, fwd_low, inv_high, inv_low, out, spectrum, product, rows):
    spectrum[...] = to_spectrum(field, fwd_high, fwd_low)
    for chunk in range(2):
        re_lanes = slice(chunk * LANES, (chunk + 1) * LANES)
        im_lanes = slice(LAGS + chunk * LANES, LAGS + (chunk + 1) * LANES)
        totals = [jnp.zeros((SHOTS_HERE, LANES), F32) for _ in range(2 * FOCI)]
        for r in range(RCV_HERE):
            re = refl[chunk, r * SHOTS_HERE : (r + 1) * SHOTS_HERE, :]
            im = refl[2 + chunk, r * SHOTS_HERE : (r + 1) * SHOTS_HERE, :]
            for q in range(FOCI):
                line = q * RCV_HERE + r
                f_re = spectrum[line : line + 1, re_lanes]
                f_im = spectrum[line : line + 1, im_lanes]
                totals[2 * q] += re * f_re - im * f_im
                totals[2 * q + 1] += re * f_im + im * f_re
        for q in range(FOCI):
            product[q * SHOTS_HERE : (q + 1) * SHOTS_HERE, re_lanes] = totals[2 * q]
            product[q * SHOTS_HERE : (q + 1) * SHOTS_HERE, im_lanes] = totals[2 * q + 1]
    scale = 1.0 / (LAGS * math.sqrt(RCV_HERE * RCV_AXIS * LAGS))
    result = to_traces(product[...], inv_high, inv_low, scale)
    for q in range(FOCI):
        for h in range(HALVES):
            rows[pl.ds(h * FOCI + q, SHOTS_HERE, 2 * FOCI), :] = result[
                q * SHOTS_HERE : (q + 1) * SHOTS_HERE, h * LANES : (h + 1) * LANES
            ]
    for place in range(RCV_AXIS):
        group = (place // 8) * 4 + place % 4
        out[place] = rows[group * SHARE : (group + 1) * SHARE, :]


def first_kernel(picked, refl, fwd_high, fwd_low, inv_high, inv_low, start_out, out, spectrum, product, rows):
    start = picked[0].astype(F32)
    for place in range(1, SHOT_AXIS):
        start = start + picked[place].astype(F32)
    start = start.astype(BF16)
    start_out[...] = start
    convolve_in(start, refl, fwd_high, fwd_low, inv_high, inv_low, out, spectrum, product, rows)


def upgoing_kernel(window, parts, up_out, out):
    total = parts[0]
    for place in range(1, RCV_AXIS):
        total = total + parts[place]
    me = lax.axis_index("rcv")
    corner = (me // 8) * 16 + (me % 4) * 2
    row = lax.broadcasted_iota(jnp.int32, (SHARE, LANES), 0)
    onset = jnp.zeros((SHARE, LANES), jnp.int32)
    ending = jnp.zeros((SHARE, LANES), jnp.int32)
    for z in range(2):
        for j in range(2):
            for q in range(FOCI):
                shot = corner + z * 8 + j
                mine = jnp.logical_and(row // 4 == z * 2 + j, row % 2 == q)
                onset = jnp.where(mine, window[0, q, shot], onset)
                ending = jnp.where(mine, window[1, q, shot], ending)
    time = lax.broadcasted_iota(jnp.int32, (SHARE, LANES), 1) + ((row // 2) % 2) * LANES
    up = jnp.where(jnp.logical_and(time >= onset, time < ending), total, 0.0)
    own = jnp.where((me // 4) % 2 == 0, up[:8], up[8:])
    for j in range(2):
        for q in range(FOCI):
            for h in range(HALVES):
                line = j * 4 + h * 2 + q
                up_out[j, q : q + 1, h * LANES : (h + 1) * LANES] = own[line : line + 1]
    rounded = up.astype(BF16)
    for place in range(out.shape[0]):
        out[place] = rounded


def correlate_kernel(upgoing, refl, fwd_high, fwd_low, inv_high, inv_low, out, rows, spectrum, product):
    for place in range(16):
        rows[place * SHARE : (place + 1) * SHARE, :] = upgoing[place].astype(F32)
    traces = jnp.concatenate(
        [
            jnp.concatenate(
                [rows[pl.ds(h * FOCI + q, SHOTS_HERE, 2 * FOCI), :] for h in range(HALVES)], axis=1
            )
            for q in range(FOCI)
        ],
        axis=0,
    ).astype(BF16)
    spectrum[...] = to_spectrum(traces, fwd_high, fwd_low)
    for chunk in range(2):
        re_lanes = slice(chunk * LANES, (chunk + 1) * LANES)
        im_lanes = slice(LAGS + chunk * LANES, LAGS + (chunk + 1) * LANES)
        for r in range(RCV_HERE):
            totals = [jnp.zeros((8, LANES), F32) for _ in range(2 * FOCI)]
            for begin in range(0, SHOTS_HERE, 8):
                re = refl[chunk, r * SHOTS_HERE + begin : r * SHOTS_HERE + begin + 8, :]
                im = refl[2 + chunk, r * SHOTS_HERE + begin : r * SHOTS_HERE + begin + 8, :]
                for q in range(FOCI):
                    lines = slice(q * SHOTS_HERE + begin, q * SHOTS_HERE + begin + 8)
                    u_re = spectrum[lines, re_lanes]
                    u_im = spectrum[lines, im_lanes]
                    totals[2 * q] += re * u_re + im * u_im
                    totals[2 * q + 1] += re * u_im - im * u_re
            for q in range(FOCI):
                line = q * RCV_HERE + r
                product[line : line + 1, re_lanes] = jnp.sum(totals[2 * q], axis=0, keepdims=True)
                product[line : line + 1, im_lanes] = jnp.sum(totals[2 * q + 1], axis=0, keepdims=True)
    scale = 1.0 / (LAGS * math.sqrt(SHOTS_HERE * SHOT_AXIS * LAGS))
    result = to_traces(product[...], inv_high, inv_low, scale)
    for place in range(SHOT_AXIS):
        out[place] = result


def add_down(window, parts, start, onset, ending):
    total = parts[0]
    for place in range(1, SHOT_AXIS):
        total = total + parts[place]
    for q in range(FOCI):
        for r in range(RCV_HERE):
            line = q * RCV_HERE + r
            onset[line : line + 1, :] = jnp.full((1, LANES), window[0, q, r], jnp.int32)
            ending[line : line + 1, :] = jnp.full((1, LANES), window[1, q, r], jnp.int32)
    time = lax.broadcasted_iota(jnp.int32, (FOCI * RCV_HERE, LANES), 1)
    kept = []
    for h in range(HALVES):
        inside = jnp.logical_and(time + h * LANES >= onset[...], time + h * LANES < ending[...])
        kept.append(jnp.where(inside, total[:, h * LANES : (h + 1) * LANES], 0.0))
    return start[...].astype(F32) + jnp.concatenate(kept, axis=1)


def next_kernel(
    window, parts, start, refl, fwd_high, fwd_low, inv_high, inv_low, out, onset, ending, spectrum, product, rows
):
    field = add_down(window, parts, start, onset, ending).astype(BF16)
    convolve_in(field, refl, fwd_high, fwd_low, inv_high, inv_low, out, spectrum, product, rows)


def last_kernel(window, parts, start, out, onset, ending):
    down = add_down(window, parts, start, onset, ending)
    share = LAGS // SHOT_AXIS
    begin = lax.axis_index("shot") * share
    mine = pltpu.roll(down, lax.rem(LAGS - begin, LAGS), 1)[:, :share]
    for q in range(FOCI):
        out[:, q, :] = mine[q * RCV_HERE : (q + 1) * RCV_HERE]


VM = pl.BlockSpec(memory_space=pltpu.VMEM)
SM = pl.BlockSpec(memory_space=pltpu.SMEM)
LIMIT = 24 * 1024 * 1024


def call(kernel, name, specs, outs, scratch, *args):
    many = len(outs) > 1
    shapes = [jax.ShapeDtypeStruct(shape, dtype) for shape, dtype in outs]
    return pl.pallas_call(
        kernel,
        name=name,
        in_specs=specs,
        out_specs=[VM] * len(outs) if many else VM,
        out_shape=shapes if many else shapes[0],
        scratch_shapes=[pltpu.VMEM(shape, dtype) for shape, dtype in scratch],
        compiler_params=pltpu.CompilerParams(vmem_limit_bytes=LIMIT),
    )(*args)


def over_plane():
    places = np.arange(RCV_AXIS).reshape(4, 2, 4)
    return places.transpose(1, 0, 2).reshape(2, 16).tolist()


def on_device(reflection, focus_index, shot_window, rcv_window):
    fwd_high, fwd_low, inv_high, inv_low, flip = [jnp.asarray(table) for table in tables()]
    waves = (fwd_high, fwd_low, inv_high, inv_low)
    shot_window = jnp.transpose(shot_window, (0, 2, 1))
    rcv_window = jnp.transpose(rcv_window, (0, 2, 1))
    traces = FOCI * RCV_HERE
    bounds = [((traces, LANES), jnp.int32)] * 2
    conv_scratch = [
        ((traces, 2 * LAGS), F32),
        ((FOCI * SHOTS_HERE, 2 * LAGS), F32),
        ((FOCI * HALVES * SHOTS_HERE, LANES), F32),
    ]
    corr_scratch = [conv_scratch[2], conv_scratch[1], conv_scratch[0]]
    conv_out = ((RCV_AXIS, SHARE, LANES), F32)
    picked = call(
        pick_kernel, "pick", [SM, VM, VM], [((SHOT_AXIS, traces, LAGS), BF16)], [], focus_index, reflection, flip
    )
    picked = lax.all_to_all(picked, "shot", 0, 0, tiled=True)
    refl = call(
        reflection_kernel, "reflection_spectra", [VM] * 3,
        [((4, RCV_HERE * SHOTS_HERE, LANES), F32)], [], reflection, fwd_high, fwd_low,
    )
    start, partial = call(
        first_kernel, "first_convolution", [VM] * 6, [((traces, LAGS), BF16), conv_out], conv_scratch,
        picked, refl, *waves,
    )
    for iteration in range(ITERS):
        parts = lax.all_to_all(partial, "rcv", 0, 0, tiled=True)
        focus_up, rounded = call(
            upgoing_kernel, "upgoing", [SM, VM],
            [((2, FOCI, LAGS), F32), ((16, SHARE, LANES), BF16)], [], shot_window, parts,
        )
        upgoing = lax.all_to_all(rounded, "rcv", 0, 0, tiled=True, axis_index_groups=over_plane())
        partial = call(
            correlate_kernel, "correlation", [VM] * 6, [((SHOT_AXIS, traces, LAGS), F32)], corr_scratch,
            upgoing, refl, *waves,
        )
        parts = lax.all_to_all(partial, "shot", 0, 0, tiled=True)
        if iteration + 1 < ITERS:
            partial = call(
                next_kernel, "next_convolution", [SM] + [VM] * 7, [conv_out], bounds + conv_scratch,
                rcv_window, parts, start, refl, *waves,
            )
    share = LAGS // SHOT_AXIS
    focus_down = call(
        last_kernel, "downgoing", [SM, VM, VM], [((RCV_HERE, FOCI, share), F32)], bounds, rcv_window, parts, start
    )
    return focus_down, focus_up


def solution(mesh):
    return jax.shard_map(
        on_device,
        mesh=mesh,
        in_specs=(P("shot", "rcv", None), P(), P(None, "shot", None), P(None, "rcv", None)),
        out_specs=(P("rcv", None, "shot"), P(("shot", "rcv"), None, None)),
        check_vma=False,
    )
```

```python
import functools
import math

import jax
import jax.numpy as jnp
import ml_dtypes
import numpy as np
from jax import lax
from jax.experimental import pallas as pl
from jax.experimental.pallas import tpu as pltpu
from jax.sharding import PartitionSpec as P


ITERS = 2
LAGS = 256
LANES = 128
FOCI = 2
SHOTS_HERE = 64
RCV_HERE = 16
RCV_AXIS = 32
SHOT_AXIS = 8
SHARE = SHOTS_HERE * FOCI * 2 // 16
HALVES = LAGS // LANES
F32 = jnp.float32
BF16 = jnp.bfloat16


def split_bf16(matrix):
    high = matrix.astype(ml_dtypes.bfloat16)
    low = (matrix - high.astype(np.float64)).astype(ml_dtypes.bfloat16)
    return high, low


def tables():
    times = np.arange(LAGS)[:, None]
    angles = (np.arange(LAGS)[None, :] + 0.5) * (np.pi / LAGS) * times
    forward = np.concatenate([np.cos(angles), -np.sin(angles)], axis=1)
    fwd_high, fwd_low = split_bf16(forward)
    inv_high, inv_low = split_bf16(np.ascontiguousarray(forward.T))
    flip = np.ascontiguousarray(np.eye(LAGS)[::-1]).astype(ml_dtypes.bfloat16)
    return fwd_high, fwd_low, inv_high, inv_low, flip


def dot(left, right):
    return jnp.dot(left, right, preferred_element_type=F32)


def to_spectrum(traces, high, low):
    return dot(traces, high[...]) + dot(traces, low[...])


def to_traces(spectrum, high, low, scale):
    top = spectrum.astype(BF16)
    rest = (spectrum - top.astype(F32)).astype(BF16)
    return (dot(top, high[...]) + (dot(top, low[...]) + dot(rest, high[...]))) * scale


def shot_slot(shot):
    y, z, x, j = shot // 16, (shot // 8) % 2, (shot // 2) % 4, shot % 2
    return y * 16 + x * 4 + z * 2 + j


def prepare_kernel(
    focus_hbm, shot_hbm, rcv_hbm, reflection_hbm, high_hbm, low_hbm, inv_high_hbm, inv_low_hbm, flip_hbm,
    picks, out, shot_mask, rcv_mask, high, low, inv_high, inv_low, flip,
    focus, shot_window, rcv_window, reflection, onset, ending, sems,
):
    def fetch(source, target, place):
        copy = pltpu.make_async_copy(source, target, sems.at[place])
        copy.start()
        return copy

    step = 16
    tables = [fetch(high_hbm, high, 0), fetch(low_hbm, low, 1)]
    blocks = [
        fetch(reflection_hbm.at[pl.ds(begin, step)], reflection.at[pl.ds(begin, step)], 2 + begin // step)
        for begin in range(0, SHOTS_HERE, step)
    ]
    scalars = [fetch(focus_hbm, focus, 6), fetch(shot_hbm, shot_window, 7), fetch(rcv_hbm, rcv_window, 8)]
    later = [fetch(inv_high_hbm, inv_high, 9), fetch(inv_low_hbm, inv_low, 10), fetch(flip_hbm, flip, 11)]
    for copy in tables:
        copy.wait()
    for begin in range(0, SHOTS_HERE, step):
        blocks[begin // step].wait()
        lines = reflection[begin : begin + step].reshape(step * RCV_HERE, LAGS)
        spectrum = to_spectrum(lines, high, low)
        for local in range(step):
            piece = spectrum[local * RCV_HERE : (local + 1) * RCV_HERE]
            slot = shot_slot(begin + local)
            for chunk in range(4):
                out[chunk, pl.ds(slot, RCV_HERE, SHOTS_HERE), :] = piece[
                    :, chunk * LANES : (chunk + 1) * LANES
                ]
    for copy in scalars:
        copy.wait()
    first = lax.axis_index("shot") * SHOTS_HERE
    for which in range(FOCI):
        row = focus[which] - first
        inside = jnp.logical_and(row >= 0, row < SHOTS_HERE)
        trace = reflection[jnp.clip(row, 0, SHOTS_HERE - 1)].astype(F32)
        picked = jnp.where(inside, trace, 0.0).astype(BF16)
        for place in range(SHOT_AXIS):
            picks[place, which * RCV_HERE : (which + 1) * RCV_HERE, :] = picked
    for copy in later:
        copy.wait()
    up_mask(shot_window, shot_mask)
    down_mask(rcv_window, rcv_mask, onset, ending)


def up_mask(window, out):
    me = lax.axis_index("rcv")
    corner = (me // 8) * 16 + (me % 4) * 2
    row = lax.broadcasted_iota(jnp.int32, (SHARE, LANES), 0)
    onset = jnp.zeros((SHARE, LANES), jnp.int32)
    ending = jnp.zeros((SHARE, LANES), jnp.int32)
    for z in range(2):
        for j in range(2):
            for q in range(FOCI):
                shot = corner + z * 8 + j
                mine = jnp.logical_and(row // 4 == z * 2 + j, row % 2 == q)
                onset = jnp.where(mine, window[0, q, shot], onset)
                ending = jnp.where(mine, window[1, q, shot], ending)
    time = lax.broadcasted_iota(jnp.int32, (SHARE, LANES), 1) + ((row // 2) % 2) * LANES
    out[...] = jnp.logical_and(time >= onset, time < ending).astype(jnp.int32)


def down_mask(window, out, onset, ending):
    for q in range(FOCI):
        for r in range(RCV_HERE):
            line = q * RCV_HERE + r
            onset[line : line + 1, :] = jnp.full((1, LANES), window[0, q, r], jnp.int32)
            ending[line : line + 1, :] = jnp.full((1, LANES), window[1, q, r], jnp.int32)
    time = lax.broadcasted_iota(jnp.int32, (FOCI * RCV_HERE, LANES), 1)
    for h in range(HALVES):
        inside = jnp.logical_and(time + h * LANES >= onset[...], time + h * LANES < ending[...])
        out[:, h * LANES : (h + 1) * LANES] = inside.astype(jnp.int32)


def convolve_in(field, refl, fwd_high, fwd_low, inv_high, inv_low, out, spectrum, product, rows):
    spectrum[...] = to_spectrum(field, fwd_high, fwd_low)
    for chunk in range(2):
        re_lanes = slice(chunk * LANES, (chunk + 1) * LANES)
        im_lanes = slice(LAGS + chunk * LANES, LAGS + (chunk + 1) * LANES)
        totals = [jnp.zeros((SHOTS_HERE, LANES), F32) for _ in range(2 * FOCI)]
        for r in range(RCV_HERE):
            re = refl[chunk, r * SHOTS_HERE : (r + 1) * SHOTS_HERE, :]
            im = refl[2 + chunk, r * SHOTS_HERE : (r + 1) * SHOTS_HERE, :]
            for q in range(FOCI):
                line = q * RCV_HERE + r
                f_re = spectrum[line : line + 1, re_lanes]
                f_im = spectrum[line : line + 1, im_lanes]
                totals[2 * q] += re * f_re - im * f_im
                totals[2 * q + 1] += re * f_im + im * f_re
        for q in range(FOCI):
            product[q * SHOTS_HERE : (q + 1) * SHOTS_HERE, re_lanes] = totals[2 * q]
            product[q * SHOTS_HERE : (q + 1) * SHOTS_HERE, im_lanes] = totals[2 * q + 1]
    scale = 1.0 / (LAGS * math.sqrt(RCV_HERE * RCV_AXIS * LAGS))
    result = to_traces(product[...], inv_high, inv_low, scale)
    for q in range(FOCI):
        for h in range(HALVES):
            rows[pl.ds(h * FOCI + q, SHOTS_HERE, 2 * FOCI), :] = result[
                q * SHOTS_HERE : (q + 1) * SHOTS_HERE, h * LANES : (h + 1) * LANES
            ]
    for place in range(RCV_AXIS):
        group = (place // 8) * 4 + place % 4
        out[place] = rows[group * SHARE : (group + 1) * SHARE, :]


def first_kernel(
    picked, flip, refl, fwd_high, fwd_low, inv_high, inv_low, start_out, out, spectrum, product, rows
):
    start = picked[0].astype(F32)
    for place in range(1, SHOT_AXIS):
        start = start + picked[place].astype(F32)
    start = dot(start.astype(BF16), flip[...]).astype(BF16)
    start_out[...] = start
    convolve_in(start, refl, fwd_high, fwd_low, inv_high, inv_low, out, spectrum, product, rows)


def upgoing_kernel(mask, parts, up_out, out):
    total = parts[0]
    for place in range(1, RCV_AXIS):
        total = total + parts[place]
    up = jnp.where(mask[...] != 0, total, 0.0)
    own = jnp.where((lax.axis_index("rcv") // 4) % 2 == 0, up[:8], up[8:])
    for j in range(2):
        for q in range(FOCI):
            for h in range(HALVES):
                line = j * 4 + h * 2 + q
                up_out[j, q : q + 1, h * LANES : (h + 1) * LANES] = own[line : line + 1]
    rounded = up.astype(BF16)
    for place in range(out.shape[0]):
        out[place] = rounded


def correlate_kernel(upgoing, refl, fwd_high, fwd_low, inv_high, inv_low, out, rows, spectrum, product):
    for place in range(16):
        rows[place * SHARE : (place + 1) * SHARE, :] = upgoing[place].astype(F32)
    traces = jnp.concatenate(
        [
            jnp.concatenate(
                [rows[pl.ds(h * FOCI + q, SHOTS_HERE, 2 * FOCI), :] for h in range(HALVES)], axis=1
            )
            for q in range(FOCI)
        ],
        axis=0,
    ).astype(BF16)
    spectrum[...] = to_spectrum(traces, fwd_high, fwd_low)
    for chunk in range(2):
        re_lanes = slice(chunk * LANES, (chunk + 1) * LANES)
        im_lanes = slice(LAGS + chunk * LANES, LAGS + (chunk + 1) * LANES)
        for r in range(RCV_HERE):
            totals = [jnp.zeros((8, LANES), F32) for _ in range(2 * FOCI)]
            for begin in range(0, SHOTS_HERE, 8):
                re = refl[chunk, r * SHOTS_HERE + begin : r * SHOTS_HERE + begin + 8, :]
                im = refl[2 + chunk, r * SHOTS_HERE + begin : r * SHOTS_HERE + begin + 8, :]
                for q in range(FOCI):
                    lines = slice(q * SHOTS_HERE + begin, q * SHOTS_HERE + begin + 8)
                    u_re = spectrum[lines, re_lanes]
                    u_im = spectrum[lines, im_lanes]
                    totals[2 * q] += re * u_re + im * u_im
                    totals[2 * q + 1] += re * u_im - im * u_re
            for q in range(FOCI):
                line = q * RCV_HERE + r
                product[line : line + 1, re_lanes] = jnp.sum(totals[2 * q], axis=0, keepdims=True)
                product[line : line + 1, im_lanes] = jnp.sum(totals[2 * q + 1], axis=0, keepdims=True)
    scale = 1.0 / (LAGS * math.sqrt(SHOTS_HERE * SHOT_AXIS * LAGS))
    result = to_traces(product[...], inv_high, inv_low, scale)
    for place in range(SHOT_AXIS):
        out[place] = result


def add_down(mask, parts, start):
    total = parts[0]
    for place in range(1, SHOT_AXIS):
        total = total + parts[place]
    return start[...].astype(F32) + jnp.where(mask[...] != 0, total, 0.0)


def next_kernel(mask, parts, start, refl, fwd_high, fwd_low, inv_high, inv_low, out, spectrum, product, rows):
    field = add_down(mask, parts, start).astype(BF16)
    convolve_in(field, refl, fwd_high, fwd_low, inv_high, inv_low, out, spectrum, product, rows)


def last_kernel(mask, parts, start, out):
    down = add_down(mask, parts, start)
    share = LAGS // SHOT_AXIS
    begin = lax.axis_index("shot") * share
    mine = pltpu.roll(down, lax.rem(LAGS - begin, LAGS), 1)[:, :share]
    for q in range(FOCI):
        out[:, q, :] = mine[q * RCV_HERE : (q + 1) * RCV_HERE]


VM = pl.BlockSpec(memory_space=pltpu.VMEM)
HB = pl.BlockSpec(memory_space=pltpu.HBM)
LIMIT = 24 * 1024 * 1024


def call(kernel, name, specs, outs, scratch, *args):
    many = len(outs) > 1
    shapes = [jax.ShapeDtypeStruct(shape, dtype) for shape, dtype in outs]
    return pl.pallas_call(
        kernel,
        name=name,
        in_specs=specs,
        out_specs=[VM] * len(outs) if many else VM,
        out_shape=shapes if many else shapes[0],
        scratch_shapes=scratch,
        compiler_params=pltpu.CompilerParams(vmem_limit_bytes=LIMIT),
    )(*args)


def over_plane():
    places = np.arange(RCV_AXIS).reshape(4, 2, 4)
    return places.transpose(1, 0, 2).reshape(2, 16).tolist()


def on_device(reflection, focus_index, shot_window, rcv_window):
    shot_window = jnp.transpose(shot_window, (0, 2, 1))
    rcv_window = jnp.transpose(rcv_window, (0, 2, 1))
    traces = FOCI * RCV_HERE
    fields = pltpu.VMEM((traces, 2 * LAGS), F32)
    products = pltpu.VMEM((FOCI * SHOTS_HERE, 2 * LAGS), F32)
    rows = pltpu.VMEM((FOCI * HALVES * SHOTS_HERE, LANES), F32)
    conv_scratch = [fields, products, rows]
    corr_scratch = [rows, products, fields]
    conv_out = ((RCV_AXIS, SHARE, LANES), F32)
    sources = [focus_index, shot_window, rcv_window, reflection] + [jnp.asarray(table) for table in tables()]
    picks, refl, shot_mask, rcv_mask, *waves, flip = call(
        prepare_kernel, "preparation", [HB] * 9,
        [
            ((SHOT_AXIS, traces, LAGS), BF16),
            ((4, RCV_HERE * SHOTS_HERE, LANES), F32),
            ((SHARE, LANES), jnp.int32),
            ((traces, LAGS), jnp.int32),
            ((LAGS, 2 * LAGS), BF16),
            ((LAGS, 2 * LAGS), BF16),
            ((2 * LAGS, LAGS), BF16),
            ((2 * LAGS, LAGS), BF16),
            ((LAGS, LAGS), BF16),
        ],
        [
            pltpu.SMEM((FOCI,), jnp.int32), pltpu.SMEM((2, FOCI, SHOTS_HERE), jnp.int32),
            pltpu.SMEM((2, FOCI, RCV_HERE), jnp.int32),
            pltpu.VMEM((SHOTS_HERE, RCV_HERE, LAGS), BF16),
            pltpu.VMEM((traces, LANES), jnp.int32), pltpu.VMEM((traces, LANES), jnp.int32),
            pltpu.SemaphoreType.DMA((12,)),
        ],
        *[pltpu.with_memory_space_constraint(source, pltpu.HBM) for source in sources],
    )
    picked = lax.all_to_all(picks, "shot", 0, 0, tiled=True)
    start, partial = call(
        first_kernel, "first_convolution", [VM] * 7, [((traces, LAGS), BF16), conv_out], conv_scratch,
        picked, flip, refl, *waves,
    )
    for iteration in range(ITERS):
        parts = lax.all_to_all(partial, "rcv", 0, 0, tiled=True)
        focus_up, rounded = call(
            upgoing_kernel, "upgoing", [VM, VM],
            [((2, FOCI, LAGS), F32), ((16, SHARE, LANES), BF16)], [], shot_mask, parts,
        )
        upgoing = lax.all_to_all(rounded, "rcv", 0, 0, tiled=True, axis_index_groups=over_plane())
        partial = call(
            correlate_kernel, "correlation", [VM] * 6, [((SHOT_AXIS, traces, LAGS), F32)], corr_scratch,
            upgoing, refl, *waves,
        )
        parts = lax.all_to_all(partial, "shot", 0, 0, tiled=True)
        if iteration + 1 < ITERS:
            partial = call(
                next_kernel, "next_convolution", [VM] * 8, [conv_out], conv_scratch,
                rcv_mask, parts, start, refl, *waves,
            )
    share = LAGS // SHOT_AXIS
    focus_down = call(
        last_kernel, "downgoing", [VM, VM, VM], [((RCV_HERE, FOCI, share), F32)], [], rcv_mask, parts, start
    )
    return focus_down, focus_up


def solution(mesh):
    return jax.shard_map(
        on_device,
        mesh=mesh,
        in_specs=(P("shot", "rcv", None), P(), P(None, "shot", None), P(None, "rcv", None)),
        out_specs=(P("rcv", None, "shot"), P(("shot", "rcv"), None, None)),
        check_vma=False,
    )
```

```python
import functools
import math

import jax
import jax.numpy as jnp
import ml_dtypes
import numpy as np
from jax import lax
from jax.experimental import pallas as pl
from jax.experimental.pallas import tpu as pltpu
from jax.sharding import PartitionSpec as P


ITERS = 2
LAGS = 256
LANES = 128
FOCI = 2
SHOTS_HERE = 64
RCV_HERE = 16
RCV_AXIS = 32
SHOT_AXIS = 8
SHARE = SHOTS_HERE * FOCI * 2 // 16
HALVES = LAGS // LANES
SHARE_LAGS = LAGS // SHOT_AXIS
F32 = jnp.float32
BF16 = jnp.bfloat16


def split_bf16(matrix):
    high = matrix.astype(ml_dtypes.bfloat16)
    low = (matrix - high.astype(np.float64)).astype(ml_dtypes.bfloat16)
    return high, low


def tables():
    times = np.arange(LAGS)[:, None]
    angles = (np.arange(LAGS)[None, :] + 0.5) * (np.pi / LAGS) * times
    forward = np.concatenate([np.cos(angles), -np.sin(angles)], axis=1)
    fwd_high, fwd_low = split_bf16(forward)
    inv_high, inv_low = split_bf16(np.ascontiguousarray(forward.T))
    flip = np.ascontiguousarray(np.eye(LAGS)[::-1]).astype(ml_dtypes.bfloat16)
    return fwd_high, fwd_low, inv_high, inv_low, flip


def dot(left, right):
    return jnp.dot(left, right, preferred_element_type=F32)


def to_spectrum(traces, high, low):
    return dot(traces, high[...]) + dot(traces, low[...])


def to_traces(spectrum, high, low, scale):
    top = spectrum.astype(BF16)
    rest = (spectrum - top.astype(F32)).astype(BF16)
    return (dot(top, high[...]) + (dot(top, low[...]) + dot(rest, high[...]))) * scale


def shot_slot(shot):
    y, z, x, j = shot // 16, (shot // 8) % 2, (shot // 2) % 4, shot % 2
    return y * 16 + x * 4 + z * 2 + j


def pick_kernel(focus_hbm, reflection_hbm, out, focus, reflection, sems):
    copies = [
        pltpu.make_async_copy(focus_hbm, focus, sems.at[0]),
        pltpu.make_async_copy(reflection_hbm, reflection, sems.at[1]),
    ]
    for copy in copies:
        copy.start()
    for copy in copies:
        copy.wait()
    first = lax.axis_index("shot") * SHOTS_HERE
    for which in range(FOCI):
        row = focus[which] - first
        inside = jnp.logical_and(row >= 0, row < SHOTS_HERE)
        trace = reflection[jnp.clip(row, 0, SHOTS_HERE - 1)].astype(F32)
        picked = jnp.where(inside, trace, 0.0).astype(BF16)
        for place in range(SHOT_AXIS):
            out[place, which * RCV_HERE : (which + 1) * RCV_HERE, :] = picked


def prepare_kernel(
    shot_hbm, rcv_hbm, reflection_hbm, high_hbm, low_hbm, inv_high_hbm, inv_low_hbm, flip_hbm,
    out, shot_mask, rcv_mask, high, low, inv_high, inv_low, flip,
    shot_window, rcv_window, reflection, onset, ending, sems,
):
    def fetch(source, target, place):
        copy = pltpu.make_async_copy(source, target, sems.at[place])
        copy.start()
        return copy

    step = 16
    tables = [fetch(high_hbm, high, 0), fetch(low_hbm, low, 1)]
    blocks = [
        fetch(reflection_hbm.at[pl.ds(begin, step)], reflection.at[pl.ds(begin, step)], 2 + begin // step)
        for begin in range(0, SHOTS_HERE, step)
    ]
    scalars = [fetch(shot_hbm, shot_window, 6), fetch(rcv_hbm, rcv_window, 7)]
    later = [fetch(inv_high_hbm, inv_high, 8), fetch(inv_low_hbm, inv_low, 9), fetch(flip_hbm, flip, 10)]
    for copy in tables:
        copy.wait()
    for begin in range(0, SHOTS_HERE, step):
        blocks[begin // step].wait()
        lines = reflection[begin : begin + step].reshape(step * RCV_HERE, LAGS)
        spectrum = to_spectrum(lines, high, low)
        for local in range(step):
            piece = spectrum[local * RCV_HERE : (local + 1) * RCV_HERE]
            slot = shot_slot(begin + local)
            for chunk in range(4):
                out[chunk, pl.ds(slot, RCV_HERE, SHOTS_HERE), :] = piece[
                    :, chunk * LANES : (chunk + 1) * LANES
                ]
    for copy in scalars:
        copy.wait()
    for copy in later:
        copy.wait()
    up_mask(shot_window, shot_mask)
    down_mask(rcv_window, rcv_mask, onset, ending)


def up_mask(window, out):
    me = lax.axis_index("rcv")
    corner = (me // 8) * 16 + (me % 4) * 2
    row = lax.broadcasted_iota(jnp.int32, (SHARE, LANES), 0)
    onset = jnp.zeros((SHARE, LANES), jnp.int32)
    ending = jnp.zeros((SHARE, LANES), jnp.int32)
    for z in range(2):
        for j in range(2):
            for q in range(FOCI):
                shot = corner + z * 8 + j
                mine = jnp.logical_and(row // 4 == z * 2 + j, row % 2 == q)
                onset = jnp.where(mine, window[0, q, shot], onset)
                ending = jnp.where(mine, window[1, q, shot], ending)
    time = lax.broadcasted_iota(jnp.int32, (SHARE, LANES), 1) + ((row // 2) % 2) * LANES
    out[...] = jnp.logical_and(time >= onset, time < ending).astype(jnp.int32)


def down_mask(window, out, onset, ending):
    for q in range(FOCI):
        for r in range(RCV_HERE):
            line = q * RCV_HERE + r
            onset[line : line + 1, :] = jnp.full((1, LANES), window[0, q, r], jnp.int32)
            ending[line : line + 1, :] = jnp.full((1, LANES), window[1, q, r], jnp.int32)
    time = lax.broadcasted_iota(jnp.int32, (FOCI * RCV_HERE, LANES), 1)
    for h in range(HALVES):
        inside = jnp.logical_and(time + h * LANES >= onset[...], time + h * LANES < ending[...])
        out[:, h * LANES : (h + 1) * LANES] = inside.astype(jnp.int32)


def convolve_in(field, refl, fwd_high, fwd_low, inv_high, inv_low, out, spectrum, product, rows):
    spectrum[...] = to_spectrum(field, fwd_high, fwd_low)
    for chunk in range(2):
        re_lanes = slice(chunk * LANES, (chunk + 1) * LANES)
        im_lanes = slice(LAGS + chunk * LANES, LAGS + (chunk + 1) * LANES)
        totals = [jnp.zeros((SHOTS_HERE, LANES), F32) for _ in range(2 * FOCI)]
        for r in range(RCV_HERE):
            re = refl[chunk, r * SHOTS_HERE : (r + 1) * SHOTS_HERE, :]
            im = refl[2 + chunk, r * SHOTS_HERE : (r + 1) * SHOTS_HERE, :]
            for q in range(FOCI):
                line = q * RCV_HERE + r
                f_re = spectrum[line : line + 1, re_lanes]
                f_im = spectrum[line : line + 1, im_lanes]
                totals[2 * q] += re * f_re - im * f_im
                totals[2 * q + 1] += re * f_im + im * f_re
        for q in range(FOCI):
            product[q * SHOTS_HERE : (q + 1) * SHOTS_HERE, re_lanes] = totals[2 * q]
            product[q * SHOTS_HERE : (q + 1) * SHOTS_HERE, im_lanes] = totals[2 * q + 1]
    scale = 1.0 / (LAGS * math.sqrt(RCV_HERE * RCV_AXIS * LAGS))
    result = to_traces(product[...], inv_high, inv_low, scale)
    for q in range(FOCI):
        for h in range(HALVES):
            rows[pl.ds(h * FOCI + q, SHOTS_HERE, 2 * FOCI), :] = result[
                q * SHOTS_HERE : (q + 1) * SHOTS_HERE, h * LANES : (h + 1) * LANES
            ]
    for place in range(RCV_AXIS):
        group = (place // 8) * 4 + place % 4
        out[place] = rows[group * SHARE : (group + 1) * SHARE, :]


def first_kernel(
    picked, flip, refl, fwd_high, fwd_low, inv_high, inv_low, start_out, out, spectrum, product, rows
):
    start = picked[0].astype(F32)
    for place in range(1, SHOT_AXIS):
        start = start + picked[place].astype(F32)
    start = dot(start.astype(BF16), flip[...]).astype(BF16)
    start_out[...] = start
    convolve_in(start, refl, fwd_high, fwd_low, inv_high, inv_low, out, spectrum, product, rows)


def upgoing_kernel(mask, parts, up_out, out):
    total = parts[0]
    for place in range(1, RCV_AXIS):
        total = total + parts[place]
    up = jnp.where(mask[...] != 0, total, 0.0)
    own = jnp.where((lax.axis_index("rcv") // 4) % 2 == 0, up[:8], up[8:])
    for j in range(2):
        for q in range(FOCI):
            for h in range(HALVES):
                line = j * 4 + h * 2 + q
                up_out[j, q : q + 1, h * LANES : (h + 1) * LANES] = own[line : line + 1]
    rounded = up.astype(BF16)
    for place in range(out.shape[0]):
        out[place] = rounded


def correlate_in(upgoing, refl, fwd_high, fwd_low, inv_high, inv_low, rows, spectrum, product):
    for place in range(16):
        rows[place * SHARE : (place + 1) * SHARE, :] = upgoing[place].astype(F32)
    traces = jnp.concatenate(
        [
            jnp.concatenate(
                [rows[pl.ds(h * FOCI + q, SHOTS_HERE, 2 * FOCI), :] for h in range(HALVES)], axis=1
            )
            for q in range(FOCI)
        ],
        axis=0,
    ).astype(BF16)
    spectrum[...] = to_spectrum(traces, fwd_high, fwd_low)
    for chunk in range(2):
        re_lanes = slice(chunk * LANES, (chunk + 1) * LANES)
        im_lanes = slice(LAGS + chunk * LANES, LAGS + (chunk + 1) * LANES)
        for r in range(RCV_HERE):
            totals = [jnp.zeros((8, LANES), F32) for _ in range(2 * FOCI)]
            for begin in range(0, SHOTS_HERE, 8):
                re = refl[chunk, r * SHOTS_HERE + begin : r * SHOTS_HERE + begin + 8, :]
                im = refl[2 + chunk, r * SHOTS_HERE + begin : r * SHOTS_HERE + begin + 8, :]
                for q in range(FOCI):
                    lines = slice(q * SHOTS_HERE + begin, q * SHOTS_HERE + begin + 8)
                    u_re = spectrum[lines, re_lanes]
                    u_im = spectrum[lines, im_lanes]
                    totals[2 * q] += re * u_re + im * u_im
                    totals[2 * q + 1] += re * u_im - im * u_re
            for q in range(FOCI):
                line = q * RCV_HERE + r
                product[line : line + 1, re_lanes] = jnp.sum(totals[2 * q], axis=0, keepdims=True)
                product[line : line + 1, im_lanes] = jnp.sum(totals[2 * q + 1], axis=0, keepdims=True)
    scale = 1.0 / (LAGS * math.sqrt(SHOTS_HERE * SHOT_AXIS * LAGS))
    return to_traces(product[...], inv_high, inv_low, scale)


def correlate_kernel(upgoing, refl, fwd_high, fwd_low, inv_high, inv_low, out, rows, spectrum, product):
    out[...] = correlate_in(upgoing, refl, fwd_high, fwd_low, inv_high, inv_low, rows, spectrum, product)


def last_correlate_kernel(upgoing, refl, fwd_high, fwd_low, inv_high, inv_low, out, rows, spectrum, product):
    result = correlate_in(upgoing, refl, fwd_high, fwd_low, inv_high, inv_low, rows, spectrum, product)
    for place in range(SHOT_AXIS):
        piece = result[:, place * SHARE_LAGS : (place + 1) * SHARE_LAGS]
        out[place] = jnp.concatenate([piece[begin : begin + 8] for begin in range(0, FOCI * RCV_HERE, 8)], axis=1)


def pair_kernel(mine, other, out):
    total = mine[...] + other[...]
    for place in range(out.shape[0]):
        out[place] = total


def total_of(parts):
    total = parts[0]
    for place in range(1, parts.shape[0]):
        total = total + parts[place]
    return total


def next_kernel(mask, parts, start, refl, fwd_high, fwd_low, inv_high, inv_low, out, spectrum, product, rows):
    down = start[...].astype(F32) + jnp.where(mask[...] != 0, total_of(parts), 0.0)
    convolve_in(down.astype(BF16), refl, fwd_high, fwd_low, inv_high, inv_low, out, spectrum, product, rows)


def last_kernel(mask, parts, start, out):
    begin = lax.axis_index("shot") * SHARE_LAGS
    shift = lax.rem(LAGS - begin, LAGS)
    start_here = pltpu.roll(start[...].astype(F32), shift, 1)[:, :SHARE_LAGS]
    mask_here = pltpu.roll(mask[...], shift, 1)[:, :SHARE_LAGS]
    total = total_of(parts)
    total = jnp.concatenate([total[:, lane : lane + SHARE_LAGS] for lane in range(0, LANES, SHARE_LAGS)], axis=0)
    down = start_here + jnp.where(mask_here != 0, total, 0.0)
    for q in range(FOCI):
        out[:, q, :] = down[q * RCV_HERE : (q + 1) * RCV_HERE]


VM = pl.BlockSpec(memory_space=pltpu.VMEM)
HB = pl.BlockSpec(memory_space=pltpu.HBM)
LIMIT = 24 * 1024 * 1024


def call(kernel, name, specs, outs, scratch, *args):
    many = len(outs) > 1
    shapes = [jax.ShapeDtypeStruct(shape, dtype) for shape, dtype in outs]
    return pl.pallas_call(
        kernel,
        name=name,
        in_specs=specs,
        out_specs=[VM] * len(outs) if many else VM,
        out_shape=shapes if many else shapes[0],
        scratch_shapes=scratch,
        compiler_params=pltpu.CompilerParams(vmem_limit_bytes=LIMIT),
    )(*args)


def over_plane():
    places = np.arange(RCV_AXIS).reshape(4, 2, 4)
    return places.transpose(1, 0, 2).reshape(2, 16).tolist()


def on_device(reflection, focus_index, shot_window, rcv_window):
    shot_window = jnp.transpose(shot_window, (0, 2, 1))
    rcv_window = jnp.transpose(rcv_window, (0, 2, 1))
    traces = FOCI * RCV_HERE
    fields = pltpu.VMEM((traces, 2 * LAGS), F32)
    products = pltpu.VMEM((FOCI * SHOTS_HERE, 2 * LAGS), F32)
    rows = pltpu.VMEM((FOCI * HALVES * SHOTS_HERE, LANES), F32)
    conv_scratch = [fields, products, rows]
    corr_scratch = [rows, products, fields]
    conv_out = ((RCV_AXIS, SHARE, LANES), F32)
    def in_hbm(*arrays):
        return [pltpu.with_memory_space_constraint(array, pltpu.HBM) for array in arrays]

    picks = call(
        pick_kernel, "pick", [HB] * 2, [((SHOT_AXIS, traces, LAGS), BF16)],
        [
            pltpu.SMEM((FOCI,), jnp.int32), pltpu.VMEM((SHOTS_HERE, RCV_HERE, LAGS), BF16),
            pltpu.SemaphoreType.DMA((2,)),
        ],
        *in_hbm(focus_index, reflection),
    )
    picked = lax.all_to_all(picks, "shot", 0, 0, tiled=True)
    refl, shot_mask, rcv_mask, *waves, flip = call(
        prepare_kernel, "preparation", [HB] * 8,
        [
            ((4, RCV_HERE * SHOTS_HERE, LANES), F32),
            ((SHARE, LANES), jnp.int32),
            ((traces, LAGS), jnp.int32),
            ((LAGS, 2 * LAGS), BF16),
            ((LAGS, 2 * LAGS), BF16),
            ((2 * LAGS, LAGS), BF16),
            ((2 * LAGS, LAGS), BF16),
            ((LAGS, LAGS), BF16),
        ],
        [
            pltpu.SMEM((2, FOCI, SHOTS_HERE), jnp.int32), pltpu.SMEM((2, FOCI, RCV_HERE), jnp.int32),
            pltpu.VMEM((SHOTS_HERE, RCV_HERE, LAGS), BF16),
            pltpu.VMEM((traces, LANES), jnp.int32), pltpu.VMEM((traces, LANES), jnp.int32),
            pltpu.SemaphoreType.DMA((11,)),
        ],
        *in_hbm(shot_window, rcv_window, reflection, *[jnp.asarray(table) for table in tables()]),
    )
    start, partial = call(
        first_kernel, "first_convolution", [VM] * 7, [((traces, LAGS), BF16), conv_out], conv_scratch,
        picked, flip, refl, *waves,
    )
    for iteration in range(ITERS):
        parts = lax.all_to_all(partial, "rcv", 0, 0, tiled=True)
        focus_up, rounded = call(
            upgoing_kernel, "upgoing", [VM, VM],
            [((2, FOCI, LAGS), F32), ((16, SHARE, LANES), BF16)], [], shot_mask, parts,
        )
        upgoing = lax.all_to_all(rounded, "rcv", 0, 0, tiled=True, axis_index_groups=over_plane())
        if iteration + 1 < ITERS:
            mine = call(
                correlate_kernel, "correlation", [VM] * 6, [((traces, LAGS), F32)], corr_scratch,
                upgoing, refl, *waves,
            )
            other = lax.ppermute(mine, "shot", [(place, place ^ 1) for place in range(SHOT_AXIS)])
            pair = call(pair_kernel, "pair_sum", [VM] * 2, [((SHOT_AXIS // 2, traces, LAGS), F32)], [], mine, other)
            chips = [list(range(core, SHOT_AXIS, 2)) for core in range(2)]
            parts = lax.all_to_all(pair, "shot", 0, 0, tiled=True, axis_index_groups=chips)
            partial = call(
                next_kernel, "next_convolution", [VM] * 8, [conv_out], conv_scratch,
                rcv_mask, parts, start, refl, *waves,
            )
        else:
            partial = call(
                last_correlate_kernel, "last_correlation", [VM] * 6, [((SHOT_AXIS, 8, LANES), F32)],
                corr_scratch, upgoing, refl, *waves,
            )
            parts = lax.all_to_all(partial, "shot", 0, 0, tiled=True)
    focus_down = call(
        last_kernel, "downgoing", [VM, VM, VM], [((RCV_HERE, FOCI, SHARE_LAGS), F32)], [], rcv_mask, parts, start
    )
    return focus_down, focus_up


def solution(mesh):
    return jax.shard_map(
        on_device,
        mesh=mesh,
        in_specs=(P("shot", "rcv", None), P(), P(None, "shot", None), P(None, "rcv", None)),
        out_specs=(P("rcv", None, "shot"), P(("shot", "rcv"), None, None)),
        check_vma=False,
    )
```

```python
import functools
import math

import jax
import jax.numpy as jnp
import ml_dtypes
import numpy as np
from jax import lax
from jax.experimental import pallas as pl
from jax.experimental.pallas import tpu as pltpu
from jax.sharding import PartitionSpec as P


ITERS = 2
LAGS = 256
LANES = 128
FOCI = 2
SHOTS_HERE = 64
RCV_HERE = 16
RCV_AXIS = 32
SHOT_AXIS = 8
SHARE = SHOTS_HERE * FOCI * 2 // 16
HALVES = LAGS // LANES
PLANE = 16
SHARE_LAGS = LAGS // SHOT_AXIS
F32 = jnp.float32
BF16 = jnp.bfloat16


def split_bf16(matrix):
    high = matrix.astype(ml_dtypes.bfloat16)
    low = (matrix - high.astype(np.float64)).astype(ml_dtypes.bfloat16)
    return high, low


def tables():
    times = np.arange(LAGS)[:, None]
    angles = (np.arange(LAGS)[None, :] + 0.5) * (np.pi / LAGS) * times
    forward = np.concatenate([np.cos(angles), -np.sin(angles)], axis=1)
    fwd_high, fwd_low = split_bf16(forward)
    inv_high, inv_low = split_bf16(np.ascontiguousarray(forward.T))
    flip = np.ascontiguousarray(np.eye(LAGS)[::-1]).astype(ml_dtypes.bfloat16)
    return fwd_high, fwd_low, inv_high, inv_low, flip


def dot(left, right):
    return jnp.dot(left, right, preferred_element_type=F32)


def to_spectrum(traces, high, low):
    return dot(traces, high[...]) + dot(traces, low[...])


def to_traces(spectrum, high, low, scale):
    top = spectrum.astype(BF16)
    rest = (spectrum - top.astype(F32)).astype(BF16)
    return (dot(top, high[...]) + (dot(top, low[...]) + dot(rest, high[...]))) * scale


def shot_slot(shot):
    y, z, x, j = shot // 16, (shot // 8) % 2, (shot // 2) % 4, shot % 2
    return y * 16 + x * 4 + z * 2 + j


def pick_kernel(focus_hbm, reflection_hbm, out, focus, reflection, sems):
    copies = [
        pltpu.make_async_copy(focus_hbm, focus, sems.at[0]),
        pltpu.make_async_copy(reflection_hbm, reflection, sems.at[1]),
    ]
    for copy in copies:
        copy.start()
    for copy in copies:
        copy.wait()
    first = lax.axis_index("shot") * SHOTS_HERE
    for which in range(FOCI):
        row = focus[which] - first
        inside = jnp.logical_and(row >= 0, row < SHOTS_HERE)
        trace = reflection[jnp.clip(row, 0, SHOTS_HERE - 1)].astype(F32)
        picked = jnp.where(inside, trace, 0.0).astype(BF16)
        for place in range(SHOT_AXIS):
            out[place, which * RCV_HERE : (which + 1) * RCV_HERE, :] = picked


def prepare_kernel(
    shot_hbm, rcv_hbm, reflection_hbm, high_hbm, low_hbm, inv_high_hbm, inv_low_hbm, flip_hbm,
    out, shot_mask, rcv_mask, high, low, inv_high, inv_low, flip,
    shot_window, rcv_window, reflection, onset, ending, sems,
):
    def fetch(source, target, place):
        copy = pltpu.make_async_copy(source, target, sems.at[place])
        copy.start()
        return copy

    step = 16
    tables = [fetch(high_hbm, high, 0), fetch(low_hbm, low, 1)]
    blocks = [
        fetch(reflection_hbm.at[pl.ds(begin, step)], reflection.at[pl.ds(begin, step)], 2 + begin // step)
        for begin in range(0, SHOTS_HERE, step)
    ]
    scalars = [fetch(shot_hbm, shot_window, 6), fetch(rcv_hbm, rcv_window, 7)]
    later = [fetch(inv_high_hbm, inv_high, 8), fetch(inv_low_hbm, inv_low, 9), fetch(flip_hbm, flip, 10)]
    for copy in tables:
        copy.wait()
    for begin in range(0, SHOTS_HERE, step):
        blocks[begin // step].wait()
        lines = reflection[begin : begin + step].reshape(step * RCV_HERE, LAGS)
        spectrum = to_spectrum(lines, high, low)
        for local in range(step):
            piece = spectrum[local * RCV_HERE : (local + 1) * RCV_HERE]
            slot = shot_slot(begin + local)
            for chunk in range(4):
                out[chunk, pl.ds(slot, RCV_HERE, SHOTS_HERE), :] = piece[
                    :, chunk * LANES : (chunk + 1) * LANES
                ]
    for copy in scalars:
        copy.wait()
    for copy in later:
        copy.wait()
    up_mask(shot_window, shot_mask)
    down_mask(rcv_window, rcv_mask, onset, ending)


def up_mask(window, out):
    me = lax.axis_index("rcv")
    corner = (me // 8) * 16 + (me % 4) * 2
    row = lax.broadcasted_iota(jnp.int32, (SHARE, LANES), 0)
    onset = jnp.zeros((SHARE, LANES), jnp.int32)
    ending = jnp.zeros((SHARE, LANES), jnp.int32)
    for z in range(2):
        for j in range(2):
            for q in range(FOCI):
                shot = corner + z * 8 + j
                mine = jnp.logical_and(row // 4 == z * 2 + j, row % 2 == q)
                onset = jnp.where(mine, window[0, q, shot], onset)
                ending = jnp.where(mine, window[1, q, shot], ending)
    time = lax.broadcasted_iota(jnp.int32, (SHARE, LANES), 1) + ((row // 2) % 2) * LANES
    out[...] = jnp.logical_and(time >= onset, time < ending).astype(jnp.int32)


def down_mask(window, out, onset, ending):
    for q in range(FOCI):
        for r in range(RCV_HERE):
            line = q * RCV_HERE + r
            onset[line : line + 1, :] = jnp.full((1, LANES), window[0, q, r], jnp.int32)
            ending[line : line + 1, :] = jnp.full((1, LANES), window[1, q, r], jnp.int32)
    time = lax.broadcasted_iota(jnp.int32, (FOCI * RCV_HERE, LANES), 1)
    for h in range(HALVES):
        inside = jnp.logical_and(time + h * LANES >= onset[...], time + h * LANES < ending[...])
        out[:, h * LANES : (h + 1) * LANES] = inside.astype(jnp.int32)


def convolve_in(field, refl, fwd_high, fwd_low, inv_high, inv_low, out, spectrum, product, rows):
    spectrum[...] = to_spectrum(field, fwd_high, fwd_low)
    for chunk in range(2):
        re_lanes = slice(chunk * LANES, (chunk + 1) * LANES)
        im_lanes = slice(LAGS + chunk * LANES, LAGS + (chunk + 1) * LANES)
        totals = [jnp.zeros((SHOTS_HERE, LANES), F32) for _ in range(2 * FOCI)]
        for r in range(RCV_HERE):
            re = refl[chunk, r * SHOTS_HERE : (r + 1) * SHOTS_HERE, :]
            im = refl[2 + chunk, r * SHOTS_HERE : (r + 1) * SHOTS_HERE, :]
            for q in range(FOCI):
                line = q * RCV_HERE + r
                f_re = spectrum[line : line + 1, re_lanes]
                f_im = spectrum[line : line + 1, im_lanes]
                totals[2 * q] += re * f_re - im * f_im
                totals[2 * q + 1] += re * f_im + im * f_re
        for q in range(FOCI):
            product[q * SHOTS_HERE : (q + 1) * SHOTS_HERE, re_lanes] = totals[2 * q]
            product[q * SHOTS_HERE : (q + 1) * SHOTS_HERE, im_lanes] = totals[2 * q + 1]
    scale = 1.0 / (LAGS * math.sqrt(RCV_HERE * RCV_AXIS * LAGS))
    result = to_traces(product[...], inv_high, inv_low, scale)
    for q in range(FOCI):
        for h in range(HALVES):
            rows[pl.ds(h * FOCI + q, SHOTS_HERE, 2 * FOCI), :] = result[
                q * SHOTS_HERE : (q + 1) * SHOTS_HERE, h * LANES : (h + 1) * LANES
            ]
    for place in range(PLANE):
        out[place] = rows[place * SHARE : (place + 1) * SHARE, :]


def first_kernel(
    picked, flip, refl, fwd_high, fwd_low, inv_high, inv_low, start_out, out, spectrum, product, rows
):
    start = picked[0].astype(F32)
    for place in range(1, SHOT_AXIS):
        start = start + picked[place].astype(F32)
    start = dot(start.astype(BF16), flip[...]).astype(BF16)
    start_out[...] = start
    convolve_in(start, refl, fwd_high, fwd_low, inv_high, inv_low, out, spectrum, product, rows)


def sum_kernel(parts, out):
    out[...] = total_of(parts)


def upgoing_kernel(mask, mine, other, *outs):
    up = jnp.where(mask[...] != 0, mine[...] + other[...], 0.0)
    if len(outs) > 1:
        outs[1][...] = jnp.where((lax.axis_index("rcv") // 4) % 2 == 0, up[:8], up[8:])
    rounded = up.astype(BF16)
    for place in range(PLANE):
        outs[0][place] = rounded


def correlate_in(upgoing, refl, fwd_high, fwd_low, inv_high, inv_low, rows, spectrum, product):
    for place in range(PLANE):
        rows[place * SHARE : (place + 1) * SHARE, :] = upgoing[place].astype(F32)
    traces = jnp.concatenate(
        [
            jnp.concatenate(
                [rows[pl.ds(h * FOCI + q, SHOTS_HERE, 2 * FOCI), :] for h in range(HALVES)], axis=1
            )
            for q in range(FOCI)
        ],
        axis=0,
    ).astype(BF16)
    spectrum[...] = to_spectrum(traces, fwd_high, fwd_low)
    for chunk in range(2):
        re_lanes = slice(chunk * LANES, (chunk + 1) * LANES)
        im_lanes = slice(LAGS + chunk * LANES, LAGS + (chunk + 1) * LANES)
        for r in range(RCV_HERE):
            totals = [jnp.zeros((8, LANES), F32) for _ in range(2 * FOCI)]
            for begin in range(0, SHOTS_HERE, 8):
                re = refl[chunk, r * SHOTS_HERE + begin : r * SHOTS_HERE + begin + 8, :]
                im = refl[2 + chunk, r * SHOTS_HERE + begin : r * SHOTS_HERE + begin + 8, :]
                for q in range(FOCI):
                    lines = slice(q * SHOTS_HERE + begin, q * SHOTS_HERE + begin + 8)
                    u_re = spectrum[lines, re_lanes]
                    u_im = spectrum[lines, im_lanes]
                    totals[2 * q] += re * u_re + im * u_im
                    totals[2 * q + 1] += re * u_im - im * u_re
            for q in range(FOCI):
                line = q * RCV_HERE + r
                product[line : line + 1, re_lanes] = jnp.sum(totals[2 * q], axis=0, keepdims=True)
                product[line : line + 1, im_lanes] = jnp.sum(totals[2 * q + 1], axis=0, keepdims=True)
    scale = 1.0 / (LAGS * math.sqrt(SHOTS_HERE * SHOT_AXIS * LAGS))
    return to_traces(product[...], inv_high, inv_low, scale)


def correlate_kernel(upgoing, refl, fwd_high, fwd_low, inv_high, inv_low, out, rows, spectrum, product):
    out[...] = correlate_in(upgoing, refl, fwd_high, fwd_low, inv_high, inv_low, rows, spectrum, product)


def last_correlate_kernel(upgoing, refl, fwd_high, fwd_low, inv_high, inv_low, out, rows, spectrum, product):
    result = correlate_in(upgoing, refl, fwd_high, fwd_low, inv_high, inv_low, rows, spectrum, product)
    for place in range(SHOT_AXIS):
        piece = result[:, place * SHARE_LAGS : (place + 1) * SHARE_LAGS]
        out[place] = jnp.concatenate([piece[begin : begin + 8] for begin in range(0, FOCI * RCV_HERE, 8)], axis=1)


def pair_kernel(mine, other, out):
    out[...] = mine[...] + other[...]


def total_of(parts):
    total = parts[0]
    for place in range(1, parts.shape[0]):
        total = total + parts[place]
    return total


def next_kernel(
    mask, mine, other, start, refl, fwd_high, fwd_low, inv_high, inv_low, out, spectrum, product, rows
):
    down = start[...].astype(F32) + jnp.where(mask[...] != 0, mine[...] + other[...], 0.0)
    convolve_in(down.astype(BF16), refl, fwd_high, fwd_low, inv_high, inv_low, out, spectrum, product, rows)


def last_kernel(mask, parts, start, own, out, up_out):
    begin = lax.axis_index("shot") * SHARE_LAGS
    shift = lax.rem(LAGS - begin, LAGS)
    start_here = pltpu.roll(start[...].astype(F32), shift, 1)[:, :SHARE_LAGS]
    mask_here = pltpu.roll(mask[...], shift, 1)[:, :SHARE_LAGS]
    total = total_of(parts)
    total = jnp.concatenate([total[:, lane : lane + SHARE_LAGS] for lane in range(0, LANES, SHARE_LAGS)], axis=0)
    down = start_here + jnp.where(mask_here != 0, total, 0.0)
    for q in range(FOCI):
        out[:, q, :] = down[q * RCV_HERE : (q + 1) * RCV_HERE]
    for j in range(2):
        for q in range(FOCI):
            for h in range(HALVES):
                line = j * 4 + h * 2 + q
                up_out[j, q : q + 1, h * LANES : (h + 1) * LANES] = own[line : line + 1]


VM = pl.BlockSpec(memory_space=pltpu.VMEM)
HB = pl.BlockSpec(memory_space=pltpu.HBM)
LIMIT = 24 * 1024 * 1024


def call(kernel, name, specs, outs, scratch, *args):
    many = len(outs) > 1
    shapes = [jax.ShapeDtypeStruct(*out) if isinstance(out, tuple) else out for out in outs]
    return pl.pallas_call(
        kernel,
        name=name,
        in_specs=specs,
        out_specs=[VM] * len(outs) if many else VM,
        out_shape=shapes if many else shapes[0],
        scratch_shapes=scratch,
        compiler_params=pltpu.CompilerParams(vmem_limit_bytes=LIMIT),
    )(*args)


def over_plane():
    places = np.arange(RCV_AXIS).reshape(4, 2, 4)
    return places.transpose(1, 0, 2).reshape(2, 16).tolist()


def on_device(reflection, focus_index, shot_window, rcv_window):
    shot_window = jnp.transpose(shot_window, (0, 2, 1))
    rcv_window = jnp.transpose(rcv_window, (0, 2, 1))
    traces = FOCI * RCV_HERE
    fields = pltpu.VMEM((traces, 2 * LAGS), F32)
    products = pltpu.VMEM((FOCI * SHOTS_HERE, 2 * LAGS), F32)
    rows = pltpu.VMEM((FOCI * HALVES * SHOTS_HERE, LANES), F32)
    conv_scratch = [fields, products, rows]
    corr_scratch = [rows, products, fields]
    conv_out = ((PLANE, SHARE, LANES), F32)
    def in_hbm(*arrays):
        return [pltpu.with_memory_space_constraint(array, pltpu.HBM) for array in arrays]

    picks = call(
        pick_kernel, "pick", [HB] * 2, [pltpu.VMEM((SHOT_AXIS, traces, LAGS), BF16)],
        [
            pltpu.SMEM((FOCI,), jnp.int32), pltpu.VMEM((SHOTS_HERE, RCV_HERE, LAGS), BF16),
            pltpu.SemaphoreType.DMA((2,)),
        ],
        *in_hbm(focus_index, reflection),
    )
    picked = lax.all_to_all(picks, "shot", 0, 0, tiled=True)
    refl, shot_mask, rcv_mask, *waves, flip = call(
        prepare_kernel, "preparation", [HB] * 8,
        [
            ((4, RCV_HERE * SHOTS_HERE, LANES), F32),
            ((SHARE, LANES), jnp.int32),
            ((traces, LAGS), jnp.int32),
            ((LAGS, 2 * LAGS), BF16),
            ((LAGS, 2 * LAGS), BF16),
            ((2 * LAGS, LAGS), BF16),
            ((2 * LAGS, LAGS), BF16),
            ((LAGS, LAGS), BF16),
        ],
        [
            pltpu.SMEM((2, FOCI, SHOTS_HERE), jnp.int32), pltpu.SMEM((2, FOCI, RCV_HERE), jnp.int32),
            pltpu.VMEM((SHOTS_HERE, RCV_HERE, LAGS), BF16),
            pltpu.VMEM((traces, LANES), jnp.int32), pltpu.VMEM((traces, LANES), jnp.int32),
            pltpu.SemaphoreType.DMA((11,)),
        ],
        *in_hbm(shot_window, rcv_window, reflection, *[jnp.asarray(table) for table in tables()]),
    )
    start, partial = call(
        first_kernel, "first_convolution", [VM] * 7, [((traces, LAGS), BF16), conv_out], conv_scratch,
        picked, flip, refl, *waves,
    )
    for iteration in range(ITERS):
        parts = lax.all_to_all(partial, "rcv", 0, 0, tiled=True, axis_index_groups=over_plane())
        mine = call(sum_kernel, "plane_sum", [VM], [((SHARE, LANES), F32)], [], parts)
        other = lax.ppermute(mine, "rcv", [(place, place ^ 4) for place in range(RCV_AXIS)])
        outs = [((PLANE, SHARE, LANES), BF16)]
        if iteration + 1 < ITERS:
            rounded = call(upgoing_kernel, "upgoing", [VM] * 3, outs, [], shot_mask, mine, other)
        else:
            rounded, own = call(
                upgoing_kernel, "last_upgoing", [VM] * 3, outs + [((8, LANES), F32)], [], shot_mask, mine, other
            )
        upgoing = lax.all_to_all(rounded, "rcv", 0, 0, tiled=True, axis_index_groups=over_plane())
        if iteration + 1 < ITERS:
            mine = call(
                correlate_kernel, "correlation", [VM] * 6, [((traces, LAGS), F32)], corr_scratch,
                upgoing, refl, *waves,
            )
            for step in (1, 2, 4):
                other = lax.ppermute(mine, "shot", [(place, place ^ step) for place in range(SHOT_AXIS)])
                if step < 4:
                    mine = call(pair_kernel, "pair_sum", [VM] * 2, [((traces, LAGS), F32)], [], mine, other)
            partial = call(
                next_kernel, "next_convolution", [VM] * 9, [conv_out], conv_scratch,
                rcv_mask, mine, other, start, refl, *waves,
            )
        else:
            partial = call(
                last_correlate_kernel, "last_correlation", [VM] * 6, [((SHOT_AXIS, 8, LANES), F32)],
                corr_scratch, upgoing, refl, *waves,
            )
            parts = lax.all_to_all(partial, "shot", 0, 0, tiled=True)
    focus_down, focus_up = call(
        last_kernel, "downgoing", [VM] * 4, [((RCV_HERE, FOCI, SHARE_LAGS), F32), ((2, FOCI, LAGS), F32)], [],
        rcv_mask, parts, start, own,
    )
    return focus_down, focus_up


def solution(mesh):
    return jax.shard_map(
        on_device,
        mesh=mesh,
        in_specs=(P("shot", "rcv", None), P(), P(None, "shot", None), P(None, "rcv", None)),
        out_specs=(P("rcv", None, "shot"), P(("shot", "rcv"), None, None)),
        check_vma=False,
    )
```

```python
import functools
import math

import jax
import jax.numpy as jnp
import ml_dtypes
import numpy as np
from jax import lax
from jax.experimental import pallas as pl
from jax.experimental.pallas import tpu as pltpu
from jax.sharding import PartitionSpec as P


ITERS = 2
LAGS = 256
LANES = 128
FOCI = 2
SHOTS_HERE = 64
RCV_HERE = 16
RCV_AXIS = 32
SHOT_AXIS = 8
SHARE = SHOTS_HERE * FOCI * 2 // 16
HALVES = LAGS // LANES
PLANE = 16
SHARE_LAGS = LAGS // SHOT_AXIS
F32 = jnp.float32
BF16 = jnp.bfloat16


def split_bf16(matrix):
    high = matrix.astype(ml_dtypes.bfloat16)
    low = (matrix - high.astype(np.float64)).astype(ml_dtypes.bfloat16)
    return high, low


def tables():
    times = np.arange(LAGS)[:, None]
    angles = (np.arange(LAGS)[None, :] + 0.5) * (np.pi / LAGS) * times
    forward = np.concatenate([np.cos(angles), -np.sin(angles)], axis=1)
    fwd_high, fwd_low = split_bf16(forward)
    inv_high, inv_low = split_bf16(np.ascontiguousarray(forward.T))
    flip = np.ascontiguousarray(np.eye(LAGS)[::-1]).astype(ml_dtypes.bfloat16)
    return fwd_high, fwd_low, inv_high, inv_low, flip


def dot(left, right):
    return jnp.dot(left, right, preferred_element_type=F32)


def to_spectrum(traces, high, low):
    return dot(traces, high[...]) + dot(traces, low[...])


def to_traces(spectrum, high, low, scale):
    top = spectrum.astype(BF16)
    rest = (spectrum - top.astype(F32)).astype(BF16)
    both = dot(jnp.concatenate([top, rest], axis=0), high[...])
    count = spectrum.shape[0]
    return (both[:count] + (dot(top, low[...]) + both[count:])) * scale


def factors(spectrum):
    re, im = spectrum[:, :LAGS], spectrum[:, LAGS:]
    return re, im - re, im + re


def shot_slot(shot):
    y, z, x, j = shot // 16, (shot // 8) % 2, (shot // 2) % 4, shot % 2
    return y * 16 + x * 4 + z * 2 + j


def pick_kernel(focus_hbm, reflection_hbm, out, focus, reflection, sems):
    copies = [
        pltpu.make_async_copy(focus_hbm, focus, sems.at[0]),
        pltpu.make_async_copy(reflection_hbm, reflection, sems.at[1]),
    ]
    for copy in copies:
        copy.start()
    for copy in copies:
        copy.wait()
    first = lax.axis_index("shot") * SHOTS_HERE
    for which in range(FOCI):
        row = focus[which] - first
        inside = jnp.logical_and(row >= 0, row < SHOTS_HERE)
        trace = reflection[jnp.clip(row, 0, SHOTS_HERE - 1)].astype(F32)
        picked = jnp.where(inside, trace, 0.0).astype(BF16)
        for place in range(SHOT_AXIS):
            out[place, which * RCV_HERE : (which + 1) * RCV_HERE, :] = picked


def prepare_kernel(
    shot_hbm, rcv_hbm, reflection_hbm, high_hbm, low_hbm, inv_high_hbm, inv_low_hbm, flip_hbm,
    out, shot_mask, rcv_mask, high, low, inv_high, inv_low, flip,
    shot_window, rcv_window, reflection, onset, ending, sems,
):
    def fetch(source, target, place):
        copy = pltpu.make_async_copy(source, target, sems.at[place])
        copy.start()
        return copy

    step = 16
    tables = [fetch(high_hbm, high, 0), fetch(low_hbm, low, 1)]
    blocks = [
        fetch(reflection_hbm.at[pl.ds(begin, step)], reflection.at[pl.ds(begin, step)], 2 + begin // step)
        for begin in range(0, SHOTS_HERE, step)
    ]
    scalars = [fetch(shot_hbm, shot_window, 6), fetch(rcv_hbm, rcv_window, 7)]
    later = [fetch(inv_high_hbm, inv_high, 8), fetch(inv_low_hbm, inv_low, 9), fetch(flip_hbm, flip, 10)]
    for copy in tables:
        copy.wait()
    for begin in range(0, SHOTS_HERE, step):
        blocks[begin // step].wait()
        lines = reflection[begin : begin + step].reshape(step * RCV_HERE, LAGS)
        spectrum = to_spectrum(lines, high, low)
        for local in range(step):
            piece = spectrum[local * RCV_HERE : (local + 1) * RCV_HERE]
            slot = shot_slot(begin + local)
            for chunk in range(4):
                out[chunk, pl.ds(slot, RCV_HERE, SHOTS_HERE), :] = piece[
                    :, chunk * LANES : (chunk + 1) * LANES
                ]
    for copy in scalars:
        copy.wait()
    for copy in later:
        copy.wait()
    up_mask(shot_window, shot_mask)
    down_mask(rcv_window, rcv_mask, onset, ending)


def up_mask(window, out):
    me = lax.axis_index("rcv")
    corner = (me // 8) * 16 + (me % 4) * 2
    row = lax.broadcasted_iota(jnp.int32, (SHARE, LANES), 0)
    onset = jnp.zeros((SHARE, LANES), jnp.int32)
    ending = jnp.zeros((SHARE, LANES), jnp.int32)
    for z in range(2):
        for j in range(2):
            for q in range(FOCI):
                shot = corner + z * 8 + j
                mine = jnp.logical_and(row // 4 == z * 2 + j, row % 2 == q)
                onset = jnp.where(mine, window[0, q, shot], onset)
                ending = jnp.where(mine, window[1, q, shot], ending)
    time = lax.broadcasted_iota(jnp.int32, (SHARE, LANES), 1) + ((row // 2) % 2) * LANES
    out[...] = jnp.logical_and(time >= onset, time < ending).astype(jnp.int32)


def down_mask(window, out, onset, ending):
    for q in range(FOCI):
        for r in range(RCV_HERE):
            line = q * RCV_HERE + r
            onset[line : line + 1, :] = jnp.full((1, LANES), window[0, q, r], jnp.int32)
            ending[line : line + 1, :] = jnp.full((1, LANES), window[1, q, r], jnp.int32)
    time = lax.broadcasted_iota(jnp.int32, (FOCI * RCV_HERE, LANES), 1)
    for h in range(HALVES):
        inside = jnp.logical_and(time + h * LANES >= onset[...], time + h * LANES < ending[...])
        out[:, h * LANES : (h + 1) * LANES] = inside.astype(jnp.int32)


def convolve_in(field, refl, fwd_high, fwd_low, inv_high, inv_low, out, spectrum, product, rows):
    for kind, part in enumerate(factors(to_spectrum(field, fwd_high, fwd_low))):
        spectrum[kind] = part
    half = SHOTS_HERE // 2
    for chunk in range(2):
        lanes = slice(chunk * LANES, (chunk + 1) * LANES)
        im_lanes = slice(LAGS + chunk * LANES, LAGS + (chunk + 1) * LANES)
        for begin in range(0, SHOTS_HERE, half):
            totals = [jnp.zeros((half, LANES), F32) for _ in range(3 * FOCI)]
            for r in range(RCV_HERE):
                lines = slice(r * SHOTS_HERE + begin, r * SHOTS_HERE + begin + half)
                re = refl[chunk, lines, :]
                im = refl[2 + chunk, lines, :]
                both = re + im
                for q in range(FOCI):
                    line = q * RCV_HERE + r
                    for kind, value in enumerate((both, re, im)):
                        totals[3 * q + kind] += value * spectrum[kind, line : line + 1, lanes]
            for q in range(FOCI):
                first, second, third = totals[3 * q : 3 * q + 3]
                lines = slice(q * SHOTS_HERE + begin, q * SHOTS_HERE + begin + half)
                product[lines, lanes] = first - third
                product[lines, im_lanes] = first + second
    scale = 1.0 / (LAGS * math.sqrt(RCV_HERE * RCV_AXIS * LAGS))
    result = to_traces(product[...], inv_high, inv_low, scale)
    for q in range(FOCI):
        for h in range(HALVES):
            rows[pl.ds(h * FOCI + q, SHOTS_HERE, 2 * FOCI), :] = result[
                q * SHOTS_HERE : (q + 1) * SHOTS_HERE, h * LANES : (h + 1) * LANES
            ]
    for place in range(PLANE):
        out[place] = rows[place * SHARE : (place + 1) * SHARE, :]


def first_kernel(
    picked, flip, refl, fwd_high, fwd_low, inv_high, inv_low, start_out, out, spectrum, product, rows
):
    start = picked[0].astype(F32)
    for place in range(1, SHOT_AXIS):
        start = start + picked[place].astype(F32)
    start = dot(start.astype(BF16), flip[...]).astype(BF16)
    start_out[...] = start
    convolve_in(start, refl, fwd_high, fwd_low, inv_high, inv_low, out, spectrum, product, rows)


def sum_kernel(parts, out):
    out[...] = total_of(parts)


def upgoing_kernel(mask, mine, other, *outs):
    up = jnp.where(mask[...] != 0, mine[...] + other[...], 0.0)
    if len(outs) > 1:
        outs[1][...] = jnp.where((lax.axis_index("rcv") // 4) % 2 == 0, up[:8], up[8:])
    rounded = up.astype(BF16)
    for place in range(PLANE):
        outs[0][place] = rounded


def correlate_in(upgoing, refl, fwd_high, fwd_low, inv_high, inv_low, rows, spectrum, product):
    for place in range(PLANE):
        rows[place * SHARE : (place + 1) * SHARE, :] = upgoing[place].astype(F32)
    traces = jnp.concatenate(
        [
            jnp.concatenate(
                [rows[pl.ds(h * FOCI + q, SHOTS_HERE, 2 * FOCI), :] for h in range(HALVES)], axis=1
            )
            for q in range(FOCI)
        ],
        axis=0,
    ).astype(BF16)
    for kind, part in enumerate(factors(to_spectrum(traces, fwd_high, fwd_low))):
        spectrum[kind] = part
    for chunk in range(2):
        lanes = slice(chunk * LANES, (chunk + 1) * LANES)
        im_lanes = slice(LAGS + chunk * LANES, LAGS + (chunk + 1) * LANES)
        for r in range(RCV_HERE):
            totals = [jnp.zeros((8, LANES), F32) for _ in range(3 * FOCI)]
            for begin in range(0, SHOTS_HERE, 8):
                re = refl[chunk, r * SHOTS_HERE + begin : r * SHOTS_HERE + begin + 8, :]
                im = refl[2 + chunk, r * SHOTS_HERE + begin : r * SHOTS_HERE + begin + 8, :]
                both = re - im
                for q in range(FOCI):
                    lines = slice(q * SHOTS_HERE + begin, q * SHOTS_HERE + begin + 8)
                    for kind, value in enumerate((both, re, im)):
                        totals[3 * q + kind] += value * spectrum[kind, lines, lanes]
            for q in range(FOCI):
                line = q * RCV_HERE + r
                first, second, third = totals[3 * q : 3 * q + 3]
                product[line : line + 1, lanes] = jnp.sum(first + third, axis=0, keepdims=True)
                product[line : line + 1, im_lanes] = jnp.sum(first + second, axis=0, keepdims=True)
    scale = 1.0 / (LAGS * math.sqrt(SHOTS_HERE * SHOT_AXIS * LAGS))
    return to_traces(product[...], inv_high, inv_low, scale)


def correlate_kernel(upgoing, refl, fwd_high, fwd_low, inv_high, inv_low, out, rows, spectrum, product):
    out[...] = correlate_in(upgoing, refl, fwd_high, fwd_low, inv_high, inv_low, rows, spectrum, product)


def last_correlate_kernel(upgoing, refl, fwd_high, fwd_low, inv_high, inv_low, out, rows, spectrum, product):
    result = correlate_in(upgoing, refl, fwd_high, fwd_low, inv_high, inv_low, rows, spectrum, product)
    for place in range(SHOT_AXIS):
        piece = result[:, place * SHARE_LAGS : (place + 1) * SHARE_LAGS]
        out[place] = jnp.concatenate([piece[begin : begin + 8] for begin in range(0, FOCI * RCV_HERE, 8)], axis=1)


def pair_kernel(mine, other, out):
    out[...] = mine[...] + other[...]


def total_of(parts):
    total = parts[0]
    for place in range(1, parts.shape[0]):
        total = total + parts[place]
    return total


def next_kernel(
    mask, mine, other, start, refl, fwd_high, fwd_low, inv_high, inv_low, out, spectrum, product, rows
):
    down = start[...].astype(F32) + jnp.where(mask[...] != 0, mine[...] + other[...], 0.0)
    convolve_in(down.astype(BF16), refl, fwd_high, fwd_low, inv_high, inv_low, out, spectrum, product, rows)


def last_kernel(mask, parts, start, own, out, up_out):
    begin = lax.axis_index("shot") * SHARE_LAGS
    shift = lax.rem(LAGS - begin, LAGS)
    start_here = pltpu.roll(start[...].astype(F32), shift, 1)[:, :SHARE_LAGS]
    mask_here = pltpu.roll(mask[...], shift, 1)[:, :SHARE_LAGS]
    total = total_of(parts)
    total = jnp.concatenate([total[:, lane : lane + SHARE_LAGS] for lane in range(0, LANES, SHARE_LAGS)], axis=0)
    down = start_here + jnp.where(mask_here != 0, total, 0.0)
    for q in range(FOCI):
        out[:, q, :] = down[q * RCV_HERE : (q + 1) * RCV_HERE]
    for j in range(2):
        for q in range(FOCI):
            for h in range(HALVES):
                line = j * 4 + h * 2 + q
                up_out[j, q : q + 1, h * LANES : (h + 1) * LANES] = own[line : line + 1]


VM = pl.BlockSpec(memory_space=pltpu.VMEM)
HB = pl.BlockSpec(memory_space=pltpu.HBM)
LIMIT = 24 * 1024 * 1024


def call(kernel, name, specs, outs, scratch, *args):
    many = len(outs) > 1
    shapes = [jax.ShapeDtypeStruct(*out) if isinstance(out, tuple) else out for out in outs]
    return pl.pallas_call(
        kernel,
        name=name,
        in_specs=specs,
        out_specs=[VM] * len(outs) if many else VM,
        out_shape=shapes if many else shapes[0],
        scratch_shapes=scratch,
        compiler_params=pltpu.CompilerParams(vmem_limit_bytes=LIMIT),
    )(*args)


def over_plane():
    places = np.arange(RCV_AXIS).reshape(4, 2, 4)
    return places.transpose(1, 0, 2).reshape(2, 16).tolist()


def on_device(reflection, focus_index, shot_window, rcv_window):
    shot_window = jnp.transpose(shot_window, (0, 2, 1))
    rcv_window = jnp.transpose(rcv_window, (0, 2, 1))
    traces = FOCI * RCV_HERE
    rows = pltpu.VMEM((FOCI * HALVES * SHOTS_HERE, LANES), F32)

    def spectra(count):
        return pltpu.VMEM((3, count, LAGS), F32)

    def products(count):
        return pltpu.VMEM((count, 2 * LAGS), F32)

    conv_scratch = [spectra(traces), products(FOCI * SHOTS_HERE), rows]
    corr_scratch = [rows, spectra(FOCI * SHOTS_HERE), products(traces)]
    conv_out = ((PLANE, SHARE, LANES), F32)
    def in_hbm(*arrays):
        return [pltpu.with_memory_space_constraint(array, pltpu.HBM) for array in arrays]

    picks = call(
        pick_kernel, "pick", [HB] * 2, [pltpu.VMEM((SHOT_AXIS, traces, LAGS), BF16)],
        [
            pltpu.SMEM((FOCI,), jnp.int32), pltpu.VMEM((SHOTS_HERE, RCV_HERE, LAGS), BF16),
            pltpu.SemaphoreType.DMA((2,)),
        ],
        *in_hbm(focus_index, reflection),
    )
    picked = lax.all_to_all(picks, "shot", 0, 0, tiled=True)
    refl, shot_mask, rcv_mask, *waves, flip = call(
        prepare_kernel, "preparation", [HB] * 8,
        [
            ((4, RCV_HERE * SHOTS_HERE, LANES), F32),
            ((SHARE, LANES), jnp.int32),
            ((traces, LAGS), jnp.int32),
            ((LAGS, 2 * LAGS), BF16),
            ((LAGS, 2 * LAGS), BF16),
            ((2 * LAGS, LAGS), BF16),
            ((2 * LAGS, LAGS), BF16),
            ((LAGS, LAGS), BF16),
        ],
        [
            pltpu.SMEM((2, FOCI, SHOTS_HERE), jnp.int32), pltpu.SMEM((2, FOCI, RCV_HERE), jnp.int32),
            pltpu.VMEM((SHOTS_HERE, RCV_HERE, LAGS), BF16),
            pltpu.VMEM((traces, LANES), jnp.int32), pltpu.VMEM((traces, LANES), jnp.int32),
            pltpu.SemaphoreType.DMA((11,)),
        ],
        *in_hbm(shot_window, rcv_window, reflection, *[jnp.asarray(table) for table in tables()]),
    )
    start, partial = call(
        first_kernel, "first_convolution", [VM] * 7, [((traces, LAGS), BF16), conv_out], conv_scratch,
        picked, flip, refl, *waves,
    )
    for iteration in range(ITERS):
        parts = lax.all_to_all(partial, "rcv", 0, 0, tiled=True, axis_index_groups=over_plane())
        mine = call(sum_kernel, "plane_sum", [VM], [((SHARE, LANES), F32)], [], parts)
        other = lax.ppermute(mine, "rcv", [(place, place ^ 4) for place in range(RCV_AXIS)])
        outs = [((PLANE, SHARE, LANES), BF16)]
        if iteration + 1 < ITERS:
            rounded = call(upgoing_kernel, "upgoing", [VM] * 3, outs, [], shot_mask, mine, other)
        else:
            rounded, own = call(
                upgoing_kernel, "last_upgoing", [VM] * 3, outs + [((8, LANES), F32)], [], shot_mask, mine, other
            )
        upgoing = lax.all_to_all(rounded, "rcv", 0, 0, tiled=True, axis_index_groups=over_plane())
        if iteration + 1 < ITERS:
            mine = call(
                correlate_kernel, "correlation", [VM] * 6, [((traces, LAGS), F32)], corr_scratch,
                upgoing, refl, *waves,
            )
            for step in (1, 2, 4):
                other = lax.ppermute(mine, "shot", [(place, place ^ step) for place in range(SHOT_AXIS)])
                if step < 4:
                    mine = call(pair_kernel, "pair_sum", [VM] * 2, [((traces, LAGS), F32)], [], mine, other)
            partial = call(
                next_kernel, "next_convolution", [VM] * 9, [conv_out], conv_scratch,
                rcv_mask, mine, other, start, refl, *waves,
            )
        else:
            partial = call(
                last_correlate_kernel, "last_correlation", [VM] * 6, [((SHOT_AXIS, 8, LANES), F32)],
                corr_scratch, upgoing, refl, *waves,
            )
            parts = lax.all_to_all(partial, "shot", 0, 0, tiled=True)
    focus_down, focus_up = call(
        last_kernel, "downgoing", [VM] * 4, [((RCV_HERE, FOCI, SHARE_LAGS), F32), ((2, FOCI, LAGS), F32)], [],
        rcv_mask, parts, start, own,
    )
    return focus_down, focus_up


def solution(mesh):
    return jax.shard_map(
        on_device,
        mesh=mesh,
        in_specs=(P("shot", "rcv", None), P(), P(None, "shot", None), P(None, "rcv", None)),
        out_specs=(P("rcv", None, "shot"), P(("shot", "rcv"), None, None)),
        check_vma=False,
    )
```

```python
import functools
import math

import jax
import jax.numpy as jnp
import ml_dtypes
import numpy as np
from jax import lax
from jax.experimental import pallas as pl
from jax.experimental.pallas import tpu as pltpu
from jax.sharding import PartitionSpec as P


ITERS = 2
LAGS = 256
LANES = 128
FOCI = 2
SHOTS_HERE = 64
RCV_HERE = 16
RCV_AXIS = 32
SHOT_AXIS = 8
SHARE = SHOTS_HERE * FOCI * 2 // 16
HALVES = LAGS // LANES
PLANE = 16
CHIPS = SHOT_AXIS // 2
SHARE_LAGS = LAGS // SHOT_AXIS
F32 = jnp.float32
BF16 = jnp.bfloat16


def split_bf16(matrix):
    high = matrix.astype(ml_dtypes.bfloat16)
    low = (matrix - high.astype(np.float64)).astype(ml_dtypes.bfloat16)
    return high, low


def tables():
    times = np.arange(LAGS)[:, None]
    angles = (np.arange(LAGS)[None, :] + 0.5) * (np.pi / LAGS) * times
    forward = np.concatenate([np.cos(angles), -np.sin(angles)], axis=1)
    fwd_high, fwd_low = split_bf16(forward)
    inv_high, inv_low = split_bf16(np.ascontiguousarray(forward.T))
    flip = np.ascontiguousarray(np.eye(LAGS)[::-1]).astype(ml_dtypes.bfloat16)
    return fwd_high, fwd_low, inv_high, inv_low, flip


def dot(left, right):
    return jnp.dot(left, right, preferred_element_type=F32)


def to_spectrum(traces, high, low):
    return dot(traces, high[...]) + dot(traces, low[...])


def to_traces(spectrum, high, low, scale):
    top = spectrum.astype(BF16)
    rest = (spectrum - top.astype(F32)).astype(BF16)
    both = dot(jnp.concatenate([top, rest], axis=0), high[...])
    count = spectrum.shape[0]
    return (both[:count] + (dot(top, low[...]) + both[count:])) * scale


def factors(spectrum):
    re, im = spectrum[:, :LAGS], spectrum[:, LAGS:]
    return re, im - re, im + re


def shot_slot(shot):
    y, z, x, j = shot // 16, (shot // 8) % 2, (shot // 2) % 4, shot % 2
    return y * 16 + x * 4 + z * 2 + j


def pick_kernel(focus_hbm, reflection_hbm, out, focus, reflection, sems):
    copies = [
        pltpu.make_async_copy(focus_hbm, focus, sems.at[0]),
        pltpu.make_async_copy(reflection_hbm, reflection, sems.at[1]),
    ]
    for copy in copies:
        copy.start()
    for copy in copies:
        copy.wait()
    first = lax.axis_index("shot") * SHOTS_HERE
    for which in range(FOCI):
        row = focus[which] - first
        inside = jnp.logical_and(row >= 0, row < SHOTS_HERE)
        trace = reflection[jnp.clip(row, 0, SHOTS_HERE - 1)].astype(F32)
        picked = jnp.where(inside, trace, 0.0).astype(BF16)
        out[which * RCV_HERE : (which + 1) * RCV_HERE, :] = picked


def prepare_kernel(
    reflection_hbm, high_hbm, low_hbm, inv_high_hbm, inv_low_hbm, flip_hbm,
    out, high, low, inv_high, inv_low, flip, reflection, sems,
):
    def fetch(source, target, place):
        copy = pltpu.make_async_copy(source, target, sems.at[place])
        copy.start()
        return copy

    step = 16
    tables = [fetch(high_hbm, high, 0), fetch(low_hbm, low, 1)]
    blocks = [
        fetch(reflection_hbm.at[pl.ds(begin, step)], reflection.at[pl.ds(begin, step)], 2 + begin // step)
        for begin in range(0, SHOTS_HERE, step)
    ]
    later = [fetch(inv_high_hbm, inv_high, 6), fetch(inv_low_hbm, inv_low, 7), fetch(flip_hbm, flip, 8)]
    for copy in tables:
        copy.wait()
    for begin in range(0, SHOTS_HERE, step):
        blocks[begin // step].wait()
        lines = reflection[begin : begin + step].reshape(step * RCV_HERE, LAGS)
        spectrum = to_spectrum(lines, high, low)
        for local in range(step):
            piece = spectrum[local * RCV_HERE : (local + 1) * RCV_HERE]
            slot = shot_slot(begin + local)
            for chunk in range(4):
                out[chunk, pl.ds(slot, RCV_HERE, SHOTS_HERE), :] = piece[
                    :, chunk * LANES : (chunk + 1) * LANES
                ]
    for copy in later:
        copy.wait()


def mask_kernel(shot_hbm, rcv_hbm, shot_mask, rcv_mask, shot_window, rcv_window, onset, ending, sems):
    copies = [
        pltpu.make_async_copy(shot_hbm, shot_window, sems.at[0]),
        pltpu.make_async_copy(rcv_hbm, rcv_window, sems.at[1]),
    ]
    for copy in copies:
        copy.start()
    for copy in copies:
        copy.wait()
    up_mask(shot_window, shot_mask)
    down_mask(rcv_window, rcv_mask, onset, ending)


def up_mask(window, out):
    me = lax.axis_index("rcv")
    corner = (me // 8) * 16 + (me % 4) * 2
    row = lax.broadcasted_iota(jnp.int32, (SHARE, LANES), 0)
    onset = jnp.zeros((SHARE, LANES), jnp.int32)
    ending = jnp.zeros((SHARE, LANES), jnp.int32)
    for z in range(2):
        for j in range(2):
            for q in range(FOCI):
                shot = corner + z * 8 + j
                mine = jnp.logical_and(row // 4 == z * 2 + j, row % 2 == q)
                onset = jnp.where(mine, window[0, q, shot], onset)
                ending = jnp.where(mine, window[1, q, shot], ending)
    time = lax.broadcasted_iota(jnp.int32, (SHARE, LANES), 1) + ((row // 2) % 2) * LANES
    out[...] = jnp.logical_and(time >= onset, time < ending).astype(jnp.int32)


def down_mask(window, out, onset, ending):
    for q in range(FOCI):
        for r in range(RCV_HERE):
            line = q * RCV_HERE + r
            onset[line : line + 1, :] = jnp.full((1, LANES), window[0, q, r], jnp.int32)
            ending[line : line + 1, :] = jnp.full((1, LANES), window[1, q, r], jnp.int32)
    time = lax.broadcasted_iota(jnp.int32, (FOCI * RCV_HERE, LANES), 1)
    for h in range(HALVES):
        inside = jnp.logical_and(time + h * LANES >= onset[...], time + h * LANES < ending[...])
        out[:, h * LANES : (h + 1) * LANES] = inside.astype(jnp.int32)


def convolve_in(field, refl, fwd_high, fwd_low, inv_high, inv_low, out, spectrum, product, rows):
    for kind, part in enumerate(factors(to_spectrum(field, fwd_high, fwd_low))):
        spectrum[kind] = part
    half = SHOTS_HERE // 2
    for chunk in range(2):
        lanes = slice(chunk * LANES, (chunk + 1) * LANES)
        im_lanes = slice(LAGS + chunk * LANES, LAGS + (chunk + 1) * LANES)
        for begin in range(0, SHOTS_HERE, half):
            totals = [jnp.zeros((half, LANES), F32) for _ in range(3 * FOCI)]
            for r in range(RCV_HERE):
                lines = slice(r * SHOTS_HERE + begin, r * SHOTS_HERE + begin + half)
                re = refl[chunk, lines, :]
                im = refl[2 + chunk, lines, :]
                both = re + im
                for q in range(FOCI):
                    line = q * RCV_HERE + r
                    for kind, value in enumerate((both, re, im)):
                        totals[3 * q + kind] += value * spectrum[kind, line : line + 1, lanes]
            for q in range(FOCI):
                first, second, third = totals[3 * q : 3 * q + 3]
                lines = slice(q * SHOTS_HERE + begin, q * SHOTS_HERE + begin + half)
                product[lines, lanes] = first - third
                product[lines, im_lanes] = first + second
    scale = 1.0 / (LAGS * math.sqrt(RCV_HERE * RCV_AXIS * LAGS))
    result = to_traces(product[...], inv_high, inv_low, scale)
    for q in range(FOCI):
        for h in range(HALVES):
            rows[pl.ds(h * FOCI + q, SHOTS_HERE, 2 * FOCI), :] = result[
                q * SHOTS_HERE : (q + 1) * SHOTS_HERE, h * LANES : (h + 1) * LANES
            ]
    for place in range(PLANE):
        out[place] = rows[place * SHARE : (place + 1) * SHARE, :]


def gather_kernel(mine, near, middle, far, flip, out):
    total = (mine[...].astype(F32) + near[...].astype(F32)) + (middle[...].astype(F32) + far[...].astype(F32))
    out[...] = dot(total.astype(BF16), flip[...]).astype(BF16)


def first_kernel(
    mine, other, refl, fwd_high, fwd_low, inv_high, inv_low, start_out, out, spectrum, product, rows
):
    start = (mine[...].astype(F32) + other[...].astype(F32)).astype(BF16)
    start_out[...] = start
    convolve_in(start, refl, fwd_high, fwd_low, inv_high, inv_low, out, spectrum, product, rows)


def sum_kernel(parts, out):
    out[...] = total_of(parts)


def upgoing_kernel(mask, mine, other, *outs):
    up = jnp.where(mask[...] != 0, mine[...] + other[...], 0.0)
    if len(outs) > 1:
        outs[1][...] = jnp.where((lax.axis_index("rcv") // 4) % 2 == 0, up[:8], up[8:])
    rounded = up.astype(BF16)
    for place in range(PLANE):
        outs[0][place] = rounded


def correlate_in(upgoing, refl, fwd_high, fwd_low, inv_high, inv_low, rows, spectrum, product):
    for place in range(PLANE):
        rows[place * SHARE : (place + 1) * SHARE, :] = upgoing[place].astype(F32)
    traces = jnp.concatenate(
        [
            jnp.concatenate(
                [rows[pl.ds(h * FOCI + q, SHOTS_HERE, 2 * FOCI), :] for h in range(HALVES)], axis=1
            )
            for q in range(FOCI)
        ],
        axis=0,
    ).astype(BF16)
    for kind, part in enumerate(factors(to_spectrum(traces, fwd_high, fwd_low))):
        spectrum[kind] = part
    for chunk in range(2):
        lanes = slice(chunk * LANES, (chunk + 1) * LANES)
        im_lanes = slice(LAGS + chunk * LANES, LAGS + (chunk + 1) * LANES)
        for r in range(RCV_HERE):
            totals = [jnp.zeros((8, LANES), F32) for _ in range(3 * FOCI)]
            for begin in range(0, SHOTS_HERE, 8):
                re = refl[chunk, r * SHOTS_HERE + begin : r * SHOTS_HERE + begin + 8, :]
                im = refl[2 + chunk, r * SHOTS_HERE + begin : r * SHOTS_HERE + begin + 8, :]
                both = re - im
                for q in range(FOCI):
                    lines = slice(q * SHOTS_HERE + begin, q * SHOTS_HERE + begin + 8)
                    for kind, value in enumerate((both, re, im)):
                        totals[3 * q + kind] += value * spectrum[kind, lines, lanes]
            for q in range(FOCI):
                line = q * RCV_HERE + r
                first, second, third = totals[3 * q : 3 * q + 3]
                product[line : line + 1, lanes] = jnp.sum(first + third, axis=0, keepdims=True)
                product[line : line + 1, im_lanes] = jnp.sum(first + second, axis=0, keepdims=True)
    scale = 1.0 / (LAGS * math.sqrt(SHOTS_HERE * SHOT_AXIS * LAGS))
    return to_traces(product[...], inv_high, inv_low, scale)


def correlate_kernel(upgoing, refl, fwd_high, fwd_low, inv_high, inv_low, out, rows, spectrum, product):
    out[...] = correlate_in(upgoing, refl, fwd_high, fwd_low, inv_high, inv_low, rows, spectrum, product)


def last_correlate_kernel(
    upgoing, refl, fwd_high, fwd_low, inv_high, inv_low, keep, send, rows, spectrum, product
):
    result = correlate_in(upgoing, refl, fwd_high, fwd_low, inv_high, inv_low, rows, spectrum, product)
    pieces = []
    for place in range(SHOT_AXIS):
        piece = result[:, place * SHARE_LAGS : (place + 1) * SHARE_LAGS]
        pieces.append(
            jnp.concatenate([piece[begin : begin + 8] for begin in range(0, FOCI * RCV_HERE, 8)], axis=1)
        )
    even = lax.rem(lax.axis_index("shot"), 2) == 0
    for chip in range(CHIPS):
        first, second = pieces[2 * chip : 2 * chip + 2]
        keep[chip] = jnp.where(even, first, second)
        send[chip] = jnp.where(even, second, first)


def last_pair_kernel(mine, other, own, near, middle, far, total):
    total[...] = mine[...] + other[...]
    chip = lax.axis_index("shot") // 2
    for step, out in enumerate((own, near, middle, far)):
        place = lax.bitwise_xor(chip, step)
        out[...] = total[place]


def pair_kernel(mine, other, out):
    out[...] = mine[...] + other[...]


def total_of(parts):
    total = parts[0]
    for place in range(1, parts.shape[0]):
        total = total + parts[place]
    return total


def next_kernel(
    mask, mine, far, middle, near, start, refl, fwd_high, fwd_low, inv_high, inv_low, out, spectrum, product, rows
):
    total = (mine[...] + near[...]) + (far[...] + middle[...])
    down = start[...].astype(F32) + jnp.where(mask[...] != 0, total, 0.0)
    convolve_in(down.astype(BF16), refl, fwd_high, fwd_low, inv_high, inv_low, out, spectrum, product, rows)


def last_kernel(mask, mine, near, middle, far, start, own, out, up_out):
    begin = lax.axis_index("shot") * SHARE_LAGS
    shift = lax.rem(LAGS - begin, LAGS)
    start_here = pltpu.roll(start[...].astype(F32), shift, 1)[:, :SHARE_LAGS]
    mask_here = pltpu.roll(mask[...], shift, 1)[:, :SHARE_LAGS]
    total = (mine[...] + near[...]) + (far[...] + middle[...])
    total = jnp.concatenate([total[:, lane : lane + SHARE_LAGS] for lane in range(0, LANES, SHARE_LAGS)], axis=0)
    down = start_here + jnp.where(mask_here != 0, total, 0.0)
    for q in range(FOCI):
        out[:, q, :] = down[q * RCV_HERE : (q + 1) * RCV_HERE]
    for j in range(2):
        for q in range(FOCI):
            for h in range(HALVES):
                line = j * 4 + h * 2 + q
                up_out[j, q : q + 1, h * LANES : (h + 1) * LANES] = own[line : line + 1]


VM = pl.BlockSpec(memory_space=pltpu.VMEM)
HB = pl.BlockSpec(memory_space=pltpu.HBM)
LIMIT = 24 * 1024 * 1024


def call(kernel, name, specs, outs, scratch, *args):
    many = len(outs) > 1
    shapes = [jax.ShapeDtypeStruct(*out) if isinstance(out, tuple) else out for out in outs]
    return pl.pallas_call(
        kernel,
        name=name,
        in_specs=specs,
        out_specs=[VM] * len(outs) if many else VM,
        out_shape=shapes if many else shapes[0],
        scratch_shapes=scratch,
        compiler_params=pltpu.CompilerParams(vmem_limit_bytes=LIMIT),
    )(*args)


def over_shot(array, step):
    return lax.ppermute(array, "shot", [(place, place ^ step) for place in range(SHOT_AXIS)])


def over_plane():
    places = np.arange(RCV_AXIS).reshape(4, 2, 4)
    return places.transpose(1, 0, 2).reshape(2, 16).tolist()


def on_device(reflection, focus_index, shot_window, rcv_window):
    shot_window = jnp.transpose(shot_window, (0, 2, 1))
    rcv_window = jnp.transpose(rcv_window, (0, 2, 1))
    traces = FOCI * RCV_HERE
    rows = pltpu.VMEM((FOCI * HALVES * SHOTS_HERE, LANES), F32)

    def spectra(count):
        return pltpu.VMEM((3, count, LAGS), F32)

    def products(count):
        return pltpu.VMEM((count, 2 * LAGS), F32)

    conv_scratch = [spectra(traces), products(FOCI * SHOTS_HERE), rows]
    corr_scratch = [rows, spectra(FOCI * SHOTS_HERE), products(traces)]
    conv_out = ((PLANE, SHARE, LANES), F32)
    def in_hbm(*arrays):
        return [pltpu.with_memory_space_constraint(array, pltpu.HBM) for array in arrays]

    picks = call(
        pick_kernel, "pick", [HB] * 2, [((traces, LAGS), BF16)],
        [
            pltpu.SMEM((FOCI,), jnp.int32), pltpu.VMEM((SHOTS_HERE, RCV_HERE, LAGS), BF16),
            pltpu.SemaphoreType.DMA((2,)),
        ],
        *in_hbm(focus_index, reflection),
    )
    far, middle, near = [over_shot(picks, step) for step in (6, 4, 2)]
    refl, *waves, flip = call(
        prepare_kernel, "preparation", [HB] * 6,
        [
            ((4, RCV_HERE * SHOTS_HERE, LANES), F32),
            ((LAGS, 2 * LAGS), BF16),
            ((LAGS, 2 * LAGS), BF16),
            ((2 * LAGS, LAGS), BF16),
            ((2 * LAGS, LAGS), BF16),
            ((LAGS, LAGS), BF16),
        ],
        [pltpu.VMEM((SHOTS_HERE, RCV_HERE, LAGS), BF16), pltpu.SemaphoreType.DMA((9,))],
        *in_hbm(reflection, *[jnp.asarray(table) for table in tables()]),
    )
    shot_mask, rcv_mask = call(
        mask_kernel, "masks", [HB] * 2, [((SHARE, LANES), jnp.int32), ((traces, LAGS), jnp.int32)],
        [
            pltpu.SMEM((2, FOCI, SHOTS_HERE), jnp.int32), pltpu.SMEM((2, FOCI, RCV_HERE), jnp.int32),
            pltpu.VMEM((traces, LANES), jnp.int32), pltpu.VMEM((traces, LANES), jnp.int32),
            pltpu.SemaphoreType.DMA((2,)),
        ],
        *in_hbm(shot_window, rcv_window),
    )
    picks = call(gather_kernel, "chip_picks", [VM] * 5, [((traces, LAGS), BF16)], [], picks, near, middle, far, flip)
    start, partial = call(
        first_kernel, "first_convolution", [VM] * 7, [((traces, LAGS), BF16), conv_out], conv_scratch,
        picks, over_shot(picks, 1), refl, *waves,
    )
    for iteration in range(ITERS):
        parts = lax.all_to_all(partial, "rcv", 0, 0, tiled=True, axis_index_groups=over_plane())
        mine = call(sum_kernel, "plane_sum", [VM], [((SHARE, LANES), F32)], [], parts)
        other = lax.ppermute(mine, "rcv", [(place, place ^ 4) for place in range(RCV_AXIS)])
        outs = [((PLANE, SHARE, LANES), BF16)]
        if iteration + 1 < ITERS:
            rounded = call(upgoing_kernel, "upgoing", [VM] * 3, outs, [], shot_mask, mine, other)
        else:
            rounded, own = call(
                upgoing_kernel, "last_upgoing", [VM] * 3, outs + [((8, LANES), F32)], [], shot_mask, mine, other
            )
        upgoing = lax.all_to_all(rounded, "rcv", 0, 0, tiled=True, axis_index_groups=over_plane())
        if iteration + 1 < ITERS:
            mine = call(
                correlate_kernel, "correlation", [VM] * 6, [((traces, LAGS), F32)], corr_scratch,
                upgoing, refl, *waves,
            )
            other = over_shot(mine, 1)
            mine = call(pair_kernel, "pair_sum", [VM] * 2, [((traces, LAGS), F32)], [], mine, other)
            others = [over_shot(mine, step) for step in (6, 4, 2)]
            partial = call(
                next_kernel, "next_convolution", [VM] * 11, [conv_out], conv_scratch,
                rcv_mask, mine, *others, start, refl, *waves,
            )
        else:
            keep, send = call(
                last_correlate_kernel, "last_correlation", [VM] * 6, [((CHIPS, 8, LANES), F32)] * 2,
                corr_scratch, upgoing, refl, *waves,
            )
            mine, near, middle, far = call(
                last_pair_kernel, "last_pair_sum", [VM] * 2, [((8, LANES), F32)] * CHIPS,
                [pltpu.VMEM((CHIPS, 8, LANES), F32)], keep, over_shot(send, 1),
            )
            parts = [mine] + [over_shot(part, step) for part, step in ((near, 2), (middle, 4), (far, 6))]
    focus_down, focus_up = call(
        last_kernel, "downgoing", [VM] * 7, [((RCV_HERE, FOCI, SHARE_LAGS), F32), ((2, FOCI, LAGS), F32)], [],
        rcv_mask, *parts, start, own,
    )
    return focus_down, focus_up


def solution(mesh):
    return jax.shard_map(
        on_device,
        mesh=mesh,
        in_specs=(P("shot", "rcv", None), P(), P(None, "shot", None), P(None, "rcv", None)),
        out_specs=(P("rcv", None, "shot"), P(("shot", "rcv"), None, None)),
        check_vma=False,
    )
```

```python
import functools
import math

import jax
import jax.numpy as jnp
import ml_dtypes
import numpy as np
from jax import lax
from jax.experimental import pallas as pl
from jax.experimental.pallas import tpu as pltpu
from jax.sharding import PartitionSpec as P


ITERS = 2
LAGS = 256
LANES = 128
FOCI = 2
SHOTS_HERE = 64
RCV_HERE = 16
RCV_AXIS = 32
SHOT_AXIS = 8
SHARE = SHOTS_HERE * FOCI * 2 // 16
HALVES = LAGS // LANES
PLANE = 16
HALF = SHOTS_HERE // 2
CHIPS = SHOT_AXIS // 2
SHARE_LAGS = LAGS // SHOT_AXIS
F32 = jnp.float32
BF16 = jnp.bfloat16


def split_bf16(matrix):
    high = matrix.astype(ml_dtypes.bfloat16)
    low = (matrix - high.astype(np.float64)).astype(ml_dtypes.bfloat16)
    return high, low


def tables():
    times = np.arange(LAGS)[:, None]
    angles = (np.arange(LAGS)[None, :] + 0.5) * (np.pi / LAGS) * times
    forward = np.concatenate([np.cos(angles), -np.sin(angles)], axis=1)
    fwd_high, fwd_low = split_bf16(forward)
    inv_high, inv_low = split_bf16(np.ascontiguousarray(forward.T))
    flip = np.ascontiguousarray(np.eye(LAGS)[::-1]).astype(ml_dtypes.bfloat16)
    return fwd_high, fwd_low, inv_high, inv_low, flip


def dot(left, right):
    return jnp.dot(left, right, preferred_element_type=F32)


def to_spectrum(traces, high, low):
    return dot(traces, high[...]) + dot(traces, low[...])


def to_traces(spectrum, high, low, scale):
    top = spectrum.astype(BF16)
    rest = (spectrum - top.astype(F32)).astype(BF16)
    both = dot(jnp.concatenate([top, rest], axis=0), high[...])
    count = spectrum.shape[0]
    return (both[:count] + (dot(top, low[...]) + both[count:])) * scale


def factors(spectrum):
    re, im = spectrum[:, :LAGS], spectrum[:, LAGS:]
    return re, im - re, im + re


def shot_slot(shot):
    y, z, x, j = shot // 16, (shot // 8) % 2, (shot // 2) % 4, shot % 2
    return y * 16 + x * 4 + z * 2 + j


def pick_kernel(focus_hbm, reflection_hbm, out, focus, reflection, sems):
    copies = [
        pltpu.make_async_copy(focus_hbm, focus, sems.at[0]),
        pltpu.make_async_copy(reflection_hbm, reflection, sems.at[1]),
    ]
    for copy in copies:
        copy.start()
    for copy in copies:
        copy.wait()
    first = lax.axis_index("shot") * SHOTS_HERE
    for which in range(FOCI):
        row = focus[which] - first
        inside = jnp.logical_and(row >= 0, row < SHOTS_HERE)
        trace = reflection[jnp.clip(row, 0, SHOTS_HERE - 1)].astype(F32)
        picked = jnp.where(inside, trace, 0.0).astype(BF16)
        out[which * RCV_HERE : (which + 1) * RCV_HERE, :] = picked


def spectra_of(reflection, high, low, out):
    step = 16
    for begin in range(0, HALF, step):
        spectrum = to_spectrum(reflection[begin : begin + step].reshape(step * RCV_HERE, LAGS), high, low)
        for local in range(step):
            piece = spectrum[local * RCV_HERE : (local + 1) * RCV_HERE]
            slot = shot_slot(begin + local)
            for chunk in range(4):
                out[chunk, pl.ds(slot, RCV_HERE, HALF), :] = piece[:, chunk * LANES : (chunk + 1) * LANES]


def prepare_kernel(
    reflection_hbm, high_hbm, low_hbm, inv_high_hbm, inv_low_hbm, flip_hbm,
    out, rest, high, low, inv_high, inv_low, flip, reflection, sems,
):
    def fetch(source, target, place):
        copy = pltpu.make_async_copy(source, target, sems.at[place])
        copy.start()
        return copy

    tables = [fetch(high_hbm, high, 0), fetch(low_hbm, low, 1)]
    block = fetch(reflection_hbm.at[pl.ds(0, HALF)], reflection, 2)
    later = [
        fetch(reflection_hbm.at[pl.ds(HALF, HALF)], rest, 3),
        fetch(inv_high_hbm, inv_high, 4),
        fetch(inv_low_hbm, inv_low, 5),
        fetch(flip_hbm, flip, 6),
    ]
    for copy in tables + [block]:
        copy.wait()
    spectra_of(reflection, high, low, out)
    for copy in later:
        copy.wait()


def rest_kernel(reflection, high, low, out):
    spectra_of(reflection, high, low, out)


def mask_kernel(shot_hbm, rcv_hbm, shot_mask, rcv_mask, shot_window, rcv_window, onset, ending, sems):
    copies = [
        pltpu.make_async_copy(shot_hbm, shot_window, sems.at[0]),
        pltpu.make_async_copy(rcv_hbm, rcv_window, sems.at[1]),
    ]
    for copy in copies:
        copy.start()
    for copy in copies:
        copy.wait()
    up_mask(shot_window, shot_mask)
    down_mask(rcv_window, rcv_mask, onset, ending)


def up_mask(window, out):
    me = lax.axis_index("rcv")
    corner = (me // 8) * 16 + (me % 4) * 2
    row = lax.broadcasted_iota(jnp.int32, (SHARE, LANES), 0)
    onset = jnp.zeros((SHARE, LANES), jnp.int32)
    ending = jnp.zeros((SHARE, LANES), jnp.int32)
    for z in range(2):
        for j in range(2):
            for q in range(FOCI):
                shot = corner + z * 8 + j
                mine = jnp.logical_and(row // 4 == z * 2 + j, row % 2 == q)
                onset = jnp.where(mine, window[0, q, shot], onset)
                ending = jnp.where(mine, window[1, q, shot], ending)
    time = lax.broadcasted_iota(jnp.int32, (SHARE, LANES), 1) + ((row // 2) % 2) * LANES
    out[...] = jnp.logical_and(time >= onset, time < ending).astype(jnp.int32)


def down_mask(window, out, onset, ending):
    for q in range(FOCI):
        for r in range(RCV_HERE):
            line = q * RCV_HERE + r
            onset[line : line + 1, :] = jnp.full((1, LANES), window[0, q, r], jnp.int32)
            ending[line : line + 1, :] = jnp.full((1, LANES), window[1, q, r], jnp.int32)
    time = lax.broadcasted_iota(jnp.int32, (FOCI * RCV_HERE, LANES), 1)
    for h in range(HALVES):
        inside = jnp.logical_and(time + h * LANES >= onset[...], time + h * LANES < ending[...])
        out[:, h * LANES : (h + 1) * LANES] = inside.astype(jnp.int32)


def convolve_in(field, refl, fwd_high, fwd_low, inv_high, inv_low, out, spectrum, product, rows):
    for kind, part in enumerate(factors(to_spectrum(field, fwd_high, fwd_low))):
        spectrum[kind] = part
    for chunk in range(2):
        lanes = slice(chunk * LANES, (chunk + 1) * LANES)
        im_lanes = slice(LAGS + chunk * LANES, LAGS + (chunk + 1) * LANES)
        for begin in range(0, SHOTS_HERE, HALF):
            totals = [jnp.zeros((HALF, LANES), F32) for _ in range(3 * FOCI)]
            here = refl[begin // HALF]
            for r in range(RCV_HERE):
                lines = slice(r * HALF, (r + 1) * HALF)
                re = here[chunk, lines, :]
                im = here[2 + chunk, lines, :]
                both = re + im
                for q in range(FOCI):
                    line = q * RCV_HERE + r
                    for kind, value in enumerate((both, re, im)):
                        totals[3 * q + kind] += value * spectrum[kind, line : line + 1, lanes]
            for q in range(FOCI):
                first, second, third = totals[3 * q : 3 * q + 3]
                lines = slice(q * SHOTS_HERE + begin, q * SHOTS_HERE + begin + HALF)
                product[lines, lanes] = first - third
                product[lines, im_lanes] = first + second
    scale = 1.0 / (LAGS * math.sqrt(RCV_HERE * RCV_AXIS * LAGS))
    result = to_traces(product[...], inv_high, inv_low, scale)
    for q in range(FOCI):
        for h in range(HALVES):
            rows[pl.ds(h * FOCI + q, SHOTS_HERE, 2 * FOCI), :] = result[
                q * SHOTS_HERE : (q + 1) * SHOTS_HERE, h * LANES : (h + 1) * LANES
            ]
    for place in range(PLANE):
        out[place] = rows[place * SHARE : (place + 1) * SHARE, :]


def gather_kernel(mine, near, middle, far, flip, out):
    total = (mine[...].astype(F32) + near[...].astype(F32)) + (middle[...].astype(F32) + far[...].astype(F32))
    out[...] = dot(total.astype(BF16), flip[...]).astype(BF16)


def first_kernel(
    mine, other, refl, refl_rest, fwd_high, fwd_low, inv_high, inv_low, start_out, out, spectrum, product, rows
):
    start = (mine[...].astype(F32) + other[...].astype(F32)).astype(BF16)
    start_out[...] = start
    convolve_in(start, (refl, refl_rest), fwd_high, fwd_low, inv_high, inv_low, out, spectrum, product, rows)


def sum_kernel(parts, out):
    out[...] = total_of(parts)


def upgoing_kernel(mask, mine, other, *outs):
    up = jnp.where(mask[...] != 0, mine[...] + other[...], 0.0)
    if len(outs) > 1:
        outs[1][...] = jnp.where((lax.axis_index("rcv") // 4) % 2 == 0, up[:8], up[8:])
    rounded = up.astype(BF16)
    for place in range(PLANE):
        outs[0][place] = rounded


def correlate_in(upgoing, refl, fwd_high, fwd_low, inv_high, inv_low, rows, spectrum, product):
    for place in range(PLANE):
        rows[place * SHARE : (place + 1) * SHARE, :] = upgoing[place].astype(F32)
    traces = jnp.concatenate(
        [
            jnp.concatenate(
                [rows[pl.ds(h * FOCI + q, SHOTS_HERE, 2 * FOCI), :] for h in range(HALVES)], axis=1
            )
            for q in range(FOCI)
        ],
        axis=0,
    ).astype(BF16)
    for kind, part in enumerate(factors(to_spectrum(traces, fwd_high, fwd_low))):
        spectrum[kind] = part
    for chunk in range(2):
        lanes = slice(chunk * LANES, (chunk + 1) * LANES)
        im_lanes = slice(LAGS + chunk * LANES, LAGS + (chunk + 1) * LANES)
        for r in range(RCV_HERE):
            totals = [jnp.zeros((8, LANES), F32) for _ in range(3 * FOCI)]
            for begin in range(0, SHOTS_HERE, 8):
                here = refl[begin // HALF]
                shots = slice(r * HALF + begin % HALF, r * HALF + begin % HALF + 8)
                re = here[chunk, shots, :]
                im = here[2 + chunk, shots, :]
                both = re - im
                for q in range(FOCI):
                    lines = slice(q * SHOTS_HERE + begin, q * SHOTS_HERE + begin + 8)
                    for kind, value in enumerate((both, re, im)):
                        totals[3 * q + kind] += value * spectrum[kind, lines, lanes]
            for q in range(FOCI):
                line = q * RCV_HERE + r
                first, second, third = totals[3 * q : 3 * q + 3]
                product[line : line + 1, lanes] = jnp.sum(first + third, axis=0, keepdims=True)
                product[line : line + 1, im_lanes] = jnp.sum(first + second, axis=0, keepdims=True)
    scale = 1.0 / (LAGS * math.sqrt(SHOTS_HERE * SHOT_AXIS * LAGS))
    return to_traces(product[...], inv_high, inv_low, scale)


def correlate_kernel(upgoing, refl, refl_rest, fwd_high, fwd_low, inv_high, inv_low, out, rows, spectrum, product):
    out[...] = correlate_in(upgoing, (refl, refl_rest), fwd_high, fwd_low, inv_high, inv_low, rows, spectrum, product)


def last_correlate_kernel(
    upgoing, refl, refl_rest, fwd_high, fwd_low, inv_high, inv_low, keep, send, rows, spectrum, product
):
    result = correlate_in(upgoing, (refl, refl_rest), fwd_high, fwd_low, inv_high, inv_low, rows, spectrum, product)
    pieces = []
    for place in range(SHOT_AXIS):
        piece = result[:, place * SHARE_LAGS : (place + 1) * SHARE_LAGS]
        pieces.append(
            jnp.concatenate([piece[begin : begin + 8] for begin in range(0, FOCI * RCV_HERE, 8)], axis=1)
        )
    even = lax.rem(lax.axis_index("shot"), 2) == 0
    for chip in range(CHIPS):
        first, second = pieces[2 * chip : 2 * chip + 2]
        keep[chip] = jnp.where(even, first, second)
        send[chip] = jnp.where(even, second, first)


def last_pair_kernel(mine, other, own, near, middle, far, total):
    total[...] = mine[...] + other[...]
    chip = lax.axis_index("shot") // 2
    for step, out in enumerate((own, near, middle, far)):
        place = lax.bitwise_xor(chip, step)
        out[...] = total[place]


def pair_kernel(mine, other, out):
    out[...] = mine[...] + other[...]


def total_of(parts):
    total = parts[0]
    for place in range(1, parts.shape[0]):
        total = total + parts[place]
    return total


def next_kernel(
    mask, mine, far, middle, near, start, refl, refl_rest, fwd_high, fwd_low, inv_high, inv_low,
    out, spectrum, product, rows,
):
    total = (mine[...] + near[...]) + (far[...] + middle[...])
    down = start[...].astype(F32) + jnp.where(mask[...] != 0, total, 0.0)
    convolve_in(down.astype(BF16), (refl, refl_rest), fwd_high, fwd_low, inv_high, inv_low, out, spectrum, product, rows)


def last_kernel(mask, mine, near, middle, far, start, own, out, up_out):
    begin = lax.axis_index("shot") * SHARE_LAGS
    shift = lax.rem(LAGS - begin, LAGS)
    start_here = pltpu.roll(start[...].astype(F32), shift, 1)[:, :SHARE_LAGS]
    mask_here = pltpu.roll(mask[...], shift, 1)[:, :SHARE_LAGS]
    total = (mine[...] + near[...]) + (far[...] + middle[...])
    total = jnp.concatenate([total[:, lane : lane + SHARE_LAGS] for lane in range(0, LANES, SHARE_LAGS)], axis=0)
    down = start_here + jnp.where(mask_here != 0, total, 0.0)
    for q in range(FOCI):
        out[:, q, :] = down[q * RCV_HERE : (q + 1) * RCV_HERE]
    for j in range(2):
        for q in range(FOCI):
            for h in range(HALVES):
                line = j * 4 + h * 2 + q
                up_out[j, q : q + 1, h * LANES : (h + 1) * LANES] = own[line : line + 1]


VM = pl.BlockSpec(memory_space=pltpu.VMEM)
HB = pl.BlockSpec(memory_space=pltpu.HBM)
LIMIT = 24 * 1024 * 1024


def call(kernel, name, specs, outs, scratch, *args):
    many = len(outs) > 1
    shapes = [jax.ShapeDtypeStruct(*out) if isinstance(out, tuple) else out for out in outs]
    return pl.pallas_call(
        kernel,
        name=name,
        in_specs=specs,
        out_specs=[VM] * len(outs) if many else VM,
        out_shape=shapes if many else shapes[0],
        scratch_shapes=scratch,
        compiler_params=pltpu.CompilerParams(vmem_limit_bytes=LIMIT),
    )(*args)


def over_shot(array, step):
    return lax.ppermute(array, "shot", [(place, place ^ step) for place in range(SHOT_AXIS)])


def over_plane():
    places = np.arange(RCV_AXIS).reshape(4, 2, 4)
    return places.transpose(1, 0, 2).reshape(2, 16).tolist()


def on_device(reflection, focus_index, shot_window, rcv_window):
    shot_window = jnp.transpose(shot_window, (0, 2, 1))
    rcv_window = jnp.transpose(rcv_window, (0, 2, 1))
    traces = FOCI * RCV_HERE
    rows = pltpu.VMEM((FOCI * HALVES * SHOTS_HERE, LANES), F32)

    def spectra(count):
        return pltpu.VMEM((3, count, LAGS), F32)

    def products(count):
        return pltpu.VMEM((count, 2 * LAGS), F32)

    conv_scratch = [spectra(traces), products(FOCI * SHOTS_HERE), rows]
    corr_scratch = [rows, spectra(FOCI * SHOTS_HERE), products(traces)]
    conv_out = ((PLANE, SHARE, LANES), F32)
    def in_hbm(*arrays):
        return [pltpu.with_memory_space_constraint(array, pltpu.HBM) for array in arrays]

    picks = call(
        pick_kernel, "pick", [HB] * 2, [((traces, LAGS), BF16)],
        [
            pltpu.SMEM((FOCI,), jnp.int32), pltpu.VMEM((SHOTS_HERE, RCV_HERE, LAGS), BF16),
            pltpu.SemaphoreType.DMA((2,)),
        ],
        *in_hbm(focus_index, reflection),
    )
    far, middle, near = [over_shot(picks, step) for step in (6, 4, 2)]
    spectra_half = ((4, RCV_HERE * HALF, LANES), F32)
    refl, rest, *waves, flip = call(
        prepare_kernel, "preparation", [HB] * 6,
        [
            spectra_half,
            ((HALF, RCV_HERE, LAGS), BF16),
            ((LAGS, 2 * LAGS), BF16),
            ((LAGS, 2 * LAGS), BF16),
            ((2 * LAGS, LAGS), BF16),
            ((2 * LAGS, LAGS), BF16),
            ((LAGS, LAGS), BF16),
        ],
        [pltpu.VMEM((HALF, RCV_HERE, LAGS), BF16), pltpu.SemaphoreType.DMA((7,))],
        *in_hbm(reflection, *[jnp.asarray(table) for table in tables()]),
    )
    refl_rest = call(rest_kernel, "rest_preparation", [VM] * 3, [spectra_half], [], rest, waves[0], waves[1])
    shot_mask, rcv_mask = call(
        mask_kernel, "masks", [HB] * 2, [((SHARE, LANES), jnp.int32), ((traces, LAGS), jnp.int32)],
        [
            pltpu.SMEM((2, FOCI, SHOTS_HERE), jnp.int32), pltpu.SMEM((2, FOCI, RCV_HERE), jnp.int32),
            pltpu.VMEM((traces, LANES), jnp.int32), pltpu.VMEM((traces, LANES), jnp.int32),
            pltpu.SemaphoreType.DMA((2,)),
        ],
        *in_hbm(shot_window, rcv_window),
    )
    picks = call(gather_kernel, "chip_picks", [VM] * 5, [((traces, LAGS), BF16)], [], picks, near, middle, far, flip)
    start, partial = call(
        first_kernel, "first_convolution", [VM] * 8, [((traces, LAGS), BF16), conv_out], conv_scratch,
        picks, over_shot(picks, 1), refl, refl_rest, *waves,
    )
    for iteration in range(ITERS):
        parts = lax.all_to_all(partial, "rcv", 0, 0, tiled=True, axis_index_groups=over_plane())
        mine = call(sum_kernel, "plane_sum", [VM], [((SHARE, LANES), F32)], [], parts)
        other = lax.ppermute(mine, "rcv", [(place, place ^ 4) for place in range(RCV_AXIS)])
        outs = [((PLANE, SHARE, LANES), BF16)]
        if iteration + 1 < ITERS:
            rounded = call(upgoing_kernel, "upgoing", [VM] * 3, outs, [], shot_mask, mine, other)
        else:
            rounded, own = call(
                upgoing_kernel, "last_upgoing", [VM] * 3, outs + [((8, LANES), F32)], [], shot_mask, mine, other
            )
        upgoing = lax.all_to_all(rounded, "rcv", 0, 0, tiled=True, axis_index_groups=over_plane())
        if iteration + 1 < ITERS:
            mine = call(
                correlate_kernel, "correlation", [VM] * 7, [((traces, LAGS), F32)], corr_scratch,
                upgoing, refl, refl_rest, *waves,
            )
            other = over_shot(mine, 1)
            mine = call(pair_kernel, "pair_sum", [VM] * 2, [((traces, LAGS), F32)], [], mine, other)
            others = [over_shot(mine, step) for step in (6, 4, 2)]
            partial = call(
                next_kernel, "next_convolution", [VM] * 12, [conv_out], conv_scratch,
                rcv_mask, mine, *others, start, refl, refl_rest, *waves,
            )
        else:
            keep, send = call(
                last_correlate_kernel, "last_correlation", [VM] * 7, [((CHIPS, 8, LANES), F32)] * 2,
                corr_scratch, upgoing, refl, refl_rest, *waves,
            )
            mine, near, middle, far = call(
                last_pair_kernel, "last_pair_sum", [VM] * 2, [((8, LANES), F32)] * CHIPS,
                [pltpu.VMEM((CHIPS, 8, LANES), F32)], keep, over_shot(send, 1),
            )
            parts = [mine] + [over_shot(part, step) for part, step in ((near, 2), (middle, 4), (far, 6))]
    focus_down, focus_up = call(
        last_kernel, "downgoing", [VM] * 7, [((RCV_HERE, FOCI, SHARE_LAGS), F32), ((2, FOCI, LAGS), F32)], [],
        rcv_mask, *parts, start, own,
    )
    return focus_down, focus_up


def solution(mesh):
    return jax.shard_map(
        on_device,
        mesh=mesh,
        in_specs=(P("shot", "rcv", None), P(), P(None, "shot", None), P(None, "rcv", None)),
        out_specs=(P("rcv", None, "shot"), P(("shot", "rcv"), None, None)),
        check_vma=False,
    )
```

```python
import functools
import math

import jax
import jax.numpy as jnp
import ml_dtypes
import numpy as np
from jax import lax
from jax.experimental import pallas as pl
from jax.experimental.pallas import tpu as pltpu
from jax.sharding import PartitionSpec as P


ITERS = 2
LAGS = 256
LANES = 128
FOCI = 2
SHOTS_HERE = 64
RCV_HERE = 16
RCV_AXIS = 32
SHOT_AXIS = 8
SHARE = SHOTS_HERE * FOCI * 2 // 16
HALVES = LAGS // LANES
PLANE = 16
HALF = SHOTS_HERE // 2
CHIPS = SHOT_AXIS // 2
SHARE_LAGS = LAGS // SHOT_AXIS
F32 = jnp.float32
BF16 = jnp.bfloat16


def split_bf16(matrix):
    high = matrix.astype(ml_dtypes.bfloat16)
    low = (matrix - high.astype(np.float64)).astype(ml_dtypes.bfloat16)
    return high, low


def tables():
    times = np.arange(LAGS)[:, None]
    angles = (np.arange(LAGS)[None, :] + 0.5) * (np.pi / LAGS) * times
    forward = np.concatenate([np.cos(angles), -np.sin(angles)], axis=1)
    fwd_high, fwd_low = split_bf16(forward)
    inv_high, inv_low = split_bf16(np.ascontiguousarray(forward.T))
    flip = np.ascontiguousarray(np.eye(LAGS)[::-1]).astype(ml_dtypes.bfloat16)
    return fwd_high, fwd_low, inv_high, inv_low, flip


def dot(left, right):
    return jnp.dot(left, right, preferred_element_type=F32)


def to_spectrum(traces, high, low):
    return dot(traces, high[...]) + dot(traces, low[...])


def to_traces(spectrum, high, low, scale):
    top = spectrum.astype(BF16)
    rest = (spectrum - top.astype(F32)).astype(BF16)
    both = dot(jnp.concatenate([top, rest], axis=0), high[...])
    count = spectrum.shape[0]
    return (both[:count] + (dot(top, low[...]) + both[count:])) * scale


def factors(spectrum):
    re, im = spectrum[:, :LAGS], spectrum[:, LAGS:]
    return re, im - re, im + re


def shot_slot(shot):
    y, z, x, j = shot // 16, (shot // 8) % 2, (shot // 2) % 4, shot % 2
    return y * 16 + x * 4 + z * 2 + j


def pick_kernel(focus_hbm, reflection_hbm, out, focus, reflection, sems):
    copies = [
        pltpu.make_async_copy(focus_hbm, focus, sems.at[0]),
        pltpu.make_async_copy(reflection_hbm, reflection, sems.at[1]),
    ]
    for copy in copies:
        copy.start()
    for copy in copies:
        copy.wait()
    first = lax.axis_index("shot") * SHOTS_HERE
    for which in range(FOCI):
        row = focus[which] - first
        inside = jnp.logical_and(row >= 0, row < SHOTS_HERE)
        trace = reflection[jnp.clip(row, 0, SHOTS_HERE - 1)].astype(F32)
        picked = jnp.where(inside, trace, 0.0).astype(BF16)
        out[which * RCV_HERE : (which + 1) * RCV_HERE, :] = picked


def spectra_of(reflection, high, low, out):
    step = 16
    for begin in range(0, HALF, step):
        spectrum = to_spectrum(reflection[begin : begin + step].reshape(step * RCV_HERE, LAGS), high, low)
        for local in range(step):
            piece = spectrum[local * RCV_HERE : (local + 1) * RCV_HERE]
            slot = shot_slot(begin + local)
            for chunk in range(4):
                out[chunk, pl.ds(slot, RCV_HERE, HALF), :] = piece[:, chunk * LANES : (chunk + 1) * LANES]


def prepare_kernel(
    reflection_hbm, high_hbm, low_hbm, inv_high_hbm, inv_low_hbm, flip_hbm,
    out, rest, high, low, inv_high, inv_low, flip, reflection, sems,
):
    def fetch(source, target, place):
        copy = pltpu.make_async_copy(source, target, sems.at[place])
        copy.start()
        return copy

    tables = [fetch(high_hbm, high, 0), fetch(low_hbm, low, 1)]
    block = fetch(reflection_hbm.at[pl.ds(0, HALF)], reflection, 2)
    later = [
        fetch(reflection_hbm.at[pl.ds(HALF, HALF)], rest, 3),
        fetch(inv_high_hbm, inv_high, 4),
        fetch(inv_low_hbm, inv_low, 5),
        fetch(flip_hbm, flip, 6),
    ]
    for copy in tables + [block]:
        copy.wait()
    spectra_of(reflection, high, low, out)
    for copy in later:
        copy.wait()


def rest_kernel(reflection, high, low, out):
    spectra_of(reflection, high, low, out)


def mask_kernel(shot_hbm, rcv_hbm, shot_mask, rcv_mask, shot_window, rcv_window, onset, ending, sems):
    copies = [
        pltpu.make_async_copy(shot_hbm, shot_window, sems.at[0]),
        pltpu.make_async_copy(rcv_hbm, rcv_window, sems.at[1]),
    ]
    for copy in copies:
        copy.start()
    for copy in copies:
        copy.wait()
    up_mask(shot_window, shot_mask)
    down_mask(rcv_window, rcv_mask, onset, ending)


def up_mask(window, out):
    me = lax.axis_index("rcv")
    corner = (me // 8) * 16 + (me % 4) * 2
    row = lax.broadcasted_iota(jnp.int32, (SHARE, LANES), 0)
    onset = jnp.zeros((SHARE, LANES), jnp.int32)
    ending = jnp.zeros((SHARE, LANES), jnp.int32)
    for z in range(2):
        for j in range(2):
            for q in range(FOCI):
                shot = corner + z * 8 + j
                mine = jnp.logical_and(row // 4 == z * 2 + j, row % 2 == q)
                onset = jnp.where(mine, window[0, q, shot], onset)
                ending = jnp.where(mine, window[1, q, shot], ending)
    time = lax.broadcasted_iota(jnp.int32, (SHARE, LANES), 1) + ((row // 2) % 2) * LANES
    out[...] = jnp.logical_and(time >= onset, time < ending).astype(jnp.int32)


def down_mask(window, out, onset, ending):
    for q in range(FOCI):
        for r in range(RCV_HERE):
            line = q * RCV_HERE + r
            onset[line : line + 1, :] = jnp.full((1, LANES), window[0, q, r], jnp.int32)
            ending[line : line + 1, :] = jnp.full((1, LANES), window[1, q, r], jnp.int32)
    time = lax.broadcasted_iota(jnp.int32, (FOCI * RCV_HERE, LANES), 1)
    for h in range(HALVES):
        inside = jnp.logical_and(time + h * LANES >= onset[...], time + h * LANES < ending[...])
        out[:, h * LANES : (h + 1) * LANES] = inside.astype(jnp.int32)


def convolve_in(field, refl, fwd_high, fwd_low, inv_high, inv_low, out, spectrum, product, rows):
    for kind, part in enumerate(factors(to_spectrum(field, fwd_high, fwd_low))):
        spectrum[kind] = part
    for chunk in range(2):
        lanes = slice(chunk * LANES, (chunk + 1) * LANES)
        im_lanes = slice(LAGS + chunk * LANES, LAGS + (chunk + 1) * LANES)
        for begin in range(0, SHOTS_HERE, HALF):
            totals = [jnp.zeros((HALF, LANES), F32) for _ in range(3 * FOCI)]
            here = refl[begin // HALF]
            for r in range(RCV_HERE):
                lines = slice(r * HALF, (r + 1) * HALF)
                re = here[chunk, lines, :]
                im = here[2 + chunk, lines, :]
                both = re + im
                for q in range(FOCI):
                    line = q * RCV_HERE + r
                    for kind, value in enumerate((both, re, im)):
                        totals[3 * q + kind] += value * spectrum[kind, line : line + 1, lanes]
            for q in range(FOCI):
                first, second, third = totals[3 * q : 3 * q + 3]
                lines = slice(q * SHOTS_HERE + begin, q * SHOTS_HERE + begin + HALF)
                product[lines, lanes] = first - third
                product[lines, im_lanes] = first + second
    scale = 1.0 / (LAGS * math.sqrt(RCV_HERE * RCV_AXIS * LAGS))
    result = to_traces(product[...], inv_high, inv_low, scale)
    for q in range(FOCI):
        for h in range(HALVES):
            rows[pl.ds(h * FOCI + q, SHOTS_HERE, 2 * FOCI), :] = result[
                q * SHOTS_HERE : (q + 1) * SHOTS_HERE, h * LANES : (h + 1) * LANES
            ]
    for place in range(PLANE):
        out[place] = rows[place * SHARE : (place + 1) * SHARE, :]


def gather_kernel(mine, near, middle, far, flip, out):
    total = (mine[...].astype(F32) + near[...].astype(F32)) + (middle[...].astype(F32) + far[...].astype(F32))
    out[...] = dot(total.astype(BF16), flip[...]).astype(BF16)


def first_kernel(
    mine, other, refl, refl_rest, fwd_high, fwd_low, inv_high, inv_low, start_out, out, spectrum, product, rows
):
    start = (mine[...].astype(F32) + other[...].astype(F32)).astype(BF16)
    start_out[...] = start
    convolve_in(start, (refl, refl_rest), fwd_high, fwd_low, inv_high, inv_low, out, spectrum, product, rows)


def sum_kernel(parts, out):
    out[...] = total_of(parts)


def upgoing_kernel(mask, mine, other, *outs):
    up = jnp.where(mask[...] != 0, mine[...] + other[...], 0.0)
    if len(outs) > 1:
        outs[1][...] = jnp.where((lax.axis_index("rcv") // 4) % 2 == 0, up[:8], up[8:])
    rounded = up.astype(BF16)
    for place in range(PLANE):
        outs[0][place] = rounded


def correlate_in(upgoing, refl, fwd_high, fwd_low, inv_high, inv_low, rows, spectrum, product):
    for place in range(PLANE):
        rows[place * SHARE : (place + 1) * SHARE, :] = upgoing[place].astype(F32)
    traces = jnp.concatenate(
        [
            jnp.concatenate(
                [rows[pl.ds(h * FOCI + q, SHOTS_HERE, 2 * FOCI), :] for h in range(HALVES)], axis=1
            )
            for q in range(FOCI)
        ],
        axis=0,
    ).astype(BF16)
    for kind, part in enumerate(factors(to_spectrum(traces, fwd_high, fwd_low))):
        spectrum[kind] = part
    for chunk in range(2):
        lanes = slice(chunk * LANES, (chunk + 1) * LANES)
        im_lanes = slice(LAGS + chunk * LANES, LAGS + (chunk + 1) * LANES)
        for r in range(RCV_HERE):
            totals = [jnp.zeros((8, LANES), F32) for _ in range(3 * FOCI)]
            for begin in range(0, SHOTS_HERE, 8):
                here = refl[begin // HALF]
                shots = slice(r * HALF + begin % HALF, r * HALF + begin % HALF + 8)
                re = here[chunk, shots, :]
                im = here[2 + chunk, shots, :]
                both = re - im
                for q in range(FOCI):
                    lines = slice(q * SHOTS_HERE + begin, q * SHOTS_HERE + begin + 8)
                    for kind, value in enumerate((both, re, im)):
                        totals[3 * q + kind] += value * spectrum[kind, lines, lanes]
            for q in range(FOCI):
                line = q * RCV_HERE + r
                first, second, third = totals[3 * q : 3 * q + 3]
                product[line : line + 1, lanes] = jnp.sum(first + third, axis=0, keepdims=True)
                product[line : line + 1, im_lanes] = jnp.sum(first + second, axis=0, keepdims=True)
    scale = 1.0 / (LAGS * math.sqrt(SHOTS_HERE * SHOT_AXIS * LAGS))
    return to_traces(product[...], inv_high, inv_low, scale)


def correlate_kernel(upgoing, refl, refl_rest, fwd_high, fwd_low, inv_high, inv_low, out, rows, spectrum, product):
    out[...] = correlate_in(upgoing, (refl, refl_rest), fwd_high, fwd_low, inv_high, inv_low, rows, spectrum, product)


def last_correlate_kernel(
    upgoing, refl, refl_rest, fwd_high, fwd_low, inv_high, inv_low, keep, send, rows, spectrum, product
):
    result = correlate_in(upgoing, (refl, refl_rest), fwd_high, fwd_low, inv_high, inv_low, rows, spectrum, product)
    pieces = []
    for place in range(SHOT_AXIS):
        piece = result[:, place * SHARE_LAGS : (place + 1) * SHARE_LAGS]
        pieces.append(
            jnp.concatenate([piece[begin : begin + 8] for begin in range(0, FOCI * RCV_HERE, 8)], axis=1)
        )
    even = lax.rem(lax.axis_index("shot"), 2) == 0
    for chip in range(CHIPS):
        first, second = pieces[2 * chip : 2 * chip + 2]
        keep[chip] = jnp.where(even, first, second)
        send[chip] = jnp.where(even, second, first)


def last_pair_kernel(mine, other, own, near, middle, far, total):
    total[...] = mine[...] + other[...]
    chip = lax.axis_index("shot") // 2
    for step, out in enumerate((own, near, middle, far)):
        place = lax.bitwise_xor(chip, step)
        out[...] = total[place]


def pair_kernel(mine, other, out):
    out[...] = mine[...] + other[...]


def total_of(parts):
    total = parts[0]
    for place in range(1, parts.shape[0]):
        total = total + parts[place]
    return total


def next_kernel(
    mask, mine, near, middle, far, start, refl, refl_rest, fwd_high, fwd_low, inv_high, inv_low,
    out, spectrum, product, rows,
):
    total = (mine[...] + near[...]) + (far[...] + middle[...])
    down = start[...].astype(F32) + jnp.where(mask[...] != 0, total, 0.0)
    convolve_in(down.astype(BF16), (refl, refl_rest), fwd_high, fwd_low, inv_high, inv_low, out, spectrum, product, rows)


def last_kernel(mask, mine, far, middle, near, start, own, out, up_out):
    begin = lax.axis_index("shot") * SHARE_LAGS
    shift = lax.rem(LAGS - begin, LAGS)
    start_here = pltpu.roll(start[...].astype(F32), shift, 1)[:, :SHARE_LAGS]
    mask_here = pltpu.roll(mask[...], shift, 1)[:, :SHARE_LAGS]
    total = (mine[...] + near[...]) + (far[...] + middle[...])
    total = jnp.concatenate([total[:, lane : lane + SHARE_LAGS] for lane in range(0, LANES, SHARE_LAGS)], axis=0)
    down = start_here + jnp.where(mask_here != 0, total, 0.0)
    for q in range(FOCI):
        out[:, q, :] = down[q * RCV_HERE : (q + 1) * RCV_HERE]
    for j in range(2):
        for q in range(FOCI):
            for h in range(HALVES):
                line = j * 4 + h * 2 + q
                up_out[j, q : q + 1, h * LANES : (h + 1) * LANES] = own[line : line + 1]


VM = pl.BlockSpec(memory_space=pltpu.VMEM)
HB = pl.BlockSpec(memory_space=pltpu.HBM)
LIMIT = 24 * 1024 * 1024


def call(kernel, name, specs, outs, scratch, *args):
    many = len(outs) > 1
    shapes = [jax.ShapeDtypeStruct(*out) if isinstance(out, tuple) else out for out in outs]
    return pl.pallas_call(
        kernel,
        name=name,
        in_specs=specs,
        out_specs=[VM] * len(outs) if many else VM,
        out_shape=shapes if many else shapes[0],
        scratch_shapes=scratch,
        compiler_params=pltpu.CompilerParams(vmem_limit_bytes=LIMIT),
    )(*args)


def over_shot(array, step):
    return lax.ppermute(array, "shot", [(place, place ^ step) for place in range(SHOT_AXIS)])


def over_plane():
    places = np.arange(RCV_AXIS).reshape(4, 2, 4)
    return places.transpose(1, 0, 2).reshape(2, 16).tolist()


def on_device(reflection, focus_index, shot_window, rcv_window):
    shot_window = jnp.transpose(shot_window, (0, 2, 1))
    rcv_window = jnp.transpose(rcv_window, (0, 2, 1))
    traces = FOCI * RCV_HERE
    rows = pltpu.VMEM((FOCI * HALVES * SHOTS_HERE, LANES), F32)

    def spectra(count):
        return pltpu.VMEM((3, count, LAGS), F32)

    def products(count):
        return pltpu.VMEM((count, 2 * LAGS), F32)

    conv_scratch = [spectra(traces), products(FOCI * SHOTS_HERE), rows]
    corr_scratch = [rows, spectra(FOCI * SHOTS_HERE), products(traces)]
    conv_out = ((PLANE, SHARE, LANES), F32)
    def in_hbm(*arrays):
        return [pltpu.with_memory_space_constraint(array, pltpu.HBM) for array in arrays]

    picks = call(
        pick_kernel, "pick", [HB] * 2, [((traces, LAGS), BF16)],
        [
            pltpu.SMEM((FOCI,), jnp.int32), pltpu.VMEM((SHOTS_HERE, RCV_HERE, LAGS), BF16),
            pltpu.SemaphoreType.DMA((2,)),
        ],
        *in_hbm(focus_index, reflection),
    )
    far, middle, near = [over_shot(picks, step) for step in (6, 4, 2)]
    spectra_half = ((4, RCV_HERE * HALF, LANES), F32)
    refl, rest, *waves, flip = call(
        prepare_kernel, "preparation", [HB] * 6,
        [
            spectra_half,
            ((HALF, RCV_HERE, LAGS), BF16),
            ((LAGS, 2 * LAGS), BF16),
            ((LAGS, 2 * LAGS), BF16),
            ((2 * LAGS, LAGS), BF16),
            ((2 * LAGS, LAGS), BF16),
            ((LAGS, LAGS), BF16),
        ],
        [pltpu.VMEM((HALF, RCV_HERE, LAGS), BF16), pltpu.SemaphoreType.DMA((7,))],
        *in_hbm(reflection, *[jnp.asarray(table) for table in tables()]),
    )
    refl_rest = call(rest_kernel, "rest_preparation", [VM] * 3, [spectra_half], [], rest, waves[0], waves[1])
    shot_mask, rcv_mask = call(
        mask_kernel, "masks", [HB] * 2, [((SHARE, LANES), jnp.int32), ((traces, LAGS), jnp.int32)],
        [
            pltpu.SMEM((2, FOCI, SHOTS_HERE), jnp.int32), pltpu.SMEM((2, FOCI, RCV_HERE), jnp.int32),
            pltpu.VMEM((traces, LANES), jnp.int32), pltpu.VMEM((traces, LANES), jnp.int32),
            pltpu.SemaphoreType.DMA((2,)),
        ],
        *in_hbm(shot_window, rcv_window),
    )
    picks = call(gather_kernel, "chip_picks", [VM] * 5, [((traces, LAGS), BF16)], [], picks, near, middle, far, flip)
    start, partial = call(
        first_kernel, "first_convolution", [VM] * 8, [((traces, LAGS), BF16), conv_out], conv_scratch,
        picks, over_shot(picks, 1), refl, refl_rest, *waves,
    )
    for iteration in range(ITERS):
        parts = lax.all_to_all(partial, "rcv", 0, 0, tiled=True, axis_index_groups=over_plane())
        mine = call(sum_kernel, "plane_sum", [VM], [((SHARE, LANES), F32)], [], parts)
        other = lax.ppermute(mine, "rcv", [(place, place ^ 4) for place in range(RCV_AXIS)])
        outs = [((PLANE, SHARE, LANES), BF16)]
        if iteration + 1 < ITERS:
            rounded = call(upgoing_kernel, "upgoing", [VM] * 3, outs, [], shot_mask, mine, other)
        else:
            rounded, own = call(
                upgoing_kernel, "last_upgoing", [VM] * 3, outs + [((8, LANES), F32)], [], shot_mask, mine, other
            )
        upgoing = lax.all_to_all(rounded, "rcv", 0, 0, tiled=True, axis_index_groups=over_plane())
        if iteration + 1 < ITERS:
            mine = call(
                correlate_kernel, "correlation", [VM] * 7, [((traces, LAGS), F32)], corr_scratch,
                upgoing, refl, refl_rest, *waves,
            )
            other = over_shot(mine, 1)
            mine = call(pair_kernel, "pair_sum", [VM] * 2, [((traces, LAGS), F32)], [], mine, other)
            others = [over_shot(mine, step) for step in (6, 4, 2)][::-1]
            partial = call(
                next_kernel, "next_convolution", [VM] * 12, [conv_out], conv_scratch,
                rcv_mask, mine, *others, start, refl, refl_rest, *waves,
            )
        else:
            keep, send = call(
                last_correlate_kernel, "last_correlation", [VM] * 7, [((CHIPS, 8, LANES), F32)] * 2,
                corr_scratch, upgoing, refl, refl_rest, *waves,
            )
            mine, near, middle, far = call(
                last_pair_kernel, "last_pair_sum", [VM] * 2, [((8, LANES), F32)] * CHIPS,
                [pltpu.VMEM((CHIPS, 8, LANES), F32)], keep, over_shot(send, 1),
            )
            parts = [mine] + [over_shot(part, step) for part, step in ((far, 6), (middle, 4), (near, 2))]
    focus_down, focus_up = call(
        last_kernel, "downgoing", [VM] * 7, [((RCV_HERE, FOCI, SHARE_LAGS), F32), ((2, FOCI, LAGS), F32)], [],
        rcv_mask, *parts, start, own,
    )
    return focus_down, focus_up


def solution(mesh):
    return jax.shard_map(
        on_device,
        mesh=mesh,
        in_specs=(P("shot", "rcv", None), P(), P(None, "shot", None), P(None, "rcv", None)),
        out_specs=(P("rcv", None, "shot"), P(("shot", "rcv"), None, None)),
        check_vma=False,
    )
```

```python
import functools
import math

import jax
import jax.numpy as jnp
import ml_dtypes
import numpy as np
from jax import lax
from jax.experimental import pallas as pl
from jax.experimental.pallas import tpu as pltpu
from jax.sharding import PartitionSpec as P


ITERS = 2
LAGS = 256
LANES = 128
FOCI = 2
SHOTS_HERE = 64
RCV_HERE = 16
RCV_AXIS = 32
SHOT_AXIS = 8
SHARE = SHOTS_HERE * FOCI * 2 // 16
HALVES = LAGS // LANES
PLANE = 16
HALF = SHOTS_HERE // 2
CHIPS = SHOT_AXIS // 2
SHARE_LAGS = LAGS // SHOT_AXIS
F32 = jnp.float32
BF16 = jnp.bfloat16


def split_bf16(matrix):
    high = matrix.astype(ml_dtypes.bfloat16)
    low = (matrix - high.astype(np.float64)).astype(ml_dtypes.bfloat16)
    return high, low


def tables():
    times = np.arange(LAGS)[:, None]
    angles = (np.arange(LAGS)[None, :] + 0.5) * (np.pi / LAGS) * times
    forward = np.concatenate([np.cos(angles), -np.sin(angles)], axis=1)
    fwd_high, fwd_low = split_bf16(forward)
    inv_high, inv_low = split_bf16(np.ascontiguousarray(forward.T))
    flip = np.ascontiguousarray(np.eye(LAGS)[::-1]).astype(ml_dtypes.bfloat16)
    return fwd_high, fwd_low, inv_high, inv_low, flip


def dot(left, right):
    return jnp.dot(left, right, preferred_element_type=F32)


def to_spectrum(traces, high, low):
    return dot(traces, high[...]) + dot(traces, low[...])


def to_traces(spectrum, high, low, scale):
    top = spectrum.astype(BF16)
    rest = (spectrum - top.astype(F32)).astype(BF16)
    both = dot(jnp.concatenate([top, rest], axis=0), high[...])
    count = spectrum.shape[0]
    return (both[:count] + (dot(top, low[...]) + both[count:])) * scale


def factors(spectrum):
    re, im = spectrum[:, :LAGS], spectrum[:, LAGS:]
    return re, im - re, im + re


def shot_slot(shot):
    y, z, x, j = shot // 16, (shot // 8) % 2, (shot // 2) % 4, shot % 2
    return y * 16 + x * 4 + z * 2 + j


def pick_kernel(focus_hbm, reflection_hbm, out, focus, reflection, sems):
    copies = [
        pltpu.make_async_copy(focus_hbm, focus, sems.at[0]),
        pltpu.make_async_copy(reflection_hbm, reflection, sems.at[1]),
    ]
    for copy in copies:
        copy.start()
    for copy in copies:
        copy.wait()
    first = lax.axis_index("shot") * SHOTS_HERE
    for which in range(FOCI):
        row = focus[which] - first
        inside = jnp.logical_and(row >= 0, row < SHOTS_HERE)
        trace = reflection[jnp.clip(row, 0, SHOTS_HERE - 1)].astype(F32)
        picked = jnp.where(inside, trace, 0.0).astype(BF16)
        out[which * RCV_HERE : (which + 1) * RCV_HERE, :] = picked


def spectra_of(reflection, high, low, out):
    step = 16
    for begin in range(0, HALF, step):
        spectrum = to_spectrum(reflection[begin : begin + step].reshape(step * RCV_HERE, LAGS), high, low)
        for local in range(step):
            piece = spectrum[local * RCV_HERE : (local + 1) * RCV_HERE]
            slot = shot_slot(begin + local)
            for chunk in range(4):
                out[chunk, pl.ds(slot, RCV_HERE, HALF), :] = piece[:, chunk * LANES : (chunk + 1) * LANES]


def prepare_kernel(
    reflection_hbm, high_hbm, low_hbm, inv_high_hbm, inv_low_hbm, flip_hbm,
    out, rest, high, low, inv_high, inv_low, flip, reflection, sems,
):
    def fetch(source, target, place):
        copy = pltpu.make_async_copy(source, target, sems.at[place])
        copy.start()
        return copy

    tables = [fetch(high_hbm, high, 0), fetch(low_hbm, low, 1)]
    block = fetch(reflection_hbm.at[pl.ds(0, HALF)], reflection, 2)
    later = [
        fetch(reflection_hbm.at[pl.ds(HALF, HALF)], rest, 3),
        fetch(inv_high_hbm, inv_high, 4),
        fetch(inv_low_hbm, inv_low, 5),
        fetch(flip_hbm, flip, 6),
    ]
    for copy in tables + [block]:
        copy.wait()
    spectra_of(reflection, high, low, out)
    for copy in later:
        copy.wait()


def rest_kernel(reflection, high, low, out):
    spectra_of(reflection, high, low, out)


def mask_kernel(shot_hbm, rcv_hbm, shot_mask, rcv_mask, shot_window, rcv_window, onset, ending, sems):
    copies = [
        pltpu.make_async_copy(shot_hbm, shot_window, sems.at[0]),
        pltpu.make_async_copy(rcv_hbm, rcv_window, sems.at[1]),
    ]
    for copy in copies:
        copy.start()
    for copy in copies:
        copy.wait()
    up_mask(shot_window, shot_mask)
    down_mask(rcv_window, rcv_mask, onset, ending)


def up_mask(window, out):
    me = lax.axis_index("rcv")
    corner = (me // 8) * 16 + (me % 4) * 2
    row = lax.broadcasted_iota(jnp.int32, (SHARE, LANES), 0)
    onset = jnp.zeros((SHARE, LANES), jnp.int32)
    ending = jnp.zeros((SHARE, LANES), jnp.int32)
    for z in range(2):
        for j in range(2):
            for q in range(FOCI):
                shot = corner + z * 8 + j
                mine = jnp.logical_and(row // 4 == z * 2 + j, row % 2 == q)
                onset = jnp.where(mine, window[0, q, shot], onset)
                ending = jnp.where(mine, window[1, q, shot], ending)
    time = lax.broadcasted_iota(jnp.int32, (SHARE, LANES), 1) + ((row // 2) % 2) * LANES
    out[...] = jnp.logical_and(time >= onset, time < ending).astype(jnp.int32)


def down_mask(window, out, onset, ending):
    for q in range(FOCI):
        for r in range(RCV_HERE):
            line = q * RCV_HERE + r
            onset[line : line + 1, :] = jnp.full((1, LANES), window[0, q, r], jnp.int32)
            ending[line : line + 1, :] = jnp.full((1, LANES), window[1, q, r], jnp.int32)
    time = lax.broadcasted_iota(jnp.int32, (FOCI * RCV_HERE, LANES), 1)
    for h in range(HALVES):
        inside = jnp.logical_and(time + h * LANES >= onset[...], time + h * LANES < ending[...])
        out[:, h * LANES : (h + 1) * LANES] = inside.astype(jnp.int32)


def convolve_in(field, refl, fwd_high, fwd_low, inv_high, inv_low, out, spectrum, product, rows):
    for kind, part in enumerate(factors(to_spectrum(field, fwd_high, fwd_low))):
        spectrum[kind] = part
    for chunk in range(2):
        lanes = slice(chunk * LANES, (chunk + 1) * LANES)
        im_lanes = slice(LAGS + chunk * LANES, LAGS + (chunk + 1) * LANES)
        for begin in range(0, SHOTS_HERE, HALF):
            totals = [jnp.zeros((HALF, LANES), F32) for _ in range(3 * FOCI)]
            here = refl[begin // HALF]
            for r in range(RCV_HERE):
                lines = slice(r * HALF, (r + 1) * HALF)
                re = here[chunk, lines, :]
                im = here[2 + chunk, lines, :]
                both = re + im
                for q in range(FOCI):
                    line = q * RCV_HERE + r
                    for kind, value in enumerate((both, re, im)):
                        totals[3 * q + kind] += value * spectrum[kind, line : line + 1, lanes]
            for q in range(FOCI):
                first, second, third = totals[3 * q : 3 * q + 3]
                lines = slice(q * SHOTS_HERE + begin, q * SHOTS_HERE + begin + HALF)
                product[lines, lanes] = first - third
                product[lines, im_lanes] = first + second
    scale = 1.0 / (LAGS * math.sqrt(RCV_HERE * RCV_AXIS * LAGS))
    result = to_traces(product[...], inv_high, inv_low, scale)
    for q in range(FOCI):
        for h in range(HALVES):
            rows[pl.ds(h * FOCI + q, SHOTS_HERE, 2 * FOCI), :] = result[
                q * SHOTS_HERE : (q + 1) * SHOTS_HERE, h * LANES : (h + 1) * LANES
            ]
    for place in range(PLANE):
        out[place] = rows[place * SHARE : (place + 1) * SHARE, :]


def gather_kernel(mine, near, middle, far, flip, out):
    total = (mine[...].astype(F32) + near[...].astype(F32)) + (middle[...].astype(F32) + far[...].astype(F32))
    out[...] = dot(total.astype(BF16), flip[...]).astype(BF16)


def first_kernel(
    mine, other, refl, refl_rest, fwd_high, fwd_low, inv_high, inv_low, start_out, out, spectrum, product, rows
):
    start = (mine[...].astype(F32) + other[...].astype(F32)).astype(BF16)
    start_out[...] = start
    convolve_in(start, (refl, refl_rest), fwd_high, fwd_low, inv_high, inv_low, out, spectrum, product, rows)


def sum_kernel(parts, out):
    out[...] = total_of(parts)


def upgoing_kernel(mask, mine, other, *outs):
    up = jnp.where(mask[...] != 0, mine[...] + other[...], 0.0)
    if len(outs) > 1:
        outs[1][...] = jnp.where((lax.axis_index("rcv") // 4) % 2 == 0, up[:8], up[8:])
    rounded = up.astype(BF16)
    for place in range(PLANE):
        outs[0][place] = rounded


def correlate_in(upgoing, refl, fwd_high, fwd_low, inv_high, inv_low, rows, spectrum, product):
    for place in range(PLANE):
        rows[place * SHARE : (place + 1) * SHARE, :] = upgoing[place].astype(F32)
    traces = jnp.concatenate(
        [
            jnp.concatenate(
                [rows[pl.ds(h * FOCI + q, SHOTS_HERE, 2 * FOCI), :] for h in range(HALVES)], axis=1
            )
            for q in range(FOCI)
        ],
        axis=0,
    ).astype(BF16)
    for kind, part in enumerate(factors(to_spectrum(traces, fwd_high, fwd_low))):
        spectrum[kind] = part
    for chunk in range(2):
        lanes = slice(chunk * LANES, (chunk + 1) * LANES)
        im_lanes = slice(LAGS + chunk * LANES, LAGS + (chunk + 1) * LANES)
        for r in range(RCV_HERE):
            totals = [jnp.zeros((8, LANES), F32) for _ in range(3 * FOCI)]
            for begin in range(0, SHOTS_HERE, 8):
                here = refl[begin // HALF]
                shots = slice(r * HALF + begin % HALF, r * HALF + begin % HALF + 8)
                re = here[chunk, shots, :]
                im = here[2 + chunk, shots, :]
                both = re - im
                for q in range(FOCI):
                    lines = slice(q * SHOTS_HERE + begin, q * SHOTS_HERE + begin + 8)
                    for kind, value in enumerate((both, re, im)):
                        totals[3 * q + kind] += value * spectrum[kind, lines, lanes]
            for q in range(FOCI):
                line = q * RCV_HERE + r
                first, second, third = totals[3 * q : 3 * q + 3]
                product[line : line + 1, lanes] = jnp.sum(first + third, axis=0, keepdims=True)
                product[line : line + 1, im_lanes] = jnp.sum(first + second, axis=0, keepdims=True)
    scale = 1.0 / (LAGS * math.sqrt(SHOTS_HERE * SHOT_AXIS * LAGS))
    return to_traces(product[...], inv_high, inv_low, scale)


def correlate_kernel(upgoing, refl, refl_rest, fwd_high, fwd_low, inv_high, inv_low, out, rows, spectrum, product):
    out[...] = correlate_in(upgoing, (refl, refl_rest), fwd_high, fwd_low, inv_high, inv_low, rows, spectrum, product)


def last_correlate_kernel(
    upgoing, refl, refl_rest, fwd_high, fwd_low, inv_high, inv_low, keep, send, rows, spectrum, product
):
    result = correlate_in(upgoing, (refl, refl_rest), fwd_high, fwd_low, inv_high, inv_low, rows, spectrum, product)
    pieces = []
    for place in range(SHOT_AXIS):
        piece = result[:, place * SHARE_LAGS : (place + 1) * SHARE_LAGS]
        pieces.append(
            jnp.concatenate([piece[begin : begin + 8] for begin in range(0, FOCI * RCV_HERE, 8)], axis=1)
        )
    even = lax.rem(lax.axis_index("shot"), 2) == 0
    for chip in range(CHIPS):
        first, second = pieces[2 * chip : 2 * chip + 2]
        keep[chip] = jnp.where(even, first, second)
        send[chip] = jnp.where(even, second, first)


def last_pair_kernel(mine, other, own, near, middle, far, total):
    total[...] = mine[...] + other[...]
    chip = lax.axis_index("shot") // 2
    for step, out in enumerate((own, near, middle, far)):
        place = lax.bitwise_xor(chip, step)
        out[...] = total[place]


def chips_kernel(mine, near, middle, far, out):
    out[...] = (mine[...] + near[...]) + (far[...] + middle[...])


def total_of(parts):
    total = parts[0]
    for place in range(1, parts.shape[0]):
        total = total + parts[place]
    return total


def next_kernel(
    mask, mine, other, start, refl, refl_rest, fwd_high, fwd_low, inv_high, inv_low,
    out, spectrum, product, rows,
):
    down = start[...].astype(F32) + jnp.where(mask[...] != 0, mine[...] + other[...], 0.0)
    convolve_in(down.astype(BF16), (refl, refl_rest), fwd_high, fwd_low, inv_high, inv_low, out, spectrum, product, rows)


def last_kernel(mask, mine, far, middle, near, start, own, out, up_out):
    begin = lax.axis_index("shot") * SHARE_LAGS
    shift = lax.rem(LAGS - begin, LAGS)
    start_here = pltpu.roll(start[...].astype(F32), shift, 1)[:, :SHARE_LAGS]
    mask_here = pltpu.roll(mask[...], shift, 1)[:, :SHARE_LAGS]
    total = (mine[...] + near[...]) + (far[...] + middle[...])
    total = jnp.concatenate([total[:, lane : lane + SHARE_LAGS] for lane in range(0, LANES, SHARE_LAGS)], axis=0)
    down = start_here + jnp.where(mask_here != 0, total, 0.0)
    for q in range(FOCI):
        out[:, q, :] = down[q * RCV_HERE : (q + 1) * RCV_HERE]
    for j in range(2):
        for q in range(FOCI):
            for h in range(HALVES):
                line = j * 4 + h * 2 + q
                up_out[j, q : q + 1, h * LANES : (h + 1) * LANES] = own[line : line + 1]


VM = pl.BlockSpec(memory_space=pltpu.VMEM)
HB = pl.BlockSpec(memory_space=pltpu.HBM)
LIMIT = 24 * 1024 * 1024


def call(kernel, name, specs, outs, scratch, *args):
    many = len(outs) > 1
    shapes = [jax.ShapeDtypeStruct(*out) if isinstance(out, tuple) else out for out in outs]
    return pl.pallas_call(
        kernel,
        name=name,
        in_specs=specs,
        out_specs=[VM] * len(outs) if many else VM,
        out_shape=shapes if many else shapes[0],
        scratch_shapes=scratch,
        compiler_params=pltpu.CompilerParams(vmem_limit_bytes=LIMIT),
    )(*args)


def over_shot(array, step):
    return lax.ppermute(array, "shot", [(place, place ^ step) for place in range(SHOT_AXIS)])


def over_plane():
    places = np.arange(RCV_AXIS).reshape(4, 2, 4)
    return places.transpose(1, 0, 2).reshape(2, 16).tolist()


def on_device(reflection, focus_index, shot_window, rcv_window):
    shot_window = jnp.transpose(shot_window, (0, 2, 1))
    rcv_window = jnp.transpose(rcv_window, (0, 2, 1))
    traces = FOCI * RCV_HERE
    rows = pltpu.VMEM((FOCI * HALVES * SHOTS_HERE, LANES), F32)

    def spectra(count):
        return pltpu.VMEM((3, count, LAGS), F32)

    def products(count):
        return pltpu.VMEM((count, 2 * LAGS), F32)

    conv_scratch = [spectra(traces), products(FOCI * SHOTS_HERE), rows]
    corr_scratch = [rows, spectra(FOCI * SHOTS_HERE), products(traces)]
    conv_out = ((PLANE, SHARE, LANES), F32)
    def in_hbm(*arrays):
        return [pltpu.with_memory_space_constraint(array, pltpu.HBM) for array in arrays]

    picks = call(
        pick_kernel, "pick", [HB] * 2, [((traces, LAGS), BF16)],
        [
            pltpu.SMEM((FOCI,), jnp.int32), pltpu.VMEM((SHOTS_HERE, RCV_HERE, LAGS), BF16),
            pltpu.SemaphoreType.DMA((2,)),
        ],
        *in_hbm(focus_index, reflection),
    )
    far, middle, near = [over_shot(picks, step) for step in (6, 4, 2)]
    spectra_half = ((4, RCV_HERE * HALF, LANES), F32)
    refl, rest, *waves, flip = call(
        prepare_kernel, "preparation", [HB] * 6,
        [
            spectra_half,
            ((HALF, RCV_HERE, LAGS), BF16),
            ((LAGS, 2 * LAGS), BF16),
            ((LAGS, 2 * LAGS), BF16),
            ((2 * LAGS, LAGS), BF16),
            ((2 * LAGS, LAGS), BF16),
            ((LAGS, LAGS), BF16),
        ],
        [pltpu.VMEM((HALF, RCV_HERE, LAGS), BF16), pltpu.SemaphoreType.DMA((7,))],
        *in_hbm(reflection, *[jnp.asarray(table) for table in tables()]),
    )
    refl_rest = call(rest_kernel, "rest_preparation", [VM] * 3, [spectra_half], [], rest, waves[0], waves[1])
    shot_mask, rcv_mask = call(
        mask_kernel, "masks", [HB] * 2, [((SHARE, LANES), jnp.int32), ((traces, LAGS), jnp.int32)],
        [
            pltpu.SMEM((2, FOCI, SHOTS_HERE), jnp.int32), pltpu.SMEM((2, FOCI, RCV_HERE), jnp.int32),
            pltpu.VMEM((traces, LANES), jnp.int32), pltpu.VMEM((traces, LANES), jnp.int32),
            pltpu.SemaphoreType.DMA((2,)),
        ],
        *in_hbm(shot_window, rcv_window),
    )
    picks = call(gather_kernel, "chip_picks", [VM] * 5, [((traces, LAGS), BF16)], [], picks, near, middle, far, flip)
    start, partial = call(
        first_kernel, "first_convolution", [VM] * 8, [((traces, LAGS), BF16), conv_out], conv_scratch,
        picks, over_shot(picks, 1), refl, refl_rest, *waves,
    )
    for iteration in range(ITERS):
        parts = lax.all_to_all(partial, "rcv", 0, 0, tiled=True, axis_index_groups=over_plane())
        mine = call(sum_kernel, "plane_sum", [VM], [((SHARE, LANES), F32)], [], parts)
        other = lax.ppermute(mine, "rcv", [(place, place ^ 4) for place in range(RCV_AXIS)])
        outs = [((PLANE, SHARE, LANES), BF16)]
        if iteration + 1 < ITERS:
            rounded = call(upgoing_kernel, "upgoing", [VM] * 3, outs, [], shot_mask, mine, other)
        else:
            rounded, own = call(
                upgoing_kernel, "last_upgoing", [VM] * 3, outs + [((8, LANES), F32)], [], shot_mask, mine, other
            )
        upgoing = lax.all_to_all(rounded, "rcv", 0, 0, tiled=True, axis_index_groups=over_plane())
        if iteration + 1 < ITERS:
            mine = call(
                correlate_kernel, "correlation", [VM] * 7, [((traces, LAGS), F32)], corr_scratch,
                upgoing, refl, refl_rest, *waves,
            )
            others = [over_shot(mine, step) for step in (6, 4, 2)][::-1]
            mine = call(chips_kernel, "chip_sum", [VM] * 4, [((traces, LAGS), F32)], [], mine, *others)
            partial = call(
                next_kernel, "next_convolution", [VM] * 10, [conv_out], conv_scratch,
                rcv_mask, mine, over_shot(mine, 1), start, refl, refl_rest, *waves,
            )
        else:
            keep, send = call(
                last_correlate_kernel, "last_correlation", [VM] * 7, [((CHIPS, 8, LANES), F32)] * 2,
                corr_scratch, upgoing, refl, refl_rest, *waves,
            )
            mine, near, middle, far = call(
                last_pair_kernel, "last_pair_sum", [VM] * 2, [((8, LANES), F32)] * CHIPS,
                [pltpu.VMEM((CHIPS, 8, LANES), F32)], keep, over_shot(send, 1),
            )
            parts = [mine] + [over_shot(part, step) for part, step in ((far, 6), (middle, 4), (near, 2))]
    focus_down, focus_up = call(
        last_kernel, "downgoing", [VM] * 7, [((RCV_HERE, FOCI, SHARE_LAGS), F32), ((2, FOCI, LAGS), F32)], [],
        rcv_mask, *parts, start, own,
    )
    return focus_down, focus_up


def solution(mesh):
    return jax.shard_map(
        on_device,
        mesh=mesh,
        in_specs=(P("shot", "rcv", None), P(), P(None, "shot", None), P(None, "rcv", None)),
        out_specs=(P("rcv", None, "shot"), P(("shot", "rcv"), None, None)),
        check_vma=False,
    )
```

```python
import functools
import math

import jax
import jax.numpy as jnp
import ml_dtypes
import numpy as np
from jax import lax
from jax.experimental import pallas as pl
from jax.experimental.pallas import tpu as pltpu
from jax.sharding import PartitionSpec as P


ITERS = 2
LAGS = 256
LANES = 128
FOCI = 2
SHOTS_HERE = 64
RCV_HERE = 16
RCV_AXIS = 32
SHOT_AXIS = 8
SHARE = SHOTS_HERE * FOCI * 2 // 16
HALVES = LAGS // LANES
PLANE = 16
HALF = SHOTS_HERE // 2
CHIPS = SHOT_AXIS // 2
SHARE_LAGS = LAGS // SHOT_AXIS
F32 = jnp.float32
BF16 = jnp.bfloat16


def split_bf16(matrix):
    high = matrix.astype(ml_dtypes.bfloat16)
    low = (matrix - high.astype(np.float64)).astype(ml_dtypes.bfloat16)
    return high, low


def tables():
    times = np.arange(LAGS)[:, None]
    angles = (np.arange(LAGS)[None, :] + 0.5) * (np.pi / LAGS) * times
    forward = np.concatenate([np.cos(angles), -np.sin(angles)], axis=1)
    fwd_high, fwd_low = split_bf16(forward)
    inv_high, inv_low = split_bf16(np.ascontiguousarray(forward.T))
    flip = np.ascontiguousarray(np.eye(LAGS)[::-1]).astype(ml_dtypes.bfloat16)
    return fwd_high, fwd_low, inv_high, inv_low, flip


def dot(left, right):
    return jnp.dot(left, right, preferred_element_type=F32)


def to_spectrum(traces, high, low):
    return dot(traces, high[...]) + dot(traces, low[...])


def to_traces(spectrum, high, low, scale):
    top = spectrum.astype(BF16)
    rest = (spectrum - top.astype(F32)).astype(BF16)
    both = dot(jnp.concatenate([top, rest], axis=0), high[...])
    count = spectrum.shape[0]
    return (both[:count] + (dot(top, low[...]) + both[count:])) * scale


def factors(spectrum):
    re, im = spectrum[:, :LAGS], spectrum[:, LAGS:]
    return re, im - re, im + re


def shot_slot(shot):
    y, z, x, j = shot // 16, (shot // 8) % 2, (shot // 2) % 4, shot % 2
    return y * 16 + x * 4 + z * 2 + j


def pick_kernel(focus_hbm, reflection_hbm, out, focus, reflection, sems):
    copies = [
        pltpu.make_async_copy(focus_hbm, focus, sems.at[0]),
    ] + [
        pltpu.make_async_copy(
            reflection_hbm.at[pl.ds(part * PLANE, PLANE)], reflection.at[pl.ds(part * PLANE, PLANE)], sems.at[1 + part]
        )
        for part in range(SHOTS_HERE // PLANE)
    ]
    for copy in copies:
        copy.start()
    for copy in copies:
        copy.wait()
    first = lax.axis_index("shot") * SHOTS_HERE
    for which in range(FOCI):
        row = focus[which] - first
        inside = jnp.logical_and(row >= 0, row < SHOTS_HERE)
        trace = reflection[jnp.clip(row, 0, SHOTS_HERE - 1)].astype(F32)
        picked = jnp.where(inside, trace, 0.0).astype(BF16)
        out[which * RCV_HERE : (which + 1) * RCV_HERE, :] = picked


def spectra_of(reflection, high, low, out):
    step = 16
    for begin in range(0, HALF, step):
        spectrum = to_spectrum(reflection[begin : begin + step].reshape(step * RCV_HERE, LAGS), high, low)
        for local in range(step):
            piece = spectrum[local * RCV_HERE : (local + 1) * RCV_HERE]
            slot = shot_slot(begin + local)
            for chunk in range(4):
                out[chunk, pl.ds(slot, RCV_HERE, HALF), :] = piece[:, chunk * LANES : (chunk + 1) * LANES]


def prepare_kernel(
    reflection_hbm, high_hbm, low_hbm, inv_high_hbm, inv_low_hbm, flip_hbm,
    out, rest, high, low, inv_high, inv_low, flip, reflection, sems,
):
    def fetch(source, target, place):
        copy = pltpu.make_async_copy(source, target, sems.at[place])
        copy.start()
        return copy

    tables = [fetch(high_hbm, high, 0), fetch(low_hbm, low, 1)]
    block = fetch(reflection_hbm.at[pl.ds(0, HALF)], reflection, 2)
    later = [
        fetch(reflection_hbm.at[pl.ds(HALF, HALF)], rest, 3),
        fetch(inv_high_hbm, inv_high, 4),
        fetch(inv_low_hbm, inv_low, 5),
        fetch(flip_hbm, flip, 6),
    ]
    for copy in tables + [block]:
        copy.wait()
    spectra_of(reflection, high, low, out)
    for copy in later:
        copy.wait()


def rest_kernel(reflection, high, low, out):
    spectra_of(reflection, high, low, out)


def mask_kernel(shot_hbm, rcv_hbm, shot_mask, rcv_mask, shot_window, rcv_window, onset, ending, sems):
    copies = [
        pltpu.make_async_copy(shot_hbm, shot_window, sems.at[0]),
        pltpu.make_async_copy(rcv_hbm, rcv_window, sems.at[1]),
    ]
    for copy in copies:
        copy.start()
    for copy in copies:
        copy.wait()
    up_mask(shot_window, shot_mask)
    down_mask(rcv_window, rcv_mask, onset, ending)


def up_mask(window, out):
    me = lax.axis_index("rcv")
    corner = (me // 8) * 16 + (me % 4) * 2
    row = lax.broadcasted_iota(jnp.int32, (SHARE, LANES), 0)
    onset = jnp.zeros((SHARE, LANES), jnp.int32)
    ending = jnp.zeros((SHARE, LANES), jnp.int32)
    for z in range(2):
        for j in range(2):
            for q in range(FOCI):
                shot = corner + z * 8 + j
                mine = jnp.logical_and(row // 4 == z * 2 + j, row % 2 == q)
                onset = jnp.where(mine, window[0, q, shot], onset)
                ending = jnp.where(mine, window[1, q, shot], ending)
    time = lax.broadcasted_iota(jnp.int32, (SHARE, LANES), 1) + ((row // 2) % 2) * LANES
    out[...] = jnp.logical_and(time >= onset, time < ending).astype(jnp.int32)


def down_mask(window, out, onset, ending):
    for q in range(FOCI):
        for r in range(RCV_HERE):
            line = q * RCV_HERE + r
            onset[line : line + 1, :] = jnp.full((1, LANES), window[0, q, r], jnp.int32)
            ending[line : line + 1, :] = jnp.full((1, LANES), window[1, q, r], jnp.int32)
    time = lax.broadcasted_iota(jnp.int32, (FOCI * RCV_HERE, LANES), 1)
    for h in range(HALVES):
        inside = jnp.logical_and(time + h * LANES >= onset[...], time + h * LANES < ending[...])
        out[:, h * LANES : (h + 1) * LANES] = inside.astype(jnp.int32)


def convolve_in(field, refl, fwd_high, fwd_low, inv_high, inv_low, out, spectrum, product, rows):
    for kind, part in enumerate(factors(to_spectrum(field, fwd_high, fwd_low))):
        spectrum[kind] = part
    for chunk in range(2):
        lanes = slice(chunk * LANES, (chunk + 1) * LANES)
        im_lanes = slice(LAGS + chunk * LANES, LAGS + (chunk + 1) * LANES)
        for begin in range(0, SHOTS_HERE, HALF):
            totals = [jnp.zeros((HALF, LANES), F32) for _ in range(3 * FOCI)]
            here = refl[begin // HALF]
            for r in range(RCV_HERE):
                lines = slice(r * HALF, (r + 1) * HALF)
                re = here[chunk, lines, :]
                im = here[2 + chunk, lines, :]
                both = re + im
                for q in range(FOCI):
                    line = q * RCV_HERE + r
                    for kind, value in enumerate((both, re, im)):
                        totals[3 * q + kind] += value * spectrum[kind, line : line + 1, lanes]
            for q in range(FOCI):
                first, second, third = totals[3 * q : 3 * q + 3]
                lines = slice(q * SHOTS_HERE + begin, q * SHOTS_HERE + begin + HALF)
                product[lines, lanes] = first - third
                product[lines, im_lanes] = first + second
    scale = 1.0 / (LAGS * math.sqrt(RCV_HERE * RCV_AXIS * LAGS))
    result = to_traces(product[...], inv_high, inv_low, scale)
    for q in range(FOCI):
        for h in range(HALVES):
            rows[pl.ds(h * FOCI + q, SHOTS_HERE, 2 * FOCI), :] = result[
                q * SHOTS_HERE : (q + 1) * SHOTS_HERE, h * LANES : (h + 1) * LANES
            ]
    for place in range(PLANE):
        out[place] = rows[place * SHARE : (place + 1) * SHARE, :]


def gather_kernel(mine, near, middle, far, flip, out):
    total = (mine[...].astype(F32) + near[...].astype(F32)) + (middle[...].astype(F32) + far[...].astype(F32))
    out[...] = dot(total.astype(BF16), flip[...]).astype(BF16)


def first_kernel(
    mine, other, refl, refl_rest, fwd_high, fwd_low, inv_high, inv_low, start_out, out, spectrum, product, rows
):
    start = (mine[...].astype(F32) + other[...].astype(F32)).astype(BF16)
    start_out[...] = start
    convolve_in(start, (refl, refl_rest), fwd_high, fwd_low, inv_high, inv_low, out, spectrum, product, rows)


def sum_kernel(parts, out):
    out[...] = total_of(parts)


def upgoing_kernel(mask, mine, other, *outs):
    up = jnp.where(mask[...] != 0, mine[...] + other[...], 0.0)
    if len(outs) > 1:
        outs[1][...] = jnp.where((lax.axis_index("rcv") // 4) % 2 == 0, up[:8], up[8:])
    rounded = up.astype(BF16)
    for place in range(PLANE):
        outs[0][place] = rounded


def correlate_in(upgoing, refl, fwd_high, fwd_low, inv_high, inv_low, rows, spectrum, product):
    for place in range(PLANE):
        rows[place * SHARE : (place + 1) * SHARE, :] = upgoing[place].astype(F32)
    traces = jnp.concatenate(
        [
            jnp.concatenate(
                [rows[pl.ds(h * FOCI + q, SHOTS_HERE, 2 * FOCI), :] for h in range(HALVES)], axis=1
            )
            for q in range(FOCI)
        ],
        axis=0,
    ).astype(BF16)
    for kind, part in enumerate(factors(to_spectrum(traces, fwd_high, fwd_low))):
        spectrum[kind] = part
    for chunk in range(2):
        lanes = slice(chunk * LANES, (chunk + 1) * LANES)
        im_lanes = slice(LAGS + chunk * LANES, LAGS + (chunk + 1) * LANES)
        for r in range(RCV_HERE):
            totals = [jnp.zeros((8, LANES), F32) for _ in range(3 * FOCI)]
            for begin in range(0, SHOTS_HERE, 8):
                here = refl[begin // HALF]
                shots = slice(r * HALF + begin % HALF, r * HALF + begin % HALF + 8)
                re = here[chunk, shots, :]
                im = here[2 + chunk, shots, :]
                both = re - im
                for q in range(FOCI):
                    lines = slice(q * SHOTS_HERE + begin, q * SHOTS_HERE + begin + 8)
                    for kind, value in enumerate((both, re, im)):
                        totals[3 * q + kind] += value * spectrum[kind, lines, lanes]
            for q in range(FOCI):
                line = q * RCV_HERE + r
                first, second, third = totals[3 * q : 3 * q + 3]
                product[line : line + 1, lanes] = jnp.sum(first + third, axis=0, keepdims=True)
                product[line : line + 1, im_lanes] = jnp.sum(first + second, axis=0, keepdims=True)
    scale = 1.0 / (LAGS * math.sqrt(SHOTS_HERE * SHOT_AXIS * LAGS))
    return to_traces(product[...], inv_high, inv_low, scale)


def correlate_kernel(upgoing, refl, refl_rest, fwd_high, fwd_low, inv_high, inv_low, out, rows, spectrum, product):
    out[...] = correlate_in(upgoing, (refl, refl_rest), fwd_high, fwd_low, inv_high, inv_low, rows, spectrum, product)


def last_correlate_kernel(
    upgoing, refl, refl_rest, fwd_high, fwd_low, inv_high, inv_low, keep, send, rows, spectrum, product
):
    result = correlate_in(upgoing, (refl, refl_rest), fwd_high, fwd_low, inv_high, inv_low, rows, spectrum, product)
    pieces = []
    for place in range(SHOT_AXIS):
        piece = result[:, place * SHARE_LAGS : (place + 1) * SHARE_LAGS]
        pieces.append(
            jnp.concatenate([piece[begin : begin + 8] for begin in range(0, FOCI * RCV_HERE, 8)], axis=1)
        )
    even = lax.rem(lax.axis_index("shot"), 2) == 0
    for chip in range(CHIPS):
        first, second = pieces[2 * chip : 2 * chip + 2]
        keep[chip] = jnp.where(even, first, second)
        send[chip] = jnp.where(even, second, first)


def last_pair_kernel(mine, other, own, near, middle, far, total):
    total[...] = mine[...] + other[...]
    chip = lax.axis_index("shot") // 2
    for step, out in enumerate((own, near, middle, far)):
        place = lax.bitwise_xor(chip, step)
        out[...] = total[place]


def chips_kernel(mine, near, middle, far, out):
    out[...] = (mine[...] + near[...]) + (far[...] + middle[...])


def total_of(parts):
    total = parts[0]
    for place in range(1, parts.shape[0]):
        total = total + parts[place]
    return total


def next_kernel(
    mask, mine, other, start, refl, refl_rest, fwd_high, fwd_low, inv_high, inv_low,
    out, spectrum, product, rows,
):
    down = start[...].astype(F32) + jnp.where(mask[...] != 0, mine[...] + other[...], 0.0)
    convolve_in(down.astype(BF16), (refl, refl_rest), fwd_high, fwd_low, inv_high, inv_low, out, spectrum, product, rows)


def last_kernel(mask, mine, far, middle, near, start, own, out, up_out):
    begin = lax.axis_index("shot") * SHARE_LAGS
    shift = lax.rem(LAGS - begin, LAGS)
    start_here = pltpu.roll(start[...].astype(F32), shift, 1)[:, :SHARE_LAGS]
    mask_here = pltpu.roll(mask[...], shift, 1)[:, :SHARE_LAGS]
    total = (mine[...] + near[...]) + (far[...] + middle[...])
    total = jnp.concatenate([total[:, lane : lane + SHARE_LAGS] for lane in range(0, LANES, SHARE_LAGS)], axis=0)
    down = start_here + jnp.where(mask_here != 0, total, 0.0)
    for q in range(FOCI):
        out[:, q, :] = down[q * RCV_HERE : (q + 1) * RCV_HERE]
    for j in range(2):
        for q in range(FOCI):
            for h in range(HALVES):
                line = j * 4 + h * 2 + q
                up_out[j, q : q + 1, h * LANES : (h + 1) * LANES] = own[line : line + 1]


VM = pl.BlockSpec(memory_space=pltpu.VMEM)
HB = pl.BlockSpec(memory_space=pltpu.HBM)
LIMIT = 24 * 1024 * 1024


def call(kernel, name, specs, outs, scratch, *args):
    many = len(outs) > 1
    shapes = [jax.ShapeDtypeStruct(*out) if isinstance(out, tuple) else out for out in outs]
    return pl.pallas_call(
        kernel,
        name=name,
        in_specs=specs,
        out_specs=[VM] * len(outs) if many else VM,
        out_shape=shapes if many else shapes[0],
        scratch_shapes=scratch,
        compiler_params=pltpu.CompilerParams(vmem_limit_bytes=LIMIT),
    )(*args)


def over_shot(array, step):
    return lax.ppermute(array, "shot", [(place, place ^ step) for place in range(SHOT_AXIS)])


def over_plane():
    places = np.arange(RCV_AXIS).reshape(4, 2, 4)
    return places.transpose(1, 0, 2).reshape(2, 16).tolist()


def on_device(reflection, focus_index, shot_window, rcv_window):
    shot_window = jnp.transpose(shot_window, (0, 2, 1))
    rcv_window = jnp.transpose(rcv_window, (0, 2, 1))
    traces = FOCI * RCV_HERE
    rows = pltpu.VMEM((FOCI * HALVES * SHOTS_HERE, LANES), F32)

    def spectra(count):
        return pltpu.VMEM((3, count, LAGS), F32)

    def products(count):
        return pltpu.VMEM((count, 2 * LAGS), F32)

    conv_scratch = [spectra(traces), products(FOCI * SHOTS_HERE), rows]
    corr_scratch = [rows, spectra(FOCI * SHOTS_HERE), products(traces)]
    conv_out = ((PLANE, SHARE, LANES), F32)
    def in_hbm(*arrays):
        return [pltpu.with_memory_space_constraint(array, pltpu.HBM) for array in arrays]

    picks = call(
        pick_kernel, "pick", [HB] * 2, [((traces, LAGS), BF16)],
        [
            pltpu.SMEM((FOCI,), jnp.int32), pltpu.VMEM((SHOTS_HERE, RCV_HERE, LAGS), BF16),
            pltpu.SemaphoreType.DMA((5,)),
        ],
        *in_hbm(focus_index, reflection),
    )
    far, middle, near = [over_shot(picks, step) for step in (6, 4, 2)]
    spectra_half = ((4, RCV_HERE * HALF, LANES), F32)
    refl, rest, *waves, flip = call(
        prepare_kernel, "preparation", [HB] * 6,
        [
            spectra_half,
            ((HALF, RCV_HERE, LAGS), BF16),
            ((LAGS, 2 * LAGS), BF16),
            ((LAGS, 2 * LAGS), BF16),
            ((2 * LAGS, LAGS), BF16),
            ((2 * LAGS, LAGS), BF16),
            ((LAGS, LAGS), BF16),
        ],
        [pltpu.VMEM((HALF, RCV_HERE, LAGS), BF16), pltpu.SemaphoreType.DMA((7,))],
        *in_hbm(reflection, *[jnp.asarray(table) for table in tables()]),
    )
    refl_rest = call(rest_kernel, "rest_preparation", [VM] * 3, [spectra_half], [], rest, waves[0], waves[1])
    shot_mask, rcv_mask = call(
        mask_kernel, "masks", [HB] * 2, [((SHARE, LANES), jnp.int32), ((traces, LAGS), jnp.int32)],
        [
            pltpu.SMEM((2, FOCI, SHOTS_HERE), jnp.int32), pltpu.SMEM((2, FOCI, RCV_HERE), jnp.int32),
            pltpu.VMEM((traces, LANES), jnp.int32), pltpu.VMEM((traces, LANES), jnp.int32),
            pltpu.SemaphoreType.DMA((2,)),
        ],
        *in_hbm(shot_window, rcv_window),
    )
    picks = call(gather_kernel, "chip_picks", [VM] * 5, [((traces, LAGS), BF16)], [], picks, near, middle, far, flip)
    start, partial = call(
        first_kernel, "first_convolution", [VM] * 8, [((traces, LAGS), BF16), conv_out], conv_scratch,
        picks, over_shot(picks, 1), refl, refl_rest, *waves,
    )
    for iteration in range(ITERS):
        parts = lax.all_to_all(partial, "rcv", 0, 0, tiled=True, axis_index_groups=over_plane())
        mine = call(sum_kernel, "plane_sum", [VM], [((SHARE, LANES), F32)], [], parts)
        other = lax.ppermute(mine, "rcv", [(place, place ^ 4) for place in range(RCV_AXIS)])
        outs = [((PLANE, SHARE, LANES), BF16)]
        if iteration + 1 < ITERS:
            rounded = call(upgoing_kernel, "upgoing", [VM] * 3, outs, [], shot_mask, mine, other)
        else:
            rounded, own = call(
                upgoing_kernel, "last_upgoing", [VM] * 3, outs + [((8, LANES), F32)], [], shot_mask, mine, other
            )
        upgoing = lax.all_to_all(rounded, "rcv", 0, 0, tiled=True, axis_index_groups=over_plane())
        if iteration + 1 < ITERS:
            mine = call(
                correlate_kernel, "correlation", [VM] * 7, [((traces, LAGS), F32)], corr_scratch,
                upgoing, refl, refl_rest, *waves,
            )
            others = [over_shot(mine, step) for step in (6, 4, 2)][::-1]
            mine = call(chips_kernel, "chip_sum", [VM] * 4, [((traces, LAGS), F32)], [], mine, *others)
            partial = call(
                next_kernel, "next_convolution", [VM] * 10, [conv_out], conv_scratch,
                rcv_mask, mine, over_shot(mine, 1), start, refl, refl_rest, *waves,
            )
        else:
            keep, send = call(
                last_correlate_kernel, "last_correlation", [VM] * 7, [((CHIPS, 8, LANES), F32)] * 2,
                corr_scratch, upgoing, refl, refl_rest, *waves,
            )
            mine, near, middle, far = call(
                last_pair_kernel, "last_pair_sum", [VM] * 2, [((8, LANES), F32)] * CHIPS,
                [pltpu.VMEM((CHIPS, 8, LANES), F32)], keep, over_shot(send, 1),
            )
            parts = [mine] + [over_shot(part, step) for part, step in ((far, 6), (middle, 4), (near, 2))]
    focus_down, focus_up = call(
        last_kernel, "downgoing", [VM] * 7, [((RCV_HERE, FOCI, SHARE_LAGS), F32), ((2, FOCI, LAGS), F32)], [],
        rcv_mask, *parts, start, own,
    )
    return focus_down, focus_up


def solution(mesh):
    return jax.shard_map(
        on_device,
        mesh=mesh,
        in_specs=(P("shot", "rcv", None), P(), P(None, "shot", None), P(None, "rcv", None)),
        out_specs=(P("rcv", None, "shot"), P(("shot", "rcv"), None, None)),
        check_vma=False,
    )
```
